32 devices in a mesh: dp: 16 (over z, x, core), tensor: 2 (over y).
Axes of the slice: x: 2, y: 2, z: 4, core: 2. Of those that a mesh axis runs over, the one named last changes fastest.
Arguments:
- short_tokens: bfloat16 [128, 64, 768], P('dp'), may hold values from -6 to 6
- long_tokens: bfloat16 [128, 256, 768], P('dp'), may hold values from -6 to 6
- short_cotangent: bfloat16 [128, 64, 768], P('dp'), may hold values from -6 to 6
- long_cotangent: bfloat16 [128, 256, 768], P('dp'), may hold values from -6 to 6
- short_lengths: int32 [128], P('dp'), may hold values from 1 to 64, 6144 in all
- long_lengths: int32 [128], P('dp'), may hold values from 1 to 256, 24576 in all
- queries: bfloat16 [256, 768], P('dp'), may hold values from -0.4375 to 0.4375
- positives: int32 [256], P('dp'), may hold values from 0 to 255, each once
- step_count: int32 [1], replicated, may hold values from 2 to 20
- mixing_weight: float32 [768, 3, 768], P('dp', None, 'tensor'), may hold values from -0.21875 to 0.21875
- mixing_moment: float32 [768, 3, 768], P('dp', None, 'tensor'), may hold values from -0.005859375 to 0.005859375
- mixing_square: float32 [768, 3, 768], P('dp', None, 'tensor'), may hold values from 4.709503e-08 to 1.8838011e-07
- mixing_average: float32 [768, 3, 768], P('dp', None, 'tensor'), may hold values from -0.21875 to 0.21875
- merging_weight: float32 [768, 768], P('tensor', 'dp'), may hold values from -1.75 to 1.75
- merging_moment: float32 [768, 768], P('tensor', 'dp'), may hold values from -0.005859375 to 0.005859375
- merging_square: float32 [768, 768], P('tensor', 'dp'), may hold values from 4.709503e-08 to 1.8838011e-07
- merging_average: float32 [768, 768], P('tensor', 'dp'), may hold values from -1.75 to 1.75
- expand_weight: float32 [768, 3072], P('dp', 'tensor'), may hold values from -0.21875 to 0.21875
- expand_moment: float32 [768, 3072], P('dp', 'tensor'), may hold values from -0.005859375 to 0.005859375
- expand_square: float32 [768, 3072], P('dp', 'tensor'), may hold values from 4.709503e-08 to 1.8838011e-07
- expand_average: float32 [768, 3072], P('dp', 'tensor'), may hold values from -0.21875 to 0.21875
- shrink_weight: float32 [3072, 768], P('tensor', 'dp'), may hold values from -0.109375 to 0.109375
- shrink_moment: float32 [3072, 768], P('tensor', 'dp'), may hold values from -0.005859375 to 0.005859375
- shrink_square: float32 [3072, 768], P('tensor', 'dp'), may hold values from 4.709503e-08 to 1.8838011e-07
- shrink_average: float32 [3072, 768], P('tensor', 'dp'), may hold values from -0.109375 to 0.109375
- scales_weight: float32 [6, 768], replicated, may hold values from -0.75 to 1.5
- scales_moment: float32 [6, 768], replicated, may hold values from -0.0234375 to 0.0234375
- scales_square: float32 [6, 768], replicated, may hold values from 7.5352045e-07 to 3.0140818e-06
- scales_average: float32 [6, 768], replicated, may hold values from -0.75 to 1.5
- offsets_weight: float32 [4608], P('tensor'), may hold values from -3 to 3
- offsets_moment: float32 [4608], P('tensor'), may hold values from -0.0234375 to 0.0234375
- offsets_square: float32 [4608], P('tensor'), may hold values from 7.5352045e-07 to 3.0140818e-06
- offsets_average: float32 [4608], P('tensor'), may hold values from -3 to 3
Outputs:
- short_output: bfloat16 [128, 64, 768], P('dp')
- long_output: bfloat16 [128, 256, 768], P('dp')
- short_gradient: float32 [128, 64, 768], P('dp')
- long_gradient: float32 [128, 256, 768], P('dp')
- query_gradient: float32 [256, 768], P('dp')
- contrast_loss: float32 [1], replicated
- gradient_norm: float32 [1], replicated
- mixing_master: float32 [768, 3, 768], P('dp', None, 'tensor')
- mixing_first: float32 [768, 3, 768], P('dp', None, 'tensor')
- mixing_second: float32 [768, 3, 768], P('dp', None, 'tensor')
- mixing_smooth: float32 [768, 3, 768], P('dp', None, 'tensor')
- merging_master: float32 [768, 768], P('tensor', 'dp')
- merging_first: float32 [768, 768], P('tensor', 'dp')
- merging_second: float32 [768, 768], P('tensor', 'dp')
- merging_smooth: float32 [768, 768], P('tensor', 'dp')
- expand_master: float32 [768, 3072], P('dp', 'tensor')
- expand_first: float32 [768, 3072], P('dp', 'tensor')
- expand_second: float32 [768, 3072], P('dp', 'tensor')
- expand_smooth: float32 [768, 3072], P('dp', 'tensor')
- shrink_master: float32 [3072, 768], P('tensor', 'dp')
- shrink_first: float32 [3072, 768], P('tensor', 'dp')
- shrink_second: float32 [3072, 768], P('tensor', 'dp')
- shrink_smooth: float32 [3072, 768], P('tensor', 'dp')
- scales_master: float32 [6, 768], replicated
- scales_first: float32 [6, 768], replicated
- scales_second: float32 [6, 768], replicated
- scales_smooth: float32 [6, 768], replicated
- offsets_master: float32 [4608], P('tensor')
- offsets_first: float32 [4608], P('tensor')
- offsets_second: float32 [4608], P('tensor')
- offsets_smooth: float32 [4608], P('tensor')
The draws below stay inside these ranges and needn't reach their ends.
Inputs may be any that keep to these rules, and one draw needn't show every extreme that they name: `short_lengths`: at least one short passage has all 64 tokens valid. `long_lengths`: at least one long passage has all 256 tokens valid. `positives`: each passage is the positive of exactly one query.
All inputs are finite; a program needn't handle non-finite values. No bound on the sum of `short_lengths` or of `long_lengths` on one device may be relied on, other than what follows from the above.
Results may differ from the reference program's by a relative error of at most 0.013.
The reference program's roundings to bfloat16 on the way count: a program that leaves them out, or rounds other values in their place, can miss the bound.
Values may be sent and summed in bfloat16 or wider, within the bound.
A program may use at most 256 MiB of HBM per device.

```python
import math
import jax
import jax.numpy as jnp
import numpy as np
from jax import lax

D = 768
FF = 3072
HEADS = 12
HEAD_DIM = 64
SHORT_LEN = 64
LONG_LEN = 256
SHORT_DEV = 8
LONG_DEV = 8
SHORTS = 128
LONGS = 128
PASSAGES = 256
N_DP = 16
N_TENSOR = 2


def scale_rows(key, salt):
    folded = jax.random.fold_in(key, salt)
    noise_part = jnp.clip(jax.random.normal(folded, (6, D), jnp.float32), -2.5, 2.5)
    row_index = lax.broadcasted_iota(jnp.int32, (6, D), 0)
    gain_rows = jnp.logical_and(row_index % 2 == 0, row_index < 4)
    return jnp.where(gain_rows, 1.0 + 0.2 * noise_part, 0.3 * noise_part)


def draw_scales_weight(key, part):
    return scale_rows(key, 11)


def draw_scales_average(key, part):
    return scale_rows(key, 29)


def level_of(own_key, shape, cuts, smallest, top_value):
    def one(dim, parts):
        draws = jax.random.uniform(jax.random.fold_in(jax.random.fold_in(own_key, 6), dim), (parts,), jnp.float32, smallest / len(cuts), top_value / len(cuts))
        return jnp.repeat(jnp.exp(draws), shape[dim] // parts).reshape((-1,) + (1,) * (len(shape) - dim - 1))

    factor_of = one(*cuts[0])
    for cut in cuts[1:]:
        factor_of = factor_of * one(*cut)
    return factor_of


def length_profile(count, total, bound, slope):
    portions = [(1 << 20) // math.isqrt(rank ** slope) + 1 for rank in range(2, count + 1)]
    surplus, given = total - bound - (count - 1), [1] * (count - 1)
    while surplus > 0:
        candidates = [i for i in range(count - 1) if given[i] < bound]
        pool, budget = sum([portions[i] for i in candidates]), surplus
        for i in candidates:
            addition = min(bound - given[i], max(1, budget * portions[i] // pool), surplus)
            given[i] = given[i] + addition
            surplus = surplus - addition
    return np.array([bound] + given)


def uneven_parts(stream_key, number_of, total, bound, lean):
    if number_of == 2:
        one = jax.random.randint(stream_key, (), max(1, total - bound), min(bound, total - 1) + 1)
        return jnp.stack([one, total - one])
    tallies = jnp.asarray(length_profile(number_of, total, bound, lean), jnp.int32)
    pairs = (number_of - 1) // 2
    giver, sink = tallies[1:1 + 2 * pairs:2], tallies[2:2 + 2 * pairs:2]
    room = jnp.minimum(giver - 1, bound - sink)
    moved = jax.random.randint(jax.random.fold_in(stream_key, 1), (pairs,), 0, 1 << 20) % (room + 1)
    tallies = tallies.at[1:1 + 2 * pairs:2].set(giver - moved).at[2:2 + 2 * pairs:2].set(sink + moved)
    return tallies[jax.random.permutation(jax.random.fold_in(stream_key, 2), number_of)]


def normal_values(key, shape, deviation, reach, pieces=(), kind=jnp.bfloat16):
    values = deviation * jax.random.normal(key, shape, jnp.float32)
    if pieces:
        values = values * level_of(key, shape, pieces, -0.22, 0.18)
    return jnp.clip(values, -reach, reach).astype(kind)


def setup_inputs(seed: int = 0) -> dict:
    key_of = jax.random.split(jax.random.key(seed), 34)
    short_tokens = normal_values(key_of[0], (SHORTS, SHORT_LEN, D), 1.0, 6.0, ((0, 16),))
    long_tokens = normal_values(key_of[1], (LONGS, LONG_LEN, D), 1.0, 6.0, ((0, 16),))
    short_cotangent = normal_values(key_of[2], (SHORTS, SHORT_LEN, D), 1.0, 6.0, ((0, 16),))
    long_cotangent = normal_values(key_of[3], (LONGS, LONG_LEN, D), 1.0, 6.0, ((0, 16),))
    short_lengths = uneven_parts(key_of[4], SHORTS, SHORTS * SHORT_LEN * 3 // 4, SHORT_LEN, 1).astype(jnp.int32)
    long_lengths = uneven_parts(key_of[5], LONGS, LONGS * LONG_LEN * 3 // 4, LONG_LEN, 1).astype(jnp.int32)
    queries = normal_values(key_of[6], (PASSAGES, D), (D // 4) ** -0.5, 0.4375, ((0, 16),))
    positives = jax.random.permutation(key_of[7], PASSAGES).astype(jnp.int32)
    step_count = jax.random.randint(key_of[8], (1,), 2, 21).astype(jnp.int32)
    mixing_weight = normal_values(key_of[9], (D, 3, D), D ** -0.5, 0.21875, ((0, 16), (2, 2)), jnp.float32)
    mixing_moment = normal_values(key_of[10], (D, 3, D), ((4 * D * D + 2 * D * FF) ** -0.5), 0.005859375, ((0, 16), (2, 2)), jnp.float32)
    mixing_square = jnp.clip(jnp.exp(math.log(1.8838011328625726e-07) - 1.3862944 * jax.random.uniform(key_of[11], (D, 3, D), jnp.float32) ** level_of(key_of[11], (D, 3, D), ((0, 16), (2, 2)), -0.2, 0.2)), 4.7095028321564314e-08, 1.8838011328625726e-07)
    mixing_average = normal_values(key_of[12], (D, 3, D), D ** -0.5, 0.21875, ((0, 16), (2, 2)), jnp.float32)
    merging_weight = normal_values(key_of[13], (D, D), (D // 64) ** -0.5, 1.75, ((0, 2), (1, 16)), jnp.float32)
    merging_moment = normal_values(key_of[14], (D, D), ((4 * D * D + 2 * D * FF) ** -0.5), 0.005859375, ((0, 2), (1, 16)), jnp.float32)
    merging_square = jnp.clip(jnp.exp(math.log(1.8838011328625726e-07) - 1.3862944 * jax.random.uniform(key_of[15], (D, D), jnp.float32) ** level_of(key_of[15], (D, D), ((0, 2), (1, 16)), -0.2, 0.2)), 4.7095028321564314e-08, 1.8838011328625726e-07)
    merging_average = normal_values(key_of[16], (D, D), (D // 64) ** -0.5, 1.75, ((0, 2), (1, 16)), jnp.float32)
    expand_weight = normal_values(key_of[17], (D, FF), D ** -0.5, 0.21875, ((0, 16), (1, 2)), jnp.float32)
    expand_moment = normal_values(key_of[18], (D, FF), ((4 * D * D + 2 * D * FF) ** -0.5), 0.005859375, ((0, 16), (1, 2)), jnp.float32)
    expand_square = jnp.clip(jnp.exp(math.log(1.8838011328625726e-07) - 1.3862944 * jax.random.uniform(key_of[19], (D, FF), jnp.float32) ** level_of(key_of[19], (D, FF), ((0, 16), (1, 2)), -0.2, 0.2)), 4.7095028321564314e-08, 1.8838011328625726e-07)
    expand_average = normal_values(key_of[20], (D, FF), D ** -0.5, 0.21875, ((0, 16), (1, 2)), jnp.float32)
    shrink_weight = normal_values(key_of[21], (FF, D), FF ** -0.5, 0.109375, ((0, 2), (1, 16)), jnp.float32)
    shrink_moment = normal_values(key_of[22], (FF, D), ((4 * D * D + 2 * D * FF) ** -0.5), 0.005859375, ((0, 2), (1, 16)), jnp.float32)
    shrink_square = jnp.clip(jnp.exp(math.log(1.8838011328625726e-07) - 1.3862944 * jax.random.uniform(key_of[23], (FF, D), jnp.float32) ** level_of(key_of[23], (FF, D), ((0, 2), (1, 16)), -0.2, 0.2)), 4.7095028321564314e-08, 1.8838011328625726e-07)
    shrink_average = normal_values(key_of[24], (FF, D), FF ** -0.5, 0.109375, ((0, 2), (1, 16)), jnp.float32)
    scales_weight = draw_scales_weight(jax.random.fold_in(key_of[33], 71), 0)
    scales_moment = normal_values(key_of[26], (6, D), (4 * (4 * D * D + 2 * D * FF) ** -0.5), 0.0234375, (), jnp.float32)
    scales_square = jnp.clip(jnp.exp(jax.random.uniform(key_of[27], (6, D), jnp.float32, math.log(7.53520453145029e-07), math.log(3.014081812580116e-06))), 7.53520453145029e-07, 3.014081812580116e-06)
    scales_average = draw_scales_average(jax.random.fold_in(key_of[33], 71), 0)
    offsets_weight = normal_values(key_of[29], (2 * D + FF,), 0.5, 3.0, ((0, 2),), jnp.float32)
    offsets_moment = normal_values(key_of[30], (2 * D + FF,), (4 * (4 * D * D + 2 * D * FF) ** -0.5), 0.0234375, ((0, 2),), jnp.float32)
    offsets_square = jnp.clip(jnp.exp(math.log(3.014081812580116e-06) - 1.3862944 * jax.random.uniform(key_of[31], (2 * D + FF,), jnp.float32) ** level_of(key_of[31], (2 * D + FF,), ((0, 2),), -0.2, 0.2)), 7.53520453145029e-07, 3.014081812580116e-06)
    offsets_average = normal_values(key_of[32], (2 * D + FF,), 0.5, 3.0, ((0, 2),), jnp.float32)
    return dict(short_tokens=short_tokens, long_tokens=long_tokens, short_cotangent=short_cotangent, long_cotangent=long_cotangent, short_lengths=short_lengths, long_lengths=long_lengths, queries=queries, positives=positives, step_count=step_count, mixing_weight=mixing_weight, mixing_moment=mixing_moment, mixing_square=mixing_square, mixing_average=mixing_average, merging_weight=merging_weight, merging_moment=merging_moment, merging_square=merging_square, merging_average=merging_average, expand_weight=expand_weight, expand_moment=expand_moment, expand_square=expand_square, expand_average=expand_average, shrink_weight=shrink_weight, shrink_moment=shrink_moment, shrink_square=shrink_square, shrink_average=shrink_average, scales_weight=scales_weight, scales_moment=scales_moment, scales_square=scales_square, scales_average=scales_average, offsets_weight=offsets_weight, offsets_moment=offsets_moment, offsets_square=offsets_square, offsets_average=offsets_average)


norm_eps = 1e-05
score_scale = 0.125
masked_value = -1e+30
first_decay = 0.5
second_decay = 0.75
smooth_decay = 0.75
decay_weight = 0.01
adam_eps = 1e-08
clip_limit = 1.0

@jax.custom_vjp
def low(v):
    return lax.optimization_barrier(v.astype(jnp.bfloat16)).astype(jnp.float32)

@jax.custom_vjp
def low_back(v):
    return v

def low_keep(v):
    return (low(v), None)

def low_pass(kept, grad):
    return (grad,)

def back_keep(v):
    return (v, None)

def back_low(kept, grad):
    return (low(grad),)
low.defvjp(low_keep, low_pass)
low_back.defvjp(back_keep, back_low)

def normalize(resid, gain, shift):
    centre = resid - lax.optimization_barrier(jnp.mean(resid, axis=-1, keepdims=True))
    variance = lax.optimization_barrier(jnp.mean(centre * centre, axis=-1, keepdims=True))
    return centre * lax.rsqrt(variance + norm_eps) * gain + shift

def attend(block):
    queries_part, keys_part, values_part, lengths = block
    product = jnp.einsum('bqhd,bkhd->bhqk', queries_part, keys_part, precision=lax.Precision.HIGHEST)
    scores = low_back(product) * score_scale
    visible = lax.broadcasted_iota(jnp.int32, scores.shape, 3) < lengths[:, None, None, None]
    scores = jnp.where(visible, scores, masked_value)
    weights = low(jax.nn.softmax(scores, axis=-1))
    return jnp.einsum('bhqk,bkhd->bqhd', weights, values_part, precision=lax.Precision.HIGHEST)

def bucket_attend(queries_rows, keys_rows, values_rows, lengths, count, span):
    shape = (N_DP, count, span, HEADS, HEAD_DIM)
    blocks = (queries_rows.reshape(shape), keys_rows.reshape(shape), values_rows.reshape(shape), lengths.reshape(N_DP, count))
    context = lax.map(jax.checkpoint(attend), blocks)
    return context.reshape(N_DP * count * span, D)

def forward(short_x, long_x, queries_f, mixing, merging, expand, shrink, scales, offsets, short_lengths, long_lengths, positives):
    short_rows = SHORT_DEV * N_DP * SHORT_LEN
    inputs = jnp.concatenate([short_x.reshape(-1, D), long_x.reshape(-1, D)], axis=0)
    projected = low_back(jnp.dot(inputs, low(mixing).reshape(D, 3 * D), precision=lax.Precision.HIGHEST)).reshape(-1, 3, D)
    blocks = offsets.reshape(N_TENSOR, -1)
    local_width = D // N_TENSOR
    query_bias = blocks[:, :local_width].reshape(D)
    value_bias = blocks[:, local_width:2 * local_width].reshape(D)
    upward_bias = blocks[:, 2 * local_width:].reshape(FF)
    queries_all = low(projected[:, 0] + query_bias)
    keys_all = low(projected[:, 1])
    values_all = low(projected[:, 2] + value_bias)
    short_context = bucket_attend(queries_all[:short_rows], keys_all[:short_rows], values_all[:short_rows], short_lengths, SHORT_DEV, SHORT_LEN)
    long_context = bucket_attend(queries_all[short_rows:], keys_all[short_rows:], values_all[short_rows:], long_lengths, LONG_DEV, LONG_LEN)
    context = low_back(low(jnp.concatenate([short_context, long_context], axis=0)))
    attention = low_back(jnp.dot(context, low(merging), precision=lax.Precision.HIGHEST)) + scales[4]
    hidden = normalize(inputs + attention, scales[0], scales[1])
    upward = low_back(jnp.dot(low(hidden), low(expand), precision=lax.Precision.HIGHEST)) + upward_bias
    activated = low(jax.nn.gelu(upward, approximate=False))
    downward = low_back(jnp.dot(activated, low(shrink), precision=lax.Precision.HIGHEST)) + scales[5]
    result = normalize(hidden + downward, scales[2], scales[3])
    short_out = result[:short_rows].reshape(short_x.shape)
    long_out = result[short_rows:].reshape(long_x.shape)
    leading = jnp.concatenate([short_out[:, 0].reshape(N_DP, SHORT_DEV, D), long_out[:, 0].reshape(N_DP, LONG_DEV, D)], axis=1).reshape(-1, D)
    passages_all = low(leading)
    logits = low_back(jnp.dot(queries_f, passages_all.T, precision=lax.Precision.HIGHEST))
    chosen = (lax.broadcasted_iota(jnp.int32, logits.shape, 1) == positives[:, None]).astype(logits.dtype)
    loss_sum = jnp.sum(jax.nn.logsumexp(logits, axis=1) - lax.optimization_barrier(jnp.sum(logits * chosen, axis=1)))
    return (short_out, long_out, loss_sum)

def update(weight, moment, square, average, gradient, factor, rate, first_fix, second_fix):
    clipped = gradient * factor
    first = first_decay * moment + (1.0 - first_decay) * clipped
    second = second_decay * square + (1.0 - second_decay) * clipped * clipped
    master = weight - rate * (first / first_fix / (jnp.sqrt(second / second_fix) + adam_eps) + decay_weight * weight)
    smooth = smooth_decay * average + (1.0 - smooth_decay) * master
    return (master, first, second, smooth)

def reference(short_tokens, long_tokens, short_cotangent, long_cotangent, short_lengths, long_lengths, queries, positives, step_count, mixing_weight, mixing_moment, mixing_square, mixing_average, merging_weight, merging_moment, merging_square, merging_average, expand_weight, expand_moment, expand_square, expand_average, shrink_weight, shrink_moment, shrink_square, shrink_average, scales_weight, scales_moment, scales_square, scales_average, offsets_weight, offsets_moment, offsets_square, offsets_average):

    def objective(short_x, long_x, queries_f, mixing, merging, expand, shrink, scales, offsets):
        return forward(short_x, long_x, queries_f, mixing, merging, expand, shrink, scales, offsets, short_lengths, long_lengths, positives)
    outputs, pullback = jax.vjp(objective, short_tokens.astype(jnp.float32), long_tokens.astype(jnp.float32), queries.astype(jnp.float32), mixing_weight, merging_weight, expand_weight, shrink_weight, scales_weight, offsets_weight)
    gradients = pullback((short_cotangent.astype(jnp.float32), long_cotangent.astype(jnp.float32), jnp.ones_like(outputs[2])))
    squares = jnp.sum(gradients[3] * gradients[3])
    for position in range(4, 9):
        squares = squares + jnp.sum(gradients[position] * gradients[position])
    gradient_norm = jnp.sqrt(squares)
    factor = clip_limit / jnp.maximum(gradient_norm, clip_limit)
    steps_float = step_count[0].astype(jnp.float32)
    first_fix = 1.0 - jnp.power(first_decay, steps_float)
    second_fix = 1.0 - jnp.power(second_decay, steps_float)
    mixing_new = update(mixing_weight, mixing_moment, mixing_square, mixing_average, gradients[3], factor, D ** (-0.5), first_fix, second_fix)
    merging_new = update(merging_weight, merging_moment, merging_square, merging_average, gradients[4], factor, 8.0 * D ** (-0.5), first_fix, second_fix)
    expand_new = update(expand_weight, expand_moment, expand_square, expand_average, gradients[5], factor, D ** (-0.5), first_fix, second_fix)
    shrink_new = update(shrink_weight, shrink_moment, shrink_square, shrink_average, gradients[6], factor, FF ** (-0.5), first_fix, second_fix)
    scales_new = update(scales_weight, scales_moment, scales_square, scales_average, gradients[7], factor, 0.3, first_fix, second_fix)
    offsets_new = update(offsets_weight, offsets_moment, offsets_square, offsets_average, gradients[8], factor, 0.3, first_fix, second_fix)
    return (outputs[0].astype(jnp.bfloat16), outputs[1].astype(jnp.bfloat16), gradients[0], gradients[1], gradients[2], (outputs[2] / PASSAGES).reshape(1), gradient_norm.reshape(1), mixing_new[0], mixing_new[1], mixing_new[2], mixing_new[3], merging_new[0], merging_new[1], merging_new[2], merging_new[3], expand_new[0], expand_new[1], expand_new[2], expand_new[3], shrink_new[0], shrink_new[1], shrink_new[2], shrink_new[3], scales_new[0], scales_new[1], scales_new[2], scales_new[3], offsets_new[0], offsets_new[1], offsets_new[2], offsets_new[3])
```

```python
import functools
import math

import jax
import jax.numpy as jnp
from jax import lax
from jax.experimental import pallas as pl
from jax.experimental.pallas import tpu as pltpu
from jax.sharding import PartitionSpec as P

D = 768
FF = 3072
HEAD_DIM = 64
PAIR = 2 * HEAD_DIM
MESH = pl.DeviceIdType.MESH

norm_eps = 1e-05
score_scale = 0.125
masked_value = -1e30
first_decay = 0.5
second_decay = 0.75
smooth_decay = 0.75
decay_weight = 0.01
adam_eps = 1e-08
clip_limit = 1.0
inverse_root_two = 0.7071067811865476
inverse_root_tau = 0.3989422804014327
big_vmem = 56 * 1024 * 1024


def dot_nn(a, b):
    return lax.dot_general(a, b, (((1,), (0,)), ((), ())), preferred_element_type=jnp.float32)


def dot_nt(a, b):
    return lax.dot_general(a, b, (((1,), (1,)), ((), ())), preferred_element_type=jnp.float32)


def dot_tn(a, b):
    return lax.dot_general(a, b, (((0,), (0,)), ((), ())), preferred_element_type=jnp.float32)


def layer_stats(resid):
    centre = resid - jnp.mean(resid, axis=-1, keepdims=True)
    rstd = lax.rsqrt(jnp.mean(centre * centre, axis=-1, keepdims=True) + norm_eps)
    return (centre * rstd, rstd)


def layer_back(gradient, normed, rstd, gain):
    scaled = gradient * gain
    return rstd * (
        scaled
        - jnp.mean(scaled, axis=-1, keepdims=True)
        - normed * jnp.mean(scaled * normed, axis=-1, keepdims=True)
    )


def visible_keys(spans, step, rows, piece, key_axis):
    shape = (rows, 1) if key_axis == 0 else (1, rows)
    place = lax.broadcasted_iota(jnp.int32, shape, key_axis)
    segment = place // piece
    limit = jnp.zeros(shape, jnp.int32)
    for index in range(rows // piece):
        limit = jnp.where(segment == index, spans[step, index], limit)
    key_valid = (place % piece) < limit
    first = lax.broadcasted_iota(jnp.int32, (rows, rows), 0) // piece
    second = lax.broadcasted_iota(jnp.int32, (rows, rows), 1) // piece
    return jnp.logical_and(jnp.logical_or(first == second, step > 0), key_valid)


def own_lanes(value, which):
    lane = lax.broadcasted_iota(jnp.int32, value.shape, 1)
    return jnp.where((lane // HEAD_DIM) == which, value, jnp.zeros_like(value))


def join_lanes(low, high):
    lane = lax.broadcasted_iota(jnp.int32, low.shape, 1)
    return jnp.where(lane < HEAD_DIM, low, high)


def attend_forward_kernel(piece, spans, x_ref, w_ref, bias_ref, qkv_ref, ctx_ref):
    step = pl.program_id(0)
    rows = x_ref.shape[0]
    width = w_ref.shape[2] // 3
    visible = visible_keys(spans, step, rows, piece, 1)
    for half in range(w_ref.shape[0]):
        base = half * 3 * width
        projected = dot_nn(x_ref[...], w_ref[half]) + bias_ref[:, base : base + 3 * width]
        qkv_ref[:, base : base + 3 * width] = projected.astype(jnp.bfloat16)
        for pair in range(width // PAIR):
            at = base + pair * PAIR
            q = qkv_ref[:, at : at + PAIR] * jnp.bfloat16(score_scale)
            k = qkv_ref[:, at + width : at + width + PAIR]
            v = qkv_ref[:, at + 2 * width : at + 2 * width + PAIR]
            parts = []
            for which in range(2):
                scores = jnp.where(visible, dot_nt(own_lanes(q, which), k), masked_value)
                powered = jnp.exp(scores - jnp.max(scores, axis=-1, keepdims=True))
                weights = powered * (1.0 / jnp.sum(powered, axis=-1, keepdims=True))
                parts.append(dot_nn(weights.astype(jnp.bfloat16), v))
            at = half * width + pair * PAIR
            ctx_ref[:, at : at + PAIR] = join_lanes(*parts).astype(jnp.bfloat16)


def feed_forward_kernel(
    ctx_ref, x_ref, mt_ref, e_ref, st_ref, scales_ref, bu_ref,
    out_ref, hb_ref, g_ref, slope_ref, n1_ref, r1_ref, n2_ref, r2_ref,
):
    width = mt_ref.shape[2]
    wide = e_ref.shape[2]
    attention = scales_ref[4:5, :]
    for half in range(mt_ref.shape[0]):
        attention = attention + dot_nt(
            ctx_ref[:, half * width : (half + 1) * width], mt_ref[half]
        )
    normed, rstd = layer_stats(x_ref[...].astype(jnp.float32) + attention)
    n1_ref[...] = normed
    r1_ref[...] = rstd
    hidden = normed * scales_ref[0:1, :] + scales_ref[1:2, :]
    hidden_low = hidden.astype(jnp.bfloat16)
    hb_ref[...] = hidden_low
    downward = scales_ref[5:6, :]
    for half in range(e_ref.shape[0]):
        at = half * wide
        upward = dot_nn(hidden_low, e_ref[half]) + bu_ref[:, at : at + wide]
        cumulative = 0.5 * (1.0 + lax.erf(upward * inverse_root_two))
        density = jnp.exp(-0.5 * upward * upward) * inverse_root_tau
        activated = (upward * cumulative).astype(jnp.bfloat16)
        g_ref[:, at : at + wide] = activated
        slope_ref[:, at : at + wide] = (cumulative + upward * density).astype(jnp.bfloat16)
        downward = downward + dot_nt(activated, st_ref[half])
    normed, rstd = layer_stats(hidden + downward)
    n2_ref[...] = normed
    r2_ref[...] = rstd
    out_ref[...] = (normed * scales_ref[2:3, :] + scales_ref[3:4, :]).astype(jnp.bfloat16)


def add_row(ref, index, value):
    ref[index : index + 1, :] += jnp.sum(value, axis=0, keepdims=True)


def feed_back_kernel(
    piece, cot_ref, lead_ref, n1_ref, r1_ref, n2_ref, r2_ref, slope_ref, mt_ref, e_ref, st_ref, scales_ref,
    dz_ref, dub_ref, da_ref, dr1_ref, dctx_ref, vec_ref, up_ref,
):
    @pl.when(pl.program_id(0) == 0)
    def _():
        vec_ref[...] = jnp.zeros_like(vec_ref)
        up_ref[...] = jnp.zeros_like(up_ref)

    width = mt_ref.shape[2]
    wide = e_ref.shape[2]
    dout = cot_ref[...].astype(jnp.float32)
    row = lax.broadcasted_iota(jnp.int32, dout.shape, 0)
    for index in range(dout.shape[0] // piece):
        dout = dout + jnp.where(row == index * piece, lead_ref[0, index : index + 1, :], 0.0)
    normed = n2_ref[...]
    add_row(vec_ref, 2, dout * normed)
    add_row(vec_ref, 3, dout)
    second = layer_back(dout, normed, r2_ref[...], scales_ref[2:3, :])
    add_row(vec_ref, 5, second)
    low = second.astype(jnp.bfloat16)
    dz_ref[...] = low
    hidden_back = second
    for half in range(e_ref.shape[0]):
        at = half * wide
        upward = dot_nn(low, st_ref[half]) * slope_ref[:, at : at + wide].astype(jnp.float32)
        up_ref[0:1, at : at + wide] += jnp.sum(upward, axis=0, keepdims=True)
        upward_low = upward.astype(jnp.bfloat16)
        dub_ref[:, at : at + wide] = upward_low
        hidden_back = hidden_back + dot_nt(upward_low, e_ref[half])
    normed = n1_ref[...]
    add_row(vec_ref, 0, hidden_back * normed)
    add_row(vec_ref, 1, hidden_back)
    first = layer_back(hidden_back, normed, r1_ref[...], scales_ref[0:1, :])
    add_row(vec_ref, 4, first)
    dr1_ref[...] = first
    low = first.astype(jnp.bfloat16)
    da_ref[...] = low
    for half in range(mt_ref.shape[0]):
        dctx_ref[:, half * width : (half + 1) * width] = dot_nn(low, mt_ref[half]).astype(
            jnp.bfloat16
        )


def attend_back_kernel(
    piece, spans, qkv_ref, dctx_ref, dr1_ref, w_ref, dproj_ref, dx_ref, low_ref, bias_ref
):
    step = pl.program_id(0)

    @pl.when(step == 0)
    def _():
        bias_ref[...] = jnp.zeros_like(bias_ref)

    rows = qkv_ref.shape[0]
    width = w_ref.shape[2] // 3
    visible = visible_keys(spans, step, rows, piece, 0)
    total = dr1_ref[...]
    for half in range(w_ref.shape[0]):
        base = half * 3 * width
        for pair in range(width // PAIR):
            at = base + pair * PAIR
            q = qkv_ref[:, at : at + PAIR]
            k = qkv_ref[:, at + width : at + width + PAIR]
            v = qkv_ref[:, at + 2 * width : at + 2 * width + PAIR]
            near = half * width + pair * PAIR
            back = dctx_ref[:, near : near + PAIR]
            parts = []
            for which in range(2):
                scores = dot_nt(own_lanes(k, which) * jnp.bfloat16(score_scale), q)
                scores = jnp.where(visible, scores, masked_value)
                powered = jnp.exp(scores - jnp.max(scores, axis=0, keepdims=True))
                weights = powered * (1.0 / jnp.sum(powered, axis=0, keepdims=True))
                weight_back = dot_nt(own_lanes(v, which), back)
                score_back = weights * (
                    weight_back - jnp.sum(weights * weight_back, axis=0, keepdims=True)
                )
                score_low = (score_back * score_scale).astype(jnp.bfloat16)
                parts.append(
                    (
                        dot_tn(score_low, k),
                        dot_nn(score_low, q),
                        dot_nn(weights.astype(jnp.bfloat16), back),
                    )
                )
            for part in range(3):
                value = join_lanes(parts[0][part], parts[1][part])
                spot = at + part * width
                if part != 1:
                    bias_ref[0:1, spot : spot + PAIR] += jnp.sum(value, axis=0, keepdims=True)
                dproj_ref[:, spot : spot + PAIR] = value.astype(jnp.bfloat16)
        total = total + dot_nt(dproj_ref[:, base : base + 3 * width], w_ref[half])
    dx_ref[...] = total
    low_ref[...] = total.astype(jnp.bfloat16)


def weight_grad_kernel(left_ref, right_ref, out_ref, turned_ref):
    @pl.when(pl.program_id(0) == 0)
    def _():
        turned_ref[...] = left_ref[...].T

    out_ref[0] = dot_nn(turned_ref[...], right_ref[...]).astype(jnp.bfloat16)


def weight_grad(left, right, groups, tile):
    rows, depth = left.shape
    columns = right.shape[1]
    per = columns // groups // tile
    return pl.pallas_call(
        weight_grad_kernel,
        grid=(columns // tile,),
        in_specs=[
            pl.BlockSpec((rows, depth), lambda i: (0, 0), pipeline_mode=pl.Buffered(1)),
            pl.BlockSpec((rows, tile), lambda i: (0, i)),
        ],
        out_specs=pl.BlockSpec((1, depth, tile), lambda i: (i // per, 0, i % per)),
        out_shape=jax.ShapeDtypeStruct((groups, depth, columns // groups), jnp.bfloat16),
        scratch_shapes=[pltpu.VMEM((depth, rows), jnp.bfloat16)],
        compiler_params=pltpu.CompilerParams(vmem_limit_bytes=big_vmem),
        cost_estimate=pl.CostEstimate(
            flops=2 * rows * depth * columns,
            bytes_accessed=2 * (rows * depth + rows * columns + depth * columns),
            transcendentals=0,
        ),
        name="weight_grad",
    )(left, right)


def contrast_kernel(
    count, own, halves, cls_ref, q_ref, pos_ref, qg_ref, lead_ref, loss_ref,
    all_ref, part_ref, got_ref, stat_ref, term_ref,
    sem_a, sem_b, sem_c, sem_d, sem_e, sem_f, sem_g, sem_h,
):
    me = lax.axis_index("dp")
    half = lax.axis_index("tensor")
    other = 1 - half
    barrier = pltpu.get_barrier_semaphore()

    @pl.loop(1, count)
    def _(gap):
        pl.semaphore_signal(
            barrier, inc=1, device_id=(lax.rem(me + gap, count), half), device_id_type=MESH
        )

    pl.semaphore_signal(barrier, inc=1, device_id=(me, other), device_id_type=MESH)
    pl.semaphore_wait(barrier, count)

    def push(source, target, sends, lands, gap):
        peer = lax.rem(me + gap, count)
        return pltpu.make_async_remote_copy(
            src_ref=source(peer),
            dst_ref=target.at[me],
            send_sem=sends.at[gap],
            recv_sem=lands.at[me],
            device_id=(peer, half),
            device_id_type=MESH,
        )

    def landed(source, target, sends, lands, gap):
        origin = lax.rem(me + count - gap, count)
        return pltpu.make_async_remote_copy(
            src_ref=target.at[origin],
            dst_ref=target.at[origin],
            send_sem=sends.at[gap],
            recv_sem=lands.at[origin],
            device_id=(origin, half),
            device_id_type=MESH,
        )

    def whole(peer):
        return cls_ref

    @pl.loop(1, count)
    def _(gap):
        push(whole, all_ref, sem_a, sem_b, gap).start()

    all_ref[me] = cls_ref[...]

    @pl.loop(1, count)
    def _(gap):
        landed(whole, all_ref, sem_a, sem_b, gap).wait_recv()

    passages = all_ref[...].reshape(count * own, D).astype(jnp.bfloat16)
    queries = q_ref[...]
    logits = dot_nt(queries, passages)
    column = lax.broadcasted_iota(jnp.int32, logits.shape, 1)
    near = column % own
    kind = own // 2
    index = (column // own) * (own * halves) + (near // kind) * (kind * halves)
    index = index + half * kind + near % kind
    chosen = jnp.where(index == pos_ref[...], 1.0, 0.0)
    highest = jnp.max(logits, axis=1, keepdims=True)
    summed = jnp.sum(jnp.exp(logits - highest), axis=1, keepdims=True)
    picked = jnp.sum(logits * chosen, axis=1, keepdims=True)
    lane = lax.broadcasted_iota(jnp.int32, (logits.shape[0], 128), 1)
    stat_ref[half] = jnp.where(lane == 0, highest, jnp.where(lane == 1, summed, picked))

    def swap(ref, send, land):
        return pltpu.make_async_remote_copy(
            src_ref=ref.at[half],
            dst_ref=ref.at[half],
            send_sem=send,
            recv_sem=land,
            device_id=(me, other),
            device_id_type=MESH,
        )

    def swapped(ref, send, land):
        return pltpu.make_async_remote_copy(
            src_ref=ref.at[other],
            dst_ref=ref.at[other],
            send_sem=send,
            recv_sem=land,
            device_id=(me, other),
            device_id_type=MESH,
        )

    swap(stat_ref, sem_e, sem_f).start()
    swapped(stat_ref, sem_e, sem_f).wait_recv()
    low, high = stat_ref[0], stat_ref[1]
    top = jnp.maximum(low[:, 0:1], high[:, 0:1])
    total = low[:, 1:2] * jnp.exp(low[:, 0:1] - top) + high[:, 1:2] * jnp.exp(high[:, 0:1] - top)
    losses = top + jnp.log(total) - (low[:, 2:3] + high[:, 2:3])
    loss_ref[...] = jnp.broadcast_to(jnp.sum(losses, axis=0, keepdims=True), loss_ref.shape)
    logit_back = (jnp.exp(logits - top) / total - chosen).astype(jnp.bfloat16)
    terms = dot_tn(logit_back, queries)
    part_ref[...] = terms.reshape(count, own, D)

    def piece(peer):
        return part_ref.at[peer]

    @pl.loop(1, count)
    def _(gap):
        push(piece, got_ref, sem_c, sem_d, gap).start()

    term_ref[half] = dot_nn(logit_back, passages)
    swap(term_ref, sem_g, sem_h).start()
    got_ref[me] = part_ref[me]
    swapped(term_ref, sem_g, sem_h).wait_recv()
    qg_ref[...] = term_ref[0] + term_ref[1]

    @pl.loop(1, count)
    def _(gap):
        landed(piece, got_ref, sem_c, sem_d, gap).wait_recv()

    lead_ref[...] = jnp.sum(got_ref[...], axis=0)

    @pl.loop(1, count)
    def _(gap):
        push(whole, all_ref, sem_a, sem_b, gap).wait_send()
        push(piece, got_ref, sem_c, sem_d, gap).wait_send()

    swap(stat_ref, sem_e, sem_f).wait_send()
    swap(term_ref, sem_g, sem_h).wait_send()


def contrast(leading, queries, positives):
    count = lax.axis_size("dp")
    halves = lax.axis_size("tensor")
    own = leading.shape[0]
    here = queries.shape[0]
    whole = pl.BlockSpec(memory_space=pltpu.VMEM)
    query_gradient, lead_back, loss = pl.pallas_call(
        functools.partial(contrast_kernel, count, own, halves),
        in_specs=[whole] * 3,
        out_specs=[whole] * 3,
        out_shape=[
            jax.ShapeDtypeStruct((here, D), jnp.float32),
            jax.ShapeDtypeStruct((own, D), jnp.float32),
            jax.ShapeDtypeStruct((8, 128), jnp.float32),
        ],
        scratch_shapes=[
            pltpu.VMEM((count, own, D), jnp.float32),
            pltpu.VMEM((count, own, D), jnp.float32),
            pltpu.VMEM((count, own, D), jnp.float32),
            pltpu.VMEM((halves, here, 128), jnp.float32),
            pltpu.VMEM((halves, here, D), jnp.float32),
            pltpu.SemaphoreType.DMA((count,)),
            pltpu.SemaphoreType.DMA((count,)),
            pltpu.SemaphoreType.DMA((count,)),
            pltpu.SemaphoreType.DMA((count,)),
            pltpu.SemaphoreType.DMA,
            pltpu.SemaphoreType.DMA,
            pltpu.SemaphoreType.DMA,
            pltpu.SemaphoreType.DMA,
        ],
        compiler_params=pltpu.CompilerParams(
            collective_id=1, has_side_effects=True, vmem_limit_bytes=big_vmem
        ),
        name="contrast",
    )(leading.astype(jnp.float32), queries, positives.reshape(here, 1))
    return query_gradient, lead_back, loss[0, 0]


def total_kernel(bits, value_ref, out_ref, slots, send_sem, recv_sem):
    me = lax.axis_index("dp")
    half = lax.axis_index("tensor")

    def partner(stage):
        if stage == bits:
            return (me, 1 - half)
        gap = 1 << stage
        up = 1 - 2 * lax.rem(me // gap, 2)
        return (me + up * gap, half)

    barrier = pltpu.get_barrier_semaphore()
    for stage in range(bits + 1):
        pl.semaphore_signal(barrier, inc=1, device_id=partner(stage), device_id_type=MESH)
    pl.semaphore_wait(barrier, bits + 1)
    out_ref[...] = value_ref[...]
    slots[0] = value_ref[...]
    copies = []
    for stage in range(bits + 1):
        copy = pltpu.make_async_remote_copy(
            src_ref=slots.at[2 * stage],
            dst_ref=slots.at[2 * stage + 1],
            send_sem=send_sem.at[stage],
            recv_sem=recv_sem.at[stage],
            device_id=partner(stage),
            device_id_type=MESH,
        )
        copy.start()
        copies.append(copy)
        copy.wait_recv()
        summed = slots[2 * stage] + slots[2 * stage + 1]
        if stage < bits:
            slots[2 * stage + 2] = summed
        else:
            out_ref[...] = summed
    for copy in copies:
        copy.wait_send()


def all_total(value):
    bits = (lax.axis_size("dp") - 1).bit_length()
    whole = pl.BlockSpec(memory_space=pltpu.VMEM)
    return pl.pallas_call(
        functools.partial(total_kernel, bits),
        in_specs=[whole],
        out_specs=whole,
        out_shape=jax.ShapeDtypeStruct(value.shape, value.dtype),
        scratch_shapes=[
            pltpu.VMEM((2 * bits + 2,) + value.shape, value.dtype),
            pltpu.SemaphoreType.DMA((bits + 1,)),
            pltpu.SemaphoreType.DMA((bits + 1,)),
        ],
        compiler_params=pltpu.CompilerParams(collective_id=2, has_side_effects=True),
        name="all_total",
    )(value)


def tensor_swap(value):
    return lax.ppermute(value, "tensor", [(0, 1), (1, 0)])


def gathered(own):
    return lax.all_gather(own, ("tensor", "dp"), axis=0, tiled=True).reshape(
        lax.axis_size("tensor"), -1, own.shape[1]
    )


def scattered(whole):
    return lax.psum_scatter(
        whole.reshape(-1, whole.shape[2]), ("tensor", "dp"), scatter_dimension=0, tiled=True
    ).astype(jnp.float32)


def row_spec(rows, columns):
    return pl.BlockSpec((rows, columns), lambda i: (i, 0))


def full_spec(shape):
    return pl.BlockSpec(shape, lambda i: (0,) * len(shape), pipeline_mode=pl.Buffered(1))


def shards(
    short_tokens,
    long_tokens,
    short_cotangent,
    long_cotangent,
    short_lengths,
    long_lengths,
    queries,
    positives,
    step_count,
    mixing_weight,
    mixing_moment,
    mixing_square,
    mixing_average,
    merging_weight,
    merging_moment,
    merging_square,
    merging_average,
    expand_weight,
    expand_moment,
    expand_square,
    expand_average,
    shrink_weight,
    shrink_moment,
    shrink_square,
    shrink_average,
    scales_weight,
    scales_moment,
    scales_square,
    scales_average,
    offsets_weight,
    offsets_moment,
    offsets_square,
    offsets_average,
):
    halves = lax.axis_size("tensor")
    place = lax.axis_index("tensor")
    short_span = short_tokens.shape[1]
    long_span = long_tokens.shape[1]
    shorts = short_tokens.shape[0] // halves
    longs = long_tokens.shape[0] // halves
    chunk = long_span
    piece = short_span
    assert shorts * short_span == chunk and shorts == longs
    chunks = longs + 1
    rows = chunks * chunk
    width = mixing_weight.shape[2]
    wide = expand_weight.shape[1]

    def own_half(short_all, long_all):
        return jnp.concatenate(
            [
                lax.dynamic_slice_in_dim(short_all, place * shorts, shorts).reshape(-1, D),
                lax.dynamic_slice_in_dim(long_all, place * longs, longs).reshape(-1, D),
            ],
            axis=0,
        )

    def both_halves(own, other):
        own_first = place == 0
        low = jnp.where(own_first, own, other)
        high = jnp.where(own_first, other, own)
        head = shorts * short_span
        return (
            jnp.concatenate([low[:head], high[:head]]).reshape(short_tokens.shape),
            jnp.concatenate([low[head:], high[head:]]).reshape(long_tokens.shape),
        )

    mixing_full = gathered(mixing_weight.astype(jnp.bfloat16).reshape(-1, 3 * width))
    merging_full = gathered(merging_weight.T.astype(jnp.bfloat16))
    expand_full = gathered(expand_weight.astype(jnp.bfloat16))
    shrink_full = gathered(shrink_weight.T.astype(jnp.bfloat16))
    offsets_other = tensor_swap(offsets_weight)
    offsets_both = jnp.where(
        place == 0,
        jnp.stack([offsets_weight, offsets_other]),
        jnp.stack([offsets_other, offsets_weight]),
    )
    mixing_bias = jnp.concatenate(
        [
            offsets_both[:, :width],
            jnp.zeros((halves, width), jnp.float32),
            offsets_both[:, width : 2 * width],
        ],
        axis=1,
    ).reshape(1, -1)
    upward_bias = offsets_both[:, 2 * width :].reshape(1, -1)
    short_limits = lax.dynamic_slice_in_dim(short_lengths, place * shorts, shorts)
    long_limits = lax.dynamic_slice_in_dim(long_lengths, place * longs, longs)
    spans = jnp.concatenate(
        [
            short_limits[None, :],
            long_limits[:, None] - piece * jnp.arange(chunk // piece, dtype=jnp.int32)[None, :],
        ],
        axis=0,
    )
    inputs = own_half(short_tokens, long_tokens)
    cotangent = own_half(short_cotangent, long_cotangent)
    bf16, f32 = jnp.bfloat16, jnp.float32

    def shaped(columns, dtype):
        return jax.ShapeDtypeStruct((rows, columns), dtype)

    smem = pl.BlockSpec(memory_space=pltpu.SMEM)
    params = pltpu.CompilerParams(vmem_limit_bytes=big_vmem)
    mixing_columns = halves * 3 * width
    scores_flops = 2 * rows * chunk * PAIR * (halves * width // HEAD_DIM)
    qkv, context = pl.pallas_call(
        functools.partial(attend_forward_kernel, piece),
        grid=(chunks,),
        in_specs=[
            smem,
            row_spec(chunk, D),
            full_spec(mixing_full.shape),
            full_spec(mixing_bias.shape),
        ],
        out_specs=[row_spec(chunk, mixing_columns), row_spec(chunk, D)],
        out_shape=[shaped(mixing_columns, bf16), shaped(D, bf16)],
        compiler_params=params,
        cost_estimate=pl.CostEstimate(
            flops=2 * rows * D * mixing_columns + 6 * scores_flops,
            bytes_accessed=16 * 1024 * 1024,
            transcendentals=rows * chunk * 12,
        ),
        name="attend_forward",
    )(spans, inputs, mixing_full, mixing_bias)
    output, hidden_low, activated, slope, normed_first, rstd_first, normed_second, rstd_second = (
        pl.pallas_call(
            feed_forward_kernel,
            grid=(chunks,),
            in_specs=[
                row_spec(chunk, D),
                row_spec(chunk, D),
                full_spec(merging_full.shape),
                full_spec(expand_full.shape),
                full_spec(shrink_full.shape),
                full_spec(scales_weight.shape),
                full_spec(upward_bias.shape),
            ],
            out_specs=[
                row_spec(chunk, D),
                row_spec(chunk, D),
                row_spec(chunk, FF),
                row_spec(chunk, FF),
                row_spec(chunk, D),
                row_spec(chunk, 1),
                row_spec(chunk, D),
                row_spec(chunk, 1),
            ],
            out_shape=[
                shaped(D, bf16),
                shaped(D, bf16),
                shaped(FF, bf16),
                shaped(FF, bf16),
                shaped(D, f32),
                shaped(1, f32),
                shaped(D, f32),
                shaped(1, f32),
            ],
            compiler_params=params,
            cost_estimate=pl.CostEstimate(
                flops=2 * rows * D * (D + 2 * FF),
                bytes_accessed=48 * 1024 * 1024,
                transcendentals=2 * rows * FF,
            ),
            name="feed_forward",
        )(
            context,
            inputs,
            merging_full,
            expand_full,
            shrink_full,
            scales_weight,
            upward_bias,
        )
    )
    output_other = tensor_swap(output)
    leading = jnp.concatenate([output[: shorts * piece : piece], output[chunk::chunk]], axis=0)
    query_gradient, lead_back, loss_part = contrast(leading, queries, positives)
    lead_rows = jnp.zeros((chunks, 8, D), f32)
    lead_rows = lead_rows.at[0, :shorts].set(lead_back[:shorts])
    lead_rows = lead_rows.at[1:, 0].set(lead_back[shorts:])
    down_low, upward_low, first_low, first_back, context_back, vector_grad, upward_grad = (
        pl.pallas_call(
            functools.partial(feed_back_kernel, piece),
            grid=(chunks,),
            in_specs=[
                row_spec(chunk, D),
                pl.BlockSpec((1, 8, D), lambda i: (i, 0, 0)),
                row_spec(chunk, D),
                row_spec(chunk, 1),
                row_spec(chunk, D),
                row_spec(chunk, 1),
                row_spec(chunk, FF),
                full_spec(merging_full.shape),
                full_spec(expand_full.shape),
                full_spec(shrink_full.shape),
                full_spec(scales_weight.shape),
            ],
            out_specs=[
                row_spec(chunk, D),
                row_spec(chunk, FF),
                row_spec(chunk, D),
                row_spec(chunk, D),
                row_spec(chunk, D),
                pl.BlockSpec((8, D), lambda i: (0, 0)),
                pl.BlockSpec((8, FF), lambda i: (0, 0)),
            ],
            out_shape=[
                shaped(D, bf16),
                shaped(FF, bf16),
                shaped(D, bf16),
                shaped(D, f32),
                shaped(D, bf16),
                jax.ShapeDtypeStruct((8, D), f32),
                jax.ShapeDtypeStruct((8, FF), f32),
            ],
            compiler_params=params,
            cost_estimate=pl.CostEstimate(
                flops=2 * rows * D * (D + 2 * FF),
                bytes_accessed=48 * 1024 * 1024,
                transcendentals=0,
            ),
            name="feed_back",
        )(
            cotangent,
            lead_rows,
            normed_first,
            rstd_first,
            normed_second,
            rstd_second,
            slope,
            merging_full,
            expand_full,
            shrink_full,
            scales_weight,
        )
    )
    shrink_sum = scattered(weight_grad(down_low, activated, halves, 512))
    expand_sum = scattered(weight_grad(hidden_low, upward_low, halves, 512))
    merging_sum = scattered(weight_grad(first_low, context, halves, 384))
    projected_back, input_back, input_low, bias_grad = pl.pallas_call(
        functools.partial(attend_back_kernel, piece),
        grid=(chunks,),
        in_specs=[
            smem,
            row_spec(chunk, mixing_columns),
            row_spec(chunk, D),
            row_spec(chunk, D),
            full_spec(mixing_full.shape),
        ],
        out_specs=[
            row_spec(chunk, mixing_columns),
            row_spec(chunk, D),
            row_spec(chunk, D),
            pl.BlockSpec((8, mixing_columns), lambda i: (0, 0)),
        ],
        out_shape=[
            shaped(mixing_columns, bf16),
            shaped(D, f32),
            shaped(D, bf16),
            jax.ShapeDtypeStruct((8, mixing_columns), f32),
        ],
        compiler_params=params,
        cost_estimate=pl.CostEstimate(
            flops=2 * rows * D * mixing_columns + 15 * scores_flops,
            bytes_accessed=24 * 1024 * 1024,
            transcendentals=rows * chunk * 12,
        ),
        name="attend_back",
    )(spans, qkv, context_back, first_back, mixing_full)
    input_other = tensor_swap(input_low)
    mixing_sum = scattered(weight_grad(inputs, projected_back, halves, 384))

    short_output, long_output = both_halves(output, output_other)
    short_gradient, long_gradient = both_halves(input_back, input_other.astype(f32))

    bias_both = bias_grad[0].reshape(halves, 3, width)
    offsets_grad = jnp.concatenate(
        [bias_both[:, 0], bias_both[:, 2], upward_grad[0].reshape(halves, wide)], axis=1
    )
    reduced = (mixing_sum.reshape(mixing_weight.shape), merging_sum.T, expand_sum, shrink_sum.T)
    squares_part = jnp.sum(mixing_sum * mixing_sum) + jnp.sum(merging_sum * merging_sum)
    squares_part = squares_part + jnp.sum(expand_sum * expand_sum)
    squares_part = squares_part + jnp.sum(shrink_sum * shrink_sum)
    lane = lax.broadcasted_iota(jnp.int32, (1, D), 1)
    scalars = jnp.where(lane == 0, squares_part, jnp.where(lane == 1, loss_part, 0.0))
    stacked = jnp.concatenate(
        [vector_grad[:6], offsets_grad.reshape(-1, D), scalars, jnp.zeros((3, D), f32)], axis=0
    )
    summed = all_total(stacked)
    scales_sum = summed[:6]
    offsets_all = summed[6:12].reshape(halves, -1)
    offsets_sum = jnp.where(place == 0, offsets_all[0], offsets_all[1])
    squares_all = summed[12, 0] + jnp.sum(summed[:12] * summed[:12])
    loss_all = summed[12, 1] / halves
    norm_value = jnp.sqrt(squares_all)
    factor = clip_limit / jnp.maximum(norm_value, clip_limit)
    steps_float = step_count[0].astype(jnp.float32)
    first_fix = 1.0 - jnp.power(first_decay, steps_float)
    second_fix = 1.0 - jnp.power(second_decay, steps_float)

    def update(weight, moment, square, average, gradient, rate):
        clipped = gradient * factor
        first = first_decay * moment + (1.0 - first_decay) * clipped
        second = second_decay * square + (1.0 - second_decay) * clipped * clipped
        master = weight - rate * (
            first / first_fix / (jnp.sqrt(second / second_fix) + adam_eps) + decay_weight * weight
        )
        smooth = smooth_decay * average + (1.0 - smooth_decay) * master
        return (master, first, second, smooth)

    mixing_new = update(
        mixing_weight, mixing_moment, mixing_square, mixing_average, reduced[0], 1.0 / math.sqrt(D)
    )
    merging_new = update(
        merging_weight,
        merging_moment,
        merging_square,
        merging_average,
        reduced[1],
        8.0 / math.sqrt(D),
    )
    expand_new = update(
        expand_weight, expand_moment, expand_square, expand_average, reduced[2], 1.0 / math.sqrt(D)
    )
    shrink_new = update(
        shrink_weight, shrink_moment, shrink_square, shrink_average, reduced[3], 1.0 / math.sqrt(FF)
    )
    scales_new = update(
        scales_weight, scales_moment, scales_square, scales_average, scales_sum, 0.3
    )
    offsets_new = update(
        offsets_weight, offsets_moment, offsets_square, offsets_average, offsets_sum, 0.3
    )
    contrast_loss = (loss_all / (queries.shape[0] * lax.axis_size("dp"))).reshape(1)
    gradient_norm = norm_value.reshape(1)
    return (
        (
            short_output,
            long_output,
            short_gradient,
            long_gradient,
            query_gradient,
            contrast_loss,
            gradient_norm,
        )
        + mixing_new
        + merging_new
        + expand_new
        + shrink_new
        + scales_new
        + offsets_new
    )


def solution(mesh):
    placed = (
        P("dp", None, None),
        P("dp", None, None),
        P("dp", None, None),
        P("dp", None, None),
        P("dp"),
        P("dp"),
        P("dp", None),
        P("dp"),
        P(),
        P("dp", None, "tensor"),
        P("dp", None, "tensor"),
        P("dp", None, "tensor"),
        P("dp", None, "tensor"),
        P("tensor", "dp"),
        P("tensor", "dp"),
        P("tensor", "dp"),
        P("tensor", "dp"),
        P("dp", "tensor"),
        P("dp", "tensor"),
        P("dp", "tensor"),
        P("dp", "tensor"),
        P("tensor", "dp"),
        P("tensor", "dp"),
        P("tensor", "dp"),
        P("tensor", "dp"),
        P(),
        P(),
        P(),
        P(),
        P("tensor"),
        P("tensor"),
        P("tensor"),
        P("tensor"),
    )
    return jax.shard_map(
        shards,
        mesh=mesh,
        in_specs=placed,
        out_specs=(
            P("dp", None, None),
            P("dp", None, None),
            P("dp", None, None),
            P("dp", None, None),
            P("dp", None),
            P(),
            P(),
            P("dp", None, "tensor"),
            P("dp", None, "tensor"),
            P("dp", None, "tensor"),
            P("dp", None, "tensor"),
            P("tensor", "dp"),
            P("tensor", "dp"),
            P("tensor", "dp"),
            P("tensor", "dp"),
            P("dp", "tensor"),
            P("dp", "tensor"),
            P("dp", "tensor"),
            P("dp", "tensor"),
            P("tensor", "dp"),
            P("tensor", "dp"),
            P("tensor", "dp"),
            P("tensor", "dp"),
            P(),
            P(),
            P(),
            P(),
            P("tensor"),
            P("tensor"),
            P("tensor"),
            P("tensor"),
        ),
        check_vma=False,
    )
```

```python
import functools
import math

import jax
import jax.numpy as jnp
from jax import lax
from jax.experimental import pallas as pl
from jax.experimental.pallas import tpu as pltpu
from jax.sharding import PartitionSpec as P

D = 768
FF = 3072
HEAD_DIM = 64
PAIR = 2 * HEAD_DIM
MESH = pl.DeviceIdType.MESH

norm_eps = 1e-05
score_scale = 0.125
masked_value = -1e30
first_decay = 0.5
second_decay = 0.75
smooth_decay = 0.75
decay_weight = 0.01
adam_eps = 1e-08
clip_limit = 1.0
inverse_root_two = 0.7071067811865476
inverse_root_tau = 0.3989422804014327
big_vmem = 56 * 1024 * 1024


def dot_nn(a, b):
    return lax.dot_general(a, b, (((1,), (0,)), ((), ())), preferred_element_type=jnp.float32)


def dot_nt(a, b):
    return lax.dot_general(a, b, (((1,), (1,)), ((), ())), preferred_element_type=jnp.float32)


def dot_tn(a, b):
    return lax.dot_general(a, b, (((0,), (0,)), ((), ())), preferred_element_type=jnp.float32)


def layer_stats(resid):
    centre = resid - jnp.mean(resid, axis=-1, keepdims=True)
    rstd = lax.rsqrt(jnp.mean(centre * centre, axis=-1, keepdims=True) + norm_eps)
    return (centre * rstd, rstd)


def layer_back(gradient, normed, rstd, gain):
    scaled = gradient * gain
    return rstd * (
        scaled
        - jnp.mean(scaled, axis=-1, keepdims=True)
        - normed * jnp.mean(scaled * normed, axis=-1, keepdims=True)
    )


def visible_keys(spans, step, rows, piece, key_axis):
    shape = (rows, 1) if key_axis == 0 else (1, rows)
    place = lax.broadcasted_iota(jnp.int32, shape, key_axis)
    segment = place // piece
    limit = jnp.zeros(shape, jnp.int32)
    for index in range(rows // piece):
        limit = jnp.where(segment == index, spans[step, index], limit)
    key_valid = (place % piece) < limit
    first = lax.broadcasted_iota(jnp.int32, (rows, rows), 0) // piece
    second = lax.broadcasted_iota(jnp.int32, (rows, rows), 1) // piece
    return jnp.logical_and(jnp.logical_or(first == second, step > 0), key_valid)


def own_lanes(value, which):
    lane = lax.broadcasted_iota(jnp.int32, value.shape, 1)
    return jnp.where((lane // HEAD_DIM) == which, value, jnp.zeros_like(value))


def join_lanes(low, high):
    lane = lax.broadcasted_iota(jnp.int32, low.shape, 1)
    return jnp.where(lane < HEAD_DIM, low, high)


def attend_half(half, weight, bias, visible, x_ref, qkv_ref, ctx_ref):
    width = weight.shape[1] // 3
    base = half * 3 * width
    projected = dot_nn(x_ref[...], weight) + bias
    qkv_ref[:, base : base + 3 * width] = projected.astype(jnp.bfloat16)
    for pair in range(width // PAIR):
        at = base + pair * PAIR
        q = qkv_ref[:, at : at + PAIR] * jnp.bfloat16(score_scale)
        k = qkv_ref[:, at + width : at + width + PAIR]
        v = qkv_ref[:, at + 2 * width : at + 2 * width + PAIR]
        parts = []
        for which in range(2):
            scores = jnp.where(visible, dot_nt(own_lanes(q, which), k), masked_value)
            powered = jnp.exp(scores - jnp.max(scores, axis=-1, keepdims=True))
            weights = powered * (1.0 / jnp.sum(powered, axis=-1, keepdims=True))
            parts.append(dot_nn(weights.astype(jnp.bfloat16), v))
        at = half * width + pair * PAIR
        ctx_ref[:, at : at + PAIR] = join_lanes(*parts).astype(jnp.bfloat16)


def attend_forward_kernel(piece, spans, x_ref, w_ref, bias_ref, qkv_ref, ctx_ref):
    step = pl.program_id(0)
    rows = x_ref.shape[0]
    width = w_ref.shape[2] // 3
    visible = visible_keys(spans, step, rows, piece, 1)
    for half in range(w_ref.shape[0]):
        bias = bias_ref[:, half * 3 * width : (half + 1) * 3 * width]
        attend_half(half, w_ref[half], bias, visible, x_ref, qkv_ref, ctx_ref)


def feed_forward_kernel(
    ctx_ref, x_ref, me_ref, st_ref, scales_ref, bu_ref,
    out_ref, hb_ref, g_ref, slope_ref, n1_ref, r1_ref, n2_ref, r2_ref,
):
    wide = st_ref.shape[2]
    width = me_ref.shape[2] - wide
    attention = scales_ref[4:5, :]
    for half in range(me_ref.shape[0]):
        attention = attention + dot_nt(
            ctx_ref[:, half * width : (half + 1) * width], me_ref[half, :, :width]
        )
    normed, rstd = layer_stats(x_ref[...].astype(jnp.float32) + attention)
    n1_ref[...] = normed
    r1_ref[...] = rstd
    hidden = normed * scales_ref[0:1, :] + scales_ref[1:2, :]
    hidden_low = hidden.astype(jnp.bfloat16)
    hb_ref[...] = hidden_low
    downward = scales_ref[5:6, :]
    for half in range(st_ref.shape[0]):
        at = half * wide
        upward = dot_nn(hidden_low, me_ref[half, :, width:]) + bu_ref[:, at : at + wide]
        cumulative = 0.5 * (1.0 + lax.erf(upward * inverse_root_two))
        density = jnp.exp(-0.5 * upward * upward) * inverse_root_tau
        activated = (upward * cumulative).astype(jnp.bfloat16)
        g_ref[:, at : at + wide] = activated
        slope_ref[:, at : at + wide] = (cumulative + upward * density).astype(jnp.bfloat16)
        downward = downward + dot_nt(activated, st_ref[half])
    normed, rstd = layer_stats(hidden + downward)
    n2_ref[...] = normed
    r2_ref[...] = rstd
    out_ref[...] = (normed * scales_ref[2:3, :] + scales_ref[3:4, :]).astype(jnp.bfloat16)


def add_row(ref, index, value):
    ref[index : index + 1, :] += jnp.sum(value, axis=0, keepdims=True)


def feed_back_kernel(
    piece, cot_ref, lead_ref, n1_ref, r1_ref, n2_ref, r2_ref, slope_ref, me_ref, st_ref, scales_ref,
    dz_ref, dub_ref, da_ref, dr1_ref, dctx_ref, vec_ref, up_ref,
):
    @pl.when(pl.program_id(0) == 0)
    def _():
        vec_ref[...] = jnp.zeros_like(vec_ref)
        up_ref[...] = jnp.zeros_like(up_ref)

    wide = st_ref.shape[2]
    width = me_ref.shape[2] - wide
    dout = cot_ref[...].astype(jnp.float32)
    row = lax.broadcasted_iota(jnp.int32, dout.shape, 0)
    for index in range(dout.shape[0] // piece):
        dout = dout + jnp.where(row == index * piece, lead_ref[0, index : index + 1, :], 0.0)
    normed = n2_ref[...]
    add_row(vec_ref, 2, dout * normed)
    add_row(vec_ref, 3, dout)
    second = layer_back(dout, normed, r2_ref[...], scales_ref[2:3, :])
    add_row(vec_ref, 5, second)
    low = second.astype(jnp.bfloat16)
    dz_ref[...] = low
    hidden_back = second
    for half in range(st_ref.shape[0]):
        at = half * wide
        upward = dot_nn(low, st_ref[half]) * slope_ref[:, at : at + wide].astype(jnp.float32)
        up_ref[0:1, at : at + wide] += jnp.sum(upward, axis=0, keepdims=True)
        upward_low = upward.astype(jnp.bfloat16)
        dub_ref[:, at : at + wide] = upward_low
        hidden_back = hidden_back + dot_nt(upward_low, me_ref[half, :, width:])
    normed = n1_ref[...]
    add_row(vec_ref, 0, hidden_back * normed)
    add_row(vec_ref, 1, hidden_back)
    first = layer_back(hidden_back, normed, r1_ref[...], scales_ref[0:1, :])
    add_row(vec_ref, 4, first)
    dr1_ref[...] = first
    low = first.astype(jnp.bfloat16)
    da_ref[...] = low
    for half in range(me_ref.shape[0]):
        dctx_ref[:, half * width : (half + 1) * width] = dot_nn(low, me_ref[half, :, :width]).astype(
            jnp.bfloat16
        )


def attend_back_kernel(
    piece, spans, qkv_ref, dctx_ref, dr1_ref, w_ref, dproj_ref, dx_ref, low_ref, bias_ref
):
    step = pl.program_id(0)

    @pl.when(step == 0)
    def _():
        bias_ref[...] = jnp.zeros_like(bias_ref)

    rows = qkv_ref.shape[0]
    width = w_ref.shape[2] // 3
    visible = visible_keys(spans, step, rows, piece, 0)
    total = dr1_ref[...]
    for half in range(w_ref.shape[0]):
        base = half * 3 * width
        for pair in range(width // PAIR):
            at = base + pair * PAIR
            q = qkv_ref[:, at : at + PAIR]
            k = qkv_ref[:, at + width : at + width + PAIR]
            v = qkv_ref[:, at + 2 * width : at + 2 * width + PAIR]
            near = half * width + pair * PAIR
            back = dctx_ref[:, near : near + PAIR]
            parts = []
            for which in range(2):
                scores = dot_nt(own_lanes(k, which) * jnp.bfloat16(score_scale), q)
                scores = jnp.where(visible, scores, masked_value)
                powered = jnp.exp(scores - jnp.max(scores, axis=0, keepdims=True))
                weights = powered * (1.0 / jnp.sum(powered, axis=0, keepdims=True))
                weight_back = dot_nt(own_lanes(v, which), back)
                score_back = weights * (
                    weight_back - jnp.sum(weights * weight_back, axis=0, keepdims=True)
                )
                score_low = (score_back * score_scale).astype(jnp.bfloat16)
                parts.append(
                    (
                        dot_tn(score_low, k),
                        dot_nn(score_low, q),
                        dot_nn(weights.astype(jnp.bfloat16), back),
                    )
                )
            for part in range(3):
                value = join_lanes(parts[0][part], parts[1][part])
                spot = at + part * width
                if part != 1:
                    bias_ref[0:1, spot : spot + PAIR] += jnp.sum(value, axis=0, keepdims=True)
                dproj_ref[:, spot : spot + PAIR] = value.astype(jnp.bfloat16)
        total = total + dot_nt(dproj_ref[:, base : base + 3 * width], w_ref[half])
    dx_ref[...] = total
    low_ref[...] = total.astype(jnp.bfloat16)


def weight_grad_kernel(left_ref, right_ref, out_ref, turned_ref):
    @pl.when(pl.program_id(0) == 0)
    def _():
        turned_ref[...] = left_ref[...].T

    out_ref[0] = dot_nn(turned_ref[...], right_ref[...]).astype(jnp.bfloat16)


def weight_grad(left, right, groups, tile):
    rows, depth = left.shape
    columns = right.shape[1]
    per = columns // groups // tile
    return pl.pallas_call(
        weight_grad_kernel,
        grid=(columns // tile,),
        in_specs=[
            pl.BlockSpec((rows, depth), lambda i: (0, 0), pipeline_mode=pl.Buffered(1)),
            pl.BlockSpec((rows, tile), lambda i: (0, i)),
        ],
        out_specs=pl.BlockSpec((1, depth, tile), lambda i: (i // per, 0, i % per)),
        out_shape=jax.ShapeDtypeStruct((groups, depth, columns // groups), jnp.bfloat16),
        scratch_shapes=[pltpu.VMEM((depth, rows), jnp.bfloat16)],
        compiler_params=pltpu.CompilerParams(vmem_limit_bytes=big_vmem),
        cost_estimate=pl.CostEstimate(
            flops=2 * rows * depth * columns,
            bytes_accessed=2 * (rows * depth + rows * columns + depth * columns),
            transcendentals=0,
        ),
        name="weight_grad",
    )(left, right)


def contrast_kernel(
    count, own, halves, cls_ref, q_ref, pos_ref, qg_ref, lead_ref, loss_ref,
    all_ref, part_ref, got_ref, stat_ref, term_ref,
    sem_a, sem_b, sem_c, sem_d, sem_e, sem_f, sem_g, sem_h,
):
    me = lax.axis_index("dp")
    half = lax.axis_index("tensor")
    other = 1 - half
    barrier = pltpu.get_barrier_semaphore()

    @pl.loop(1, count)
    def _(gap):
        pl.semaphore_signal(
            barrier, inc=1, device_id=(lax.rem(me + gap, count), half), device_id_type=MESH
        )

    pl.semaphore_signal(barrier, inc=1, device_id=(me, other), device_id_type=MESH)
    pl.semaphore_wait(barrier, count)

    def push(source, target, sends, lands, gap):
        peer = lax.rem(me + gap, count)
        return pltpu.make_async_remote_copy(
            src_ref=source(peer),
            dst_ref=target.at[me],
            send_sem=sends.at[gap],
            recv_sem=lands.at[me],
            device_id=(peer, half),
            device_id_type=MESH,
        )

    def landed(source, target, sends, lands, gap):
        origin = lax.rem(me + count - gap, count)
        return pltpu.make_async_remote_copy(
            src_ref=target.at[origin],
            dst_ref=target.at[origin],
            send_sem=sends.at[gap],
            recv_sem=lands.at[origin],
            device_id=(origin, half),
            device_id_type=MESH,
        )

    def whole(peer):
        return cls_ref

    @pl.loop(1, count)
    def _(gap):
        push(whole, all_ref, sem_a, sem_b, gap).start()

    all_ref[me] = cls_ref[...]

    @pl.loop(1, count)
    def _(gap):
        landed(whole, all_ref, sem_a, sem_b, gap).wait_recv()

    passages = all_ref[...].astype(jnp.float32).reshape(count * own, D).astype(jnp.bfloat16)
    queries = q_ref[...]
    logits = dot_nt(queries, passages)
    column = lax.broadcasted_iota(jnp.int32, logits.shape, 1)
    near = column % own
    kind = own // 2
    index = (column // own) * (own * halves) + (near // kind) * (kind * halves)
    index = index + half * kind + near % kind
    chosen = jnp.where(index == pos_ref[...], 1.0, 0.0)
    highest = jnp.max(logits, axis=1, keepdims=True)
    summed = jnp.sum(jnp.exp(logits - highest), axis=1, keepdims=True)
    picked = jnp.sum(logits * chosen, axis=1, keepdims=True)
    lane = lax.broadcasted_iota(jnp.int32, (logits.shape[0], 128), 1)
    stat_ref[half] = jnp.where(lane == 0, highest, jnp.where(lane == 1, summed, picked))

    def swap(ref, send, land):
        return pltpu.make_async_remote_copy(
            src_ref=ref.at[half],
            dst_ref=ref.at[half],
            send_sem=send,
            recv_sem=land,
            device_id=(me, other),
            device_id_type=MESH,
        )

    def swapped(ref, send, land):
        return pltpu.make_async_remote_copy(
            src_ref=ref.at[other],
            dst_ref=ref.at[other],
            send_sem=send,
            recv_sem=land,
            device_id=(me, other),
            device_id_type=MESH,
        )

    swap(stat_ref, sem_e, sem_f).start()
    swapped(stat_ref, sem_e, sem_f).wait_recv()
    low, high = stat_ref[0], stat_ref[1]
    top = jnp.maximum(low[:, 0:1], high[:, 0:1])
    total = low[:, 1:2] * jnp.exp(low[:, 0:1] - top) + high[:, 1:2] * jnp.exp(high[:, 0:1] - top)
    losses = top + jnp.log(total) - (low[:, 2:3] + high[:, 2:3])
    loss_ref[...] = jnp.broadcast_to(jnp.sum(losses, axis=0, keepdims=True), loss_ref.shape)
    logit_back = (jnp.exp(logits - top) / total - chosen).astype(jnp.bfloat16)
    terms = dot_tn(logit_back, queries)
    part_ref[...] = terms.reshape(count, own, D).astype(jnp.bfloat16)

    def piece(peer):
        return part_ref.at[peer]

    @pl.loop(1, count)
    def _(gap):
        push(piece, got_ref, sem_c, sem_d, gap).start()

    term_ref[half] = dot_nn(logit_back, passages)
    swap(term_ref, sem_g, sem_h).start()
    got_ref[me] = part_ref[me]
    swapped(term_ref, sem_g, sem_h).wait_recv()
    qg_ref[...] = term_ref[0] + term_ref[1]

    @pl.loop(1, count)
    def _(gap):
        landed(piece, got_ref, sem_c, sem_d, gap).wait_recv()

    lead_ref[...] = jnp.sum(got_ref[...].astype(jnp.float32), axis=0)

    @pl.loop(1, count)
    def _(gap):
        push(whole, all_ref, sem_a, sem_b, gap).wait_send()
        push(piece, got_ref, sem_c, sem_d, gap).wait_send()

    swap(stat_ref, sem_e, sem_f).wait_send()
    swap(term_ref, sem_g, sem_h).wait_send()


def contrast(leading, queries, positives):
    count = lax.axis_size("dp")
    halves = lax.axis_size("tensor")
    own = leading.shape[0]
    here = queries.shape[0]
    whole = pl.BlockSpec(memory_space=pltpu.VMEM)
    query_gradient, lead_back, loss = pl.pallas_call(
        functools.partial(contrast_kernel, count, own, halves),
        in_specs=[whole] * 3,
        out_specs=[whole] * 3,
        out_shape=[
            jax.ShapeDtypeStruct((here, D), jnp.float32),
            jax.ShapeDtypeStruct((own, D), jnp.float32),
            jax.ShapeDtypeStruct((8, 128), jnp.float32),
        ],
        scratch_shapes=[
            pltpu.VMEM((count, own, D), jnp.bfloat16),
            pltpu.VMEM((count, own, D), jnp.bfloat16),
            pltpu.VMEM((count, own, D), jnp.bfloat16),
            pltpu.VMEM((halves, here, 128), jnp.float32),
            pltpu.VMEM((halves, here, D), jnp.float32),
            pltpu.SemaphoreType.DMA((count,)),
            pltpu.SemaphoreType.DMA((count,)),
            pltpu.SemaphoreType.DMA((count,)),
            pltpu.SemaphoreType.DMA((count,)),
            pltpu.SemaphoreType.DMA,
            pltpu.SemaphoreType.DMA,
            pltpu.SemaphoreType.DMA,
            pltpu.SemaphoreType.DMA,
        ],
        compiler_params=pltpu.CompilerParams(
            collective_id=1, has_side_effects=True, vmem_limit_bytes=big_vmem
        ),
        name="contrast",
    )(leading, queries, positives.reshape(here, 1))
    return query_gradient, lead_back, loss[0, 0]


def total_kernel(bits, value_ref, out_ref, slots, send_sem, recv_sem):
    me = lax.axis_index("dp")
    half = lax.axis_index("tensor")

    def partner(stage):
        if stage == bits:
            return (me, 1 - half)
        gap = 1 << stage
        up = 1 - 2 * lax.rem(me // gap, 2)
        return (me + up * gap, half)

    barrier = pltpu.get_barrier_semaphore()
    for stage in range(bits + 1):
        pl.semaphore_signal(barrier, inc=1, device_id=partner(stage), device_id_type=MESH)
    pl.semaphore_wait(barrier, bits + 1)
    out_ref[...] = value_ref[...]
    slots[0] = value_ref[...]
    copies = []
    for stage in range(bits + 1):
        copy = pltpu.make_async_remote_copy(
            src_ref=slots.at[2 * stage],
            dst_ref=slots.at[2 * stage + 1],
            send_sem=send_sem.at[stage],
            recv_sem=recv_sem.at[stage],
            device_id=partner(stage),
            device_id_type=MESH,
        )
        copy.start()
        copies.append(copy)
        copy.wait_recv()
        summed = slots[2 * stage] + slots[2 * stage + 1]
        if stage < bits:
            slots[2 * stage + 2] = summed
        else:
            out_ref[...] = summed
    for copy in copies:
        copy.wait_send()


def all_total(value):
    bits = (lax.axis_size("dp") - 1).bit_length()
    whole = pl.BlockSpec(memory_space=pltpu.VMEM)
    return pl.pallas_call(
        functools.partial(total_kernel, bits),
        in_specs=[whole],
        out_specs=whole,
        out_shape=jax.ShapeDtypeStruct(value.shape, value.dtype),
        scratch_shapes=[
            pltpu.VMEM((2 * bits + 2,) + value.shape, value.dtype),
            pltpu.SemaphoreType.DMA((bits + 1,)),
            pltpu.SemaphoreType.DMA((bits + 1,)),
        ],
        compiler_params=pltpu.CompilerParams(collective_id=2, has_side_effects=True),
        name="all_total",
    )(value)


def tensor_swap(value):
    return lax.ppermute(value, "tensor", [(0, 1), (1, 0)])


def gathered(own):
    return lax.all_gather(own, ("tensor", "dp"), axis=0, tiled=True).reshape(
        lax.axis_size("tensor"), -1, own.shape[1]
    )


def scattered(whole):
    return lax.psum_scatter(
        whole.reshape(-1, whole.shape[2]), ("tensor", "dp"), scatter_dimension=0, tiled=True
    ).astype(jnp.float32)


def grid_place():
    me = lax.axis_index("dp")
    return lax.axis_index("tensor"), me // 4, lax.rem(me // 2, 2), lax.rem(me, 2)


def at_place(t, z, x, c):
    return (z * 4 + x * 2 + c, t)


def greet_neighbours():
    t, z, x, c = grid_place()
    barrier = pltpu.get_barrier_semaphore()
    others = [at_place(t, lax.rem(z + gap, 4), x, c) for gap in range(1, 4)]
    others += [at_place(1 - t, z, x, c), at_place(t, z, 1 - x, c), at_place(t, z, x, 1 - c)]
    for other in others:
        pl.semaphore_signal(barrier, inc=1, device_id=other, device_id_type=MESH)
    pl.semaphore_wait(barrier, len(others))


class Gather:
    def __init__(self, own, buffer, sends, lands, local, index):
        self.own, self.buffer, self.index = own, buffer, index
        self.sends, self.lands, self.local = sends, lands, local
        t, z, x, c = self.place = grid_place()
        even = c == 0
        self.mid = (jnp.where(even, t, 1 - t), jnp.where(even, 1 - x, x))
        self.last = (jnp.where(even, 1 - t, t), jnp.where(even, x, 1 - x))
        self.both = (1 - t, 1 - x)

    def group(self, spot, c):
        return self.buffer.at[spot[0], :, spot[1], c]

    def slot(self, z):
        t, _, x, c = self.place
        return self.buffer.at[t, z, x, c]

    def copy(self, source, target, which, device):
        return pltpu.make_async_remote_copy(
            src_ref=source,
            dst_ref=target,
            send_sem=self.sends.at[self.index, which],
            recv_sem=self.lands.at[self.index, which],
            device_id=device,
            device_id_type=MESH,
        )

    def outgoing(self, which):
        t, z, x, c = self.place
        if which < 3:
            device = at_place(t, lax.rem(z + which + 1, 4), x, c)
            return self.copy(self.own, self.slot(z), which, device)
        spot = {3: (t, x), 4: (t, x), 5: self.mid, 6: (t, x), 7: self.mid, 8: self.last, 9: self.both}[which]
        group = self.group(spot, c)
        if which == 3:
            device = at_place(self.mid[0], z, self.mid[1], c)
        elif which < 6:
            device = at_place(self.last[0], z, self.last[1], c)
        else:
            device = at_place(t, z, x, 1 - c)
        return self.copy(group, group, which, device)

    def arrived(self, which):
        t, z, x, c = self.place
        if which < 3:
            target = self.slot(lax.rem(z + 3 - which, 4))
        elif which < 6:
            target = self.group({3: self.mid, 4: self.last, 5: self.both}[which], c)
        else:
            spot = {6: (t, x), 7: self.last, 8: self.mid, 9: self.both}[which]
            target = self.group(spot, 1 - c)
        self.copy(target, target, which, at_place(t, z, x, 1 - c)).wait_recv()

    def start(self):
        _, z, _, _ = self.place
        pltpu.make_async_copy(self.own, self.slot(z), self.local.at[self.index]).start()
        for which in range(3):
            self.outgoing(which).start()

    def own_ready(self):
        _, z, _, _ = self.place
        pltpu.make_async_copy(self.own, self.slot(z), self.local.at[self.index]).wait()
        for which in range(3):
            self.arrived(which)
        for which in (3, 4, 6):
            self.outgoing(which).start()

    def mid_ready(self):
        self.arrived(3)
        for which in (5, 7):
            self.outgoing(which).start()

    def last_ready(self):
        self.arrived(4)
        self.outgoing(8).start()
        self.arrived(5)
        self.outgoing(9).start()

    def finish(self):
        for which in range(6, 10):
            self.arrived(which)

    def drain(self):
        for which in range(10):
            self.outgoing(which).wait_send()


def attend_gather_kernel(
    piece, spans, mixing_ref, middle_ref, shrink_ref, offsets_ref, x_ref,
    qkv_ref, ctx_ref, mixing_out, middle_out, shrink_out, offsets_out,
    w_ref, both_ref, sends, lands, local, swap_send, swap_land, load_sem,
):
    step = pl.program_id(0)
    t, z, x, c = grid_place()
    mixing, middle, shrink = (
        Gather(own, out, sends, lands, local, index)
        for index, (own, out) in enumerate(
            ((mixing_ref, mixing_out), (middle_ref, middle_out), (shrink_ref, shrink_out))
        )
    )

    def swap(which):
        return pltpu.make_async_remote_copy(
            src_ref=both_ref.at[which],
            dst_ref=both_ref.at[which],
            send_sem=swap_send,
            recv_sem=swap_land,
            device_id=at_place(1 - t, z, x, c),
            device_id_type=MESH,
        )

    @pl.when(step == 0)
    def _():
        both_ref[t] = offsets_ref[...]
        greet_neighbours()
        mixing.start()
        swap(t).start()
        middle.start()
        mixing.own_ready()
        mixing.mid_ready()
        shrink.start()
        middle.own_ready()
        mixing.last_ready()
        mixing.finish()
        load = pltpu.make_async_copy(mixing_out, w_ref, load_sem)
        load.start()
        swap(1 - t).wait_recv()
        offsets_out[...] = both_ref[...]
        load.wait()

    @pl.when(step == 2)
    def _():
        middle.mid_ready()
        shrink.own_ready()

    rows = x_ref.shape[0]
    width = w_ref.shape[5] // 3
    visible = visible_keys(spans, step, rows, piece, 1)
    for half in range(w_ref.shape[0]):
        weight = w_ref[half].reshape(D, 3 * width)
        bias = both_ref[half]
        bias = jnp.concatenate(
            [bias[:, :width], jnp.zeros((1, width), jnp.float32), bias[:, width : 2 * width]], axis=1
        )
        attend_half(half, weight, bias, visible, x_ref, qkv_ref, ctx_ref)

    @pl.when(step == pl.num_programs(0) - 1)
    def _():
        shrink.mid_ready()
        middle.last_ready()
        shrink.last_ready()
        middle.finish()
        shrink.finish()
        swap(t).wait_send()
        for each in (mixing, middle, shrink):
            each.drain()


def attend_gather(piece, spans, inputs, mixing_own, middle_own, shrink_own, offsets, chunk):
    rows = inputs.shape[0]
    halves = lax.axis_size("tensor")
    columns = halves * mixing_own.shape[1]
    anywhere = pl.BlockSpec(memory_space=pl.ANY)
    bf16 = jnp.bfloat16

    def buffer(own):
        return jax.ShapeDtypeStruct((halves, 4, 2, 2) + own.shape, bf16)

    owns = (mixing_own, middle_own, shrink_own)
    both = jax.ShapeDtypeStruct((halves, 1, offsets.shape[0]), jnp.float32)
    outs = pl.pallas_call(
        functools.partial(attend_gather_kernel, piece),
        grid=(rows // chunk,),
        in_specs=[
            pl.BlockSpec(memory_space=pltpu.SMEM),
            anywhere,
            anywhere,
            anywhere,
            full_spec((1, offsets.shape[0])),
            row_spec(chunk, D),
        ],
        out_specs=[
            row_spec(chunk, columns),
            row_spec(chunk, D),
            anywhere,
            anywhere,
            anywhere,
            full_spec(both.shape),
        ],
        out_shape=[
            jax.ShapeDtypeStruct((rows, columns), bf16),
            jax.ShapeDtypeStruct((rows, D), bf16),
            *(buffer(own) for own in owns),
            both,
        ],
        scratch_shapes=[
            pltpu.VMEM(buffer(mixing_own).shape, bf16),
            pltpu.VMEM(both.shape, jnp.float32),
            pltpu.SemaphoreType.DMA((3, 10)),
            pltpu.SemaphoreType.DMA((3, 10)),
            pltpu.SemaphoreType.DMA((3,)),
            pltpu.SemaphoreType.DMA,
            pltpu.SemaphoreType.DMA,
            pltpu.SemaphoreType.DMA,
        ],
        compiler_params=pltpu.CompilerParams(
            collective_id=3, has_side_effects=True, vmem_limit_bytes=big_vmem
        ),
        cost_estimate=pl.CostEstimate(
            flops=2 * rows * D * columns,
            bytes_accessed=64 * 1024 * 1024,
            transcendentals=rows * chunk * 12,
        ),
        name="attend_gather",
    )(spans, *owns, offsets.reshape(1, -1), inputs)
    qkv, context, *fulls, offsets_both = outs
    fulls = [full.reshape(halves, -1, full.shape[-1]) for full in fulls]
    return qkv, context, *fulls, offsets_both.reshape(halves, -1)


class Scatter:
    def __init__(self, whole, acc, sib, one, two, line, out, sends, lands, local, index):
        self.whole, self.acc, self.sib, self.out, self.index = whole, acc, sib, out, index
        self.one, self.two, self.line = one, two, line
        self.sends, self.lands, self.local = sends, lands, local
        t, z, x, c = self.place = grid_place()
        even = c == 0
        self.first = (jnp.where(even, 1 - t, t), jnp.where(even, x, 1 - x))
        self.second = (jnp.where(even, t, 1 - t), jnp.where(even, 1 - x, x))
        self.spots = (self.first, (1 - t, 1 - x), self.second, (t, x))

    def copy(self, source, target, which, device):
        return pltpu.make_async_remote_copy(
            src_ref=source,
            dst_ref=target,
            send_sem=self.sends.at[self.index, which],
            recv_sem=self.lands.at[self.index, which],
            device_id=device,
            device_id_type=MESH,
        )

    def outgoing(self, which):
        t, z, x, c = self.place
        if which < 4:
            spot = self.spots[{0: 2, 1: 1, 2: 0, 3: 3}[which]]
            return self.copy(
                self.whole.at[spot[0], :, spot[1], 1 - c],
                self.sib.at[spot[0], :, spot[1]],
                which,
                at_place(t, z, x, 1 - c),
            )
        if which < 6:
            spot = self.spots[which - 4]
            device = at_place(self.first[0], z, self.first[1], c)
            return self.copy(self.acc.at[spot[0], :, spot[1]], self.one.at[which - 4], which, device)
        if which == 6:
            spot = self.second
            device = at_place(spot[0], z, spot[1], c)
            return self.copy(self.acc.at[spot[0], :, spot[1]], self.two, which, device)
        there = lax.rem(z + which - 6, 4)
        return self.copy(
            self.acc.at[t, there, x], self.line.at[which - 7], which, at_place(t, there, x, c)
        )

    def arrived(self, which):
        t, z, x, c = self.place
        if which < 4:
            spot = self.spots[which]
            target = self.sib.at[spot[0], :, spot[1]]
        elif which < 6:
            target = self.one.at[which - 4]
        elif which == 6:
            target = self.two
        else:
            target = self.line.at[which - 7]
        self.copy(target, target, which, at_place(t, z, x, 1 - c)).wait_recv()

    def load(self, which):
        c = self.place[3]
        spot = self.spots[which]
        return pltpu.make_async_copy(
            self.whole.at[spot[0], :, spot[1], c],
            self.acc.at[spot[0], :, spot[1]],
            self.local.at[self.index, which],
        )

    def add(self, spot, read):
        @pl.loop(0, 4)
        def _(z):
            low = self.acc[spot[0], z, spot[1]].astype(jnp.float32)
            low = low + read(z).astype(jnp.float32)
            self.acc[spot[0], z, spot[1]] = low.astype(jnp.bfloat16)

    def start(self):
        for which in range(4):
            self.outgoing(which).start()
            self.load(which).start()

    def cores_ready(self):
        for which in range(4):
            spot = self.spots[which]
            self.arrived(which)
            self.load(which).wait()
            self.add(spot, lambda z: self.sib[spot[0], z, spot[1]])
            if which < 2:
                self.outgoing(4 + which).start()

    def first_ready(self):
        self.arrived(5)
        self.add(self.second, lambda z: self.one[1, z])
        self.outgoing(6).start()
        self.arrived(4)
        self.add(self.spots[3], lambda z: self.one[0, z])

    def second_ready(self):
        self.arrived(6)
        self.add(self.spots[3], lambda z: self.two[z])
        for which in range(7, 10):
            self.outgoing(which).start()

    def finish(self):
        t, z, x, c = self.place
        total = self.acc[t, z, x].astype(jnp.float32)
        for which in range(7, 10):
            self.arrived(which)
            total = total + self.line[which - 7].astype(jnp.float32)
        self.out[...] = total
        return jnp.sum(total * total, axis=0, keepdims=True)

    def drain(self):
        for which in range(10):
            self.outgoing(which).wait_send()


class Total:
    def __init__(self, slots, line, sends, lands):
        self.slots, self.line, self.sends, self.lands = slots, line, sends, lands
        t, z, x, c = self.place = grid_place()
        self.partners = (at_place(t, z, x, 1 - c), at_place(t, z, 1 - x, c), at_place(1 - t, z, x, c))

    def pair(self, stage):
        return pltpu.make_async_remote_copy(
            src_ref=self.slots.at[2 * stage],
            dst_ref=self.slots.at[2 * stage + 1],
            send_sem=self.sends.at[stage],
            recv_sem=self.lands.at[stage],
            device_id=self.partners[stage],
            device_id_type=MESH,
        )

    def along(self, gap):
        t, z, x, c = self.place
        return pltpu.make_async_remote_copy(
            src_ref=self.line.at[z],
            dst_ref=self.line.at[z],
            send_sem=self.sends.at[2 + gap],
            recv_sem=self.lands.at[2 + gap],
            device_id=at_place(t, lax.rem(z + gap, 4), x, c),
            device_id_type=MESH,
        )

    def landed(self, gap):
        t, z, x, c = self.place
        spot = self.line.at[lax.rem(z + 4 - gap, 4)]
        pltpu.make_async_remote_copy(
            src_ref=spot,
            dst_ref=spot,
            send_sem=self.sends.at[2 + gap],
            recv_sem=self.lands.at[2 + gap],
            device_id=self.partners[0],
            device_id_type=MESH,
        ).wait_recv()

    def start(self, value):
        self.slots[0] = value
        self.pair(0).start()

    def advance(self, stage):
        self.pair(stage).wait_recv()
        summed = self.slots[2 * stage] + self.slots[2 * stage + 1]
        if stage < 2:
            self.slots[2 * stage + 2] = summed
            self.pair(stage + 1).start()
            return
        z = self.place[1]
        self.line[z] = summed
        for gap in range(1, 4):
            self.along(gap).start()

    def finish(self):
        for gap in range(1, 4):
            self.landed(gap)
        return (self.line[0] + self.line[1]) + (self.line[2] + self.line[3])

    def drain(self):
        for stage in range(3):
            self.pair(stage).wait_send()
        for gap in range(1, 4):
            self.along(gap).wait_send()


def scatter_kernel(count, *refs):
    wholes, vector_ref = refs[:count], refs[count]
    outs, total_ref, norm_ref = refs[count + 1 : 2 * count + 1], refs[2 * count + 1], refs[2 * count + 2]
    rest = refs[2 * count + 3 :]
    buffers = [rest[5 * index : 5 * index + 5] for index in range(count)]
    sends, lands, local, vs, vl, vsend, vland, ns, nl, nsend, nland = rest[5 * count :]
    parts = [
        Scatter(wholes[i], *buffers[i], outs[i], sends, lands, local, i) for i in range(count)
    ]
    vector = Total(vs, vl, vsend, vland)
    norm = Total(ns, nl, nsend, nland)
    greet_neighbours()
    parts[0].start()
    vector.start(vector_ref[...])
    parts[1].start()
    parts[0].cores_ready()
    vector.advance(0)
    for part in parts[2:]:
        part.start()
    parts[1].cores_ready()
    parts[0].first_ready()
    vector.advance(1)
    parts[2].cores_ready()
    parts[1].first_ready()
    parts[0].second_ready()
    vector.advance(2)
    parts[3].cores_ready()
    parts[2].first_ready()
    parts[1].second_ready()
    squares = []
    squares.append(jnp.sum(parts[0].finish()))
    parts[3].first_ready()
    parts[2].second_ready()
    squares.append(jnp.sum(parts[1].finish()))
    total_ref[...] = vector.finish()
    parts[3].second_ready()
    squares.append(jnp.sum(parts[2].finish()))
    squares.append(jnp.sum(parts[3].finish()))
    norm.start(jnp.full(norm_ref.shape, sum(squares[1:], squares[0])))
    for stage in range(3):
        norm.advance(stage)
    norm_ref[...] = norm.finish()
    for each in parts + [vector, norm]:
        each.drain()


def scatter_all(wholes, vector):
    count = len(wholes)
    anywhere = pl.BlockSpec(memory_space=pl.ANY)
    vmem = pl.BlockSpec(memory_space=pltpu.VMEM)
    halves = lax.axis_size("tensor")
    bf16, f32 = jnp.bfloat16, jnp.float32
    rows = wholes[0].shape[1] // lax.axis_size("dp")
    scratch = []
    for whole in wholes:
        columns = whole.shape[2]
        scratch += [
            pltpu.VMEM((halves, 4, 2, rows, columns), bf16),
            pltpu.VMEM((halves, 4, 2, rows, columns), bf16),
            pltpu.VMEM((2, 4, rows, columns), bf16),
            pltpu.VMEM((4, rows, columns), bf16),
            pltpu.VMEM((3, rows, columns), bf16),
        ]
    small = (8, 128)
    scratch += [
        pltpu.SemaphoreType.DMA((count, 10)),
        pltpu.SemaphoreType.DMA((count, 10)),
        pltpu.SemaphoreType.DMA((count, 4)),
    ]
    for shape in (vector.shape, small):
        scratch += [
            pltpu.VMEM((6,) + shape, f32),
            pltpu.VMEM((4,) + shape, f32),
            pltpu.SemaphoreType.DMA((6,)),
            pltpu.SemaphoreType.DMA((6,)),
        ]
    outs = pl.pallas_call(
        functools.partial(scatter_kernel, count),
        in_specs=[anywhere] * count + [vmem],
        out_specs=[vmem] * (count + 2),
        out_shape=[jax.ShapeDtypeStruct((rows, whole.shape[2]), f32) for whole in wholes]
        + [jax.ShapeDtypeStruct(vector.shape, f32), jax.ShapeDtypeStruct(small, f32)],
        scratch_shapes=scratch,
        compiler_params=pltpu.CompilerParams(
            collective_id=4, has_side_effects=True, vmem_limit_bytes=big_vmem
        ),
        name="scatter_all",
    )(*(whole.reshape(halves, 4, 2, 2, rows, -1) for whole in wholes), vector)
    return outs[:count], outs[count], outs[count + 1][0, 0]


def row_spec(rows, columns):
    return pl.BlockSpec((rows, columns), lambda i: (i, 0))


def full_spec(shape):
    return pl.BlockSpec(shape, lambda i: (0,) * len(shape), pipeline_mode=pl.Buffered(1))


def shards(
    short_tokens,
    long_tokens,
    short_cotangent,
    long_cotangent,
    short_lengths,
    long_lengths,
    queries,
    positives,
    step_count,
    mixing_weight,
    mixing_moment,
    mixing_square,
    mixing_average,
    merging_weight,
    merging_moment,
    merging_square,
    merging_average,
    expand_weight,
    expand_moment,
    expand_square,
    expand_average,
    shrink_weight,
    shrink_moment,
    shrink_square,
    shrink_average,
    scales_weight,
    scales_moment,
    scales_square,
    scales_average,
    offsets_weight,
    offsets_moment,
    offsets_square,
    offsets_average,
):
    halves = lax.axis_size("tensor")
    place = lax.axis_index("tensor")
    short_span = short_tokens.shape[1]
    long_span = long_tokens.shape[1]
    shorts = short_tokens.shape[0] // halves
    longs = long_tokens.shape[0] // halves
    chunk = long_span
    piece = short_span
    assert shorts * short_span == chunk and shorts == longs
    chunks = longs + 1
    rows = chunks * chunk
    width = mixing_weight.shape[2]
    wide = expand_weight.shape[1]

    def own_half(short_all, long_all):
        return jnp.concatenate(
            [
                lax.dynamic_slice_in_dim(short_all, place * shorts, shorts).reshape(-1, D),
                lax.dynamic_slice_in_dim(long_all, place * longs, longs).reshape(-1, D),
            ],
            axis=0,
        )

    def both_halves(own, other):
        own_first = place == 0
        low = jnp.where(own_first, own, other)
        high = jnp.where(own_first, other, own)
        head = shorts * short_span
        return (
            jnp.concatenate([low[:head], high[:head]]).reshape(short_tokens.shape),
            jnp.concatenate([low[head:], high[head:]]).reshape(long_tokens.shape),
        )

    fast = lax.axis_size("dp") == 16 and halves == 2
    mixing_own = mixing_weight.astype(jnp.bfloat16).reshape(-1, 3 * width)
    middle_own = jnp.concatenate([merging_weight.T, expand_weight], axis=1).astype(jnp.bfloat16)
    shrink_own = shrink_weight.T.astype(jnp.bfloat16)
    short_limits = lax.dynamic_slice_in_dim(short_lengths, place * shorts, shorts)
    long_limits = lax.dynamic_slice_in_dim(long_lengths, place * longs, longs)
    spans = jnp.concatenate(
        [
            short_limits[None, :],
            long_limits[:, None] - piece * jnp.arange(chunk // piece, dtype=jnp.int32)[None, :],
        ],
        axis=0,
    )
    inputs = own_half(short_tokens, long_tokens)
    cotangent = own_half(short_cotangent, long_cotangent)
    bf16, f32 = jnp.bfloat16, jnp.float32

    def shaped(columns, dtype):
        return jax.ShapeDtypeStruct((rows, columns), dtype)

    smem = pl.BlockSpec(memory_space=pltpu.SMEM)
    params = pltpu.CompilerParams(vmem_limit_bytes=big_vmem)
    mixing_columns = halves * 3 * width
    scores_flops = 2 * rows * chunk * PAIR * (halves * width // HEAD_DIM)
    if fast:
        qkv, context, mixing_full, middle_full, shrink_full, offsets_both = attend_gather(
            piece, spans, inputs, mixing_own, middle_own, shrink_own, offsets_weight, chunk
        )
    else:
        mixing_full, middle_full, shrink_full = (
            gathered(own) for own in (mixing_own, middle_own, shrink_own)
        )
        offsets_other = tensor_swap(offsets_weight)
        offsets_both = jnp.where(
            place == 0,
            jnp.stack([offsets_weight, offsets_other]),
            jnp.stack([offsets_other, offsets_weight]),
        )
        mixing_bias = jnp.concatenate(
            [
                offsets_both[:, :width],
                jnp.zeros((halves, width), jnp.float32),
                offsets_both[:, width : 2 * width],
            ],
            axis=1,
        ).reshape(1, -1)
        qkv, context = pl.pallas_call(
            functools.partial(attend_forward_kernel, piece),
            grid=(chunks,),
            in_specs=[
                smem,
                row_spec(chunk, D),
                full_spec(mixing_full.shape),
                full_spec(mixing_bias.shape),
            ],
            out_specs=[row_spec(chunk, mixing_columns), row_spec(chunk, D)],
            out_shape=[shaped(mixing_columns, bf16), shaped(D, bf16)],
            compiler_params=params,
            cost_estimate=pl.CostEstimate(
                flops=2 * rows * D * mixing_columns + 6 * scores_flops,
                bytes_accessed=16 * 1024 * 1024,
                transcendentals=rows * chunk * 12,
            ),
            name="attend_forward",
        )(spans, inputs, mixing_full, mixing_bias)
    upward_bias = offsets_both[:, 2 * width :].reshape(1, -1)
    output, hidden_low, activated, slope, normed_first, rstd_first, normed_second, rstd_second = (
        pl.pallas_call(
            feed_forward_kernel,
            grid=(chunks,),
            in_specs=[
                row_spec(chunk, D),
                row_spec(chunk, D),
                full_spec(middle_full.shape),
                full_spec(shrink_full.shape),
                full_spec(scales_weight.shape),
                full_spec(upward_bias.shape),
            ],
            out_specs=[
                row_spec(chunk, D),
                row_spec(chunk, D),
                row_spec(chunk, FF),
                row_spec(chunk, FF),
                row_spec(chunk, D),
                row_spec(chunk, 1),
                row_spec(chunk, D),
                row_spec(chunk, 1),
            ],
            out_shape=[
                shaped(D, bf16),
                shaped(D, bf16),
                shaped(FF, bf16),
                shaped(FF, bf16),
                shaped(D, f32),
                shaped(1, f32),
                shaped(D, f32),
                shaped(1, f32),
            ],
            compiler_params=params,
            cost_estimate=pl.CostEstimate(
                flops=2 * rows * D * (D + 2 * FF),
                bytes_accessed=48 * 1024 * 1024,
                transcendentals=2 * rows * FF,
            ),
            name="feed_forward",
        )(
            context,
            inputs,
            middle_full,
            shrink_full,
            scales_weight,
            upward_bias,
        )
    )
    leading = jnp.concatenate([output[: shorts * piece : piece], output[chunk::chunk]], axis=0)
    query_gradient, lead_back, loss_part = contrast(leading, queries, positives)
    output_other = tensor_swap(lax.optimization_barrier((output, lead_back))[0])
    lead_rows = jnp.zeros((chunks, 8, D), f32)
    lead_rows = lead_rows.at[0, :shorts].set(lead_back[:shorts])
    lead_rows = lead_rows.at[1:, 0].set(lead_back[shorts:])
    down_low, upward_low, first_low, first_back, context_back, vector_grad, upward_grad = (
        pl.pallas_call(
            functools.partial(feed_back_kernel, piece),
            grid=(chunks,),
            in_specs=[
                row_spec(chunk, D),
                pl.BlockSpec((1, 8, D), lambda i: (i, 0, 0)),
                row_spec(chunk, D),
                row_spec(chunk, 1),
                row_spec(chunk, D),
                row_spec(chunk, 1),
                row_spec(chunk, FF),
                full_spec(middle_full.shape),
                full_spec(shrink_full.shape),
                full_spec(scales_weight.shape),
            ],
            out_specs=[
                row_spec(chunk, D),
                row_spec(chunk, FF),
                row_spec(chunk, D),
                row_spec(chunk, D),
                row_spec(chunk, D),
                pl.BlockSpec((8, D), lambda i: (0, 0)),
                pl.BlockSpec((8, FF), lambda i: (0, 0)),
            ],
            out_shape=[
                shaped(D, bf16),
                shaped(FF, bf16),
                shaped(D, bf16),
                shaped(D, f32),
                shaped(D, bf16),
                jax.ShapeDtypeStruct((8, D), f32),
                jax.ShapeDtypeStruct((8, FF), f32),
            ],
            compiler_params=params,
            cost_estimate=pl.CostEstimate(
                flops=2 * rows * D * (D + 2 * FF),
                bytes_accessed=48 * 1024 * 1024,
                transcendentals=0,
            ),
            name="feed_back",
        )(
            cotangent,
            lead_rows,
            normed_first,
            rstd_first,
            normed_second,
            rstd_second,
            slope,
            middle_full,
            shrink_full,
            scales_weight,
        )
    )
    projected_back, input_back, input_low, bias_grad = pl.pallas_call(
        functools.partial(attend_back_kernel, piece),
        grid=(chunks,),
        in_specs=[
            smem,
            row_spec(chunk, mixing_columns),
            row_spec(chunk, D),
            row_spec(chunk, D),
            full_spec(mixing_full.shape),
        ],
        out_specs=[
            row_spec(chunk, mixing_columns),
            row_spec(chunk, D),
            row_spec(chunk, D),
            pl.BlockSpec((8, mixing_columns), lambda i: (0, 0)),
        ],
        out_shape=[
            shaped(mixing_columns, bf16),
            shaped(D, f32),
            shaped(D, bf16),
            jax.ShapeDtypeStruct((8, mixing_columns), f32),
        ],
        compiler_params=params,
        cost_estimate=pl.CostEstimate(
            flops=2 * rows * D * mixing_columns + 15 * scores_flops,
            bytes_accessed=24 * 1024 * 1024,
            transcendentals=rows * chunk * 12,
        ),
        name="attend_back",
    )(spans, qkv, context_back, first_back, mixing_full)
    input_other = tensor_swap(input_low)
    down_low, hidden_low, first_low, inputs, output_other, input_back = lax.optimization_barrier(
        (down_low, hidden_low, first_low, inputs, output_other, input_back)
    )
    shrink_grad = weight_grad(down_low, activated, halves, 512)
    expand_grad = weight_grad(hidden_low, upward_low, halves, 512)
    merging_grad = weight_grad(first_low, context, halves, 384)
    mixing_grad = weight_grad(inputs, projected_back, halves, 384)

    mixing_grad, input_other = lax.optimization_barrier((mixing_grad, input_other))
    short_output, long_output = both_halves(output, output_other)
    short_gradient, long_gradient = both_halves(input_back, input_other.astype(f32))

    bias_both = bias_grad[0].reshape(halves, 3, width)
    offsets_grad = jnp.concatenate(
        [bias_both[:, 0], bias_both[:, 2], upward_grad[0].reshape(halves, wide)], axis=1
    )
    lane = lax.broadcasted_iota(jnp.int32, (1, D), 1)
    grads = (shrink_grad, expand_grad, merging_grad, mixing_grad)

    def stacked(scalars):
        scalars = jnp.pad(scalars, ((0, 3), (0, 0)))
        return jnp.concatenate([vector_grad[:6], offsets_grad.reshape(-1, D), scalars], axis=0)

    losses = jnp.where(lane == 1, loss_part, 0.0)
    if fast:
        sums, summed, squares_all = scatter_all(grads, stacked(losses))
    else:
        sums = [scattered(grad) for grad in grads]
        squares_part = sum(jnp.sum(each * each) for each in sums)
        summed = all_total(stacked(jnp.where(lane == 0, squares_part, losses)))
        squares_all = summed[12, 0]
    shrink_sum, expand_sum, merging_sum, mixing_sum = sums
    reduced = (mixing_sum.reshape(mixing_weight.shape), merging_sum.T, expand_sum, shrink_sum.T)
    scales_sum = summed[:6]
    offsets_all = summed[6:12].reshape(halves, -1)
    offsets_sum = jnp.where(place == 0, offsets_all[0], offsets_all[1])
    squares_all = squares_all + jnp.sum(summed[:12] * summed[:12])
    loss_all = summed[12, 1] / halves
    norm_value = jnp.sqrt(squares_all)
    factor = clip_limit / jnp.maximum(norm_value, clip_limit)
    steps_float = step_count[0].astype(jnp.float32)
    first_fix = 1.0 - jnp.power(first_decay, steps_float)
    second_fix = 1.0 - jnp.power(second_decay, steps_float)

    def update(weight, moment, square, average, gradient, rate):
        clipped = gradient * factor
        first = first_decay * moment + (1.0 - first_decay) * clipped
        second = second_decay * square + (1.0 - second_decay) * clipped * clipped
        master = weight - rate * (
            first / first_fix / (jnp.sqrt(second / second_fix) + adam_eps) + decay_weight * weight
        )
        smooth = smooth_decay * average + (1.0 - smooth_decay) * master
        return (master, first, second, smooth)

    mixing_new = update(
        mixing_weight, mixing_moment, mixing_square, mixing_average, reduced[0], 1.0 / math.sqrt(D)
    )
    merging_new = update(
        merging_weight,
        merging_moment,
        merging_square,
        merging_average,
        reduced[1],
        8.0 / math.sqrt(D),
    )
    expand_new = update(
        expand_weight, expand_moment, expand_square, expand_average, reduced[2], 1.0 / math.sqrt(D)
    )
    shrink_new = update(
        shrink_weight, shrink_moment, shrink_square, shrink_average, reduced[3], 1.0 / math.sqrt(FF)
    )
    scales_new = update(
        scales_weight, scales_moment, scales_square, scales_average, scales_sum, 0.3
    )
    offsets_new = update(
        offsets_weight, offsets_moment, offsets_square, offsets_average, offsets_sum, 0.3
    )
    contrast_loss = (loss_all / (queries.shape[0] * lax.axis_size("dp"))).reshape(1)
    gradient_norm = norm_value.reshape(1)
    return (
        (
            short_output,
            long_output,
            short_gradient,
            long_gradient,
            query_gradient,
            contrast_loss,
            gradient_norm,
        )
        + mixing_new
        + merging_new
        + expand_new
        + shrink_new
        + scales_new
        + offsets_new
    )


def solution(mesh):
    placed = (
        P("dp", None, None),
        P("dp", None, None),
        P("dp", None, None),
        P("dp", None, None),
        P("dp"),
        P("dp"),
        P("dp", None),
        P("dp"),
        P(),
        P("dp", None, "tensor"),
        P("dp", None, "tensor"),
        P("dp", None, "tensor"),
        P("dp", None, "tensor"),
        P("tensor", "dp"),
        P("tensor", "dp"),
        P("tensor", "dp"),
        P("tensor", "dp"),
        P("dp", "tensor"),
        P("dp", "tensor"),
        P("dp", "tensor"),
        P("dp", "tensor"),
        P("tensor", "dp"),
        P("tensor", "dp"),
        P("tensor", "dp"),
        P("tensor", "dp"),
        P(),
        P(),
        P(),
        P(),
        P("tensor"),
        P("tensor"),
        P("tensor"),
        P("tensor"),
    )
    return jax.shard_map(
        shards,
        mesh=mesh,
        in_specs=placed,
        out_specs=(
            P("dp", None, None),
            P("dp", None, None),
            P("dp", None, None),
            P("dp", None, None),
            P("dp", None),
            P(),
            P(),
            P("dp", None, "tensor"),
            P("dp", None, "tensor"),
            P("dp", None, "tensor"),
            P("dp", None, "tensor"),
            P("tensor", "dp"),
            P("tensor", "dp"),
            P("tensor", "dp"),
            P("tensor", "dp"),
            P("dp", "tensor"),
            P("dp", "tensor"),
            P("dp", "tensor"),
            P("dp", "tensor"),
            P("tensor", "dp"),
            P("tensor", "dp"),
            P("tensor", "dp"),
            P("tensor", "dp"),
            P(),
            P(),
            P(),
            P(),
            P("tensor"),
            P("tensor"),
            P("tensor"),
            P("tensor"),
        ),
        check_vma=False,
    )
```

```python
import functools
import math

import jax
import jax.numpy as jnp
from jax import lax
from jax.experimental import pallas as pl
from jax.experimental.pallas import tpu as pltpu
from jax.sharding import PartitionSpec as P

D = 768
FF = 3072
HEAD_DIM = 64
PAIR = 2 * HEAD_DIM
MESH = pl.DeviceIdType.MESH

norm_eps = 1e-05
score_scale = 0.125
masked_value = -1e30
first_decay = 0.5
second_decay = 0.75
smooth_decay = 0.75
decay_weight = 0.01
adam_eps = 1e-08
clip_limit = 1.0
inverse_root_two = 0.7071067811865476
inverse_root_tau = 0.3989422804014327
big_vmem = 56 * 1024 * 1024


def dot_nn(a, b):
    return lax.dot_general(a, b, (((1,), (0,)), ((), ())), preferred_element_type=jnp.float32)


def dot_nt(a, b):
    return lax.dot_general(a, b, (((1,), (1,)), ((), ())), preferred_element_type=jnp.float32)


def dot_tn(a, b):
    return lax.dot_general(a, b, (((0,), (0,)), ((), ())), preferred_element_type=jnp.float32)


def layer_stats(resid):
    centre = resid - jnp.mean(resid, axis=-1, keepdims=True)
    rstd = lax.rsqrt(jnp.mean(centre * centre, axis=-1, keepdims=True) + norm_eps)
    return (centre * rstd, rstd)


def layer_back(gradient, normed, rstd, gain):
    scaled = gradient * gain
    return rstd * (
        scaled
        - jnp.mean(scaled, axis=-1, keepdims=True)
        - normed * jnp.mean(scaled * normed, axis=-1, keepdims=True)
    )


def visible_keys(spans, step, rows, piece, key_axis):
    shape = (rows, 1) if key_axis == 0 else (1, rows)
    place = lax.broadcasted_iota(jnp.int32, shape, key_axis)
    segment = place // piece
    limit = jnp.zeros(shape, jnp.int32)
    for index in range(rows // piece):
        limit = jnp.where(segment == index, spans[step, index], limit)
    key_valid = (place % piece) < limit
    first = lax.broadcasted_iota(jnp.int32, (rows, rows), 0) // piece
    second = lax.broadcasted_iota(jnp.int32, (rows, rows), 1) // piece
    return jnp.logical_and(jnp.logical_or(first == second, step > 0), key_valid)


def own_lanes(value, which):
    lane = lax.broadcasted_iota(jnp.int32, value.shape, 1)
    return jnp.where((lane // HEAD_DIM) == which, value, jnp.zeros_like(value))


def join_lanes(low, high):
    lane = lax.broadcasted_iota(jnp.int32, low.shape, 1)
    return jnp.where(lane < HEAD_DIM, low, high)


def attend_half(half, weight, bias, visible, x_ref, qkv_ref, ctx_ref):
    width = weight.shape[1] // 3
    base = half * 3 * width
    projected = dot_nn(x_ref[...], weight) + bias
    qkv_ref[:, base : base + 3 * width] = projected.astype(jnp.bfloat16)
    for pair in range(width // PAIR):
        at = base + pair * PAIR
        q = qkv_ref[:, at : at + PAIR] * jnp.bfloat16(score_scale)
        k = qkv_ref[:, at + width : at + width + PAIR]
        v = qkv_ref[:, at + 2 * width : at + 2 * width + PAIR]
        parts = []
        for which in range(2):
            scores = jnp.where(visible, dot_nt(own_lanes(q, which), k), masked_value)
            powered = jnp.exp(scores - jnp.max(scores, axis=-1, keepdims=True))
            weights = powered * (1.0 / jnp.sum(powered, axis=-1, keepdims=True))
            parts.append(dot_nn(weights.astype(jnp.bfloat16), v))
        at = half * width + pair * PAIR
        ctx_ref[:, at : at + PAIR] = join_lanes(*parts).astype(jnp.bfloat16)


def attend_forward_kernel(piece, spans, x_ref, w_ref, bias_ref, qkv_ref, ctx_ref):
    step = pl.program_id(0)
    rows = x_ref.shape[0]
    width = w_ref.shape[2] // 3
    visible = visible_keys(spans, step, rows, piece, 1)
    for half in range(w_ref.shape[0]):
        bias = bias_ref[:, half * 3 * width : (half + 1) * 3 * width]
        attend_half(half, w_ref[half], bias, visible, x_ref, qkv_ref, ctx_ref)


def feed_up(context, inputs, me_ref, scales_ref, bu_ref, outs):
    hb_ref, g_ref, slope_ref, n1_ref, r1_ref = outs
    wide = bu_ref.shape[1] // 2
    width = me_ref.shape[-1] - wide
    attention = scales_ref[4:5, :]

    def weight(half, columns):
        place = (half,) + (slice(None),) * (len(me_ref.shape) - 2) + (columns,)
        return me_ref[place].reshape(D, -1)

    for half in range(2):
        attention = attention + dot_nt(
            context[:, half * width : (half + 1) * width], weight(half, slice(0, width))
        )
    normed, rstd = layer_stats(inputs.astype(jnp.float32) + attention)
    n1_ref[...] = normed
    r1_ref[...] = rstd
    hidden = normed * scales_ref[0:1, :] + scales_ref[1:2, :]
    hidden_low = hidden.astype(jnp.bfloat16)
    hb_ref[...] = hidden_low
    activated = []
    for half in range(2):
        at = half * wide
        upward = dot_nn(hidden_low, weight(half, slice(width, width + wide))) + bu_ref[:, at : at + wide]
        cumulative = 0.5 * (1.0 + lax.erf(upward * inverse_root_two))
        density = jnp.exp(-0.5 * upward * upward) * inverse_root_tau
        activated.append((upward * cumulative).astype(jnp.bfloat16))
        g_ref[:, at : at + wide] = activated[half]
        slope_ref[:, at : at + wide] = (cumulative + upward * density).astype(jnp.bfloat16)
    return hidden, activated


def feed_down(piece, hidden, activated, st_ref, scales_ref, outs):
    out_ref, n2_ref, r2_ref, lead_ref = outs
    downward = scales_ref[5:6, :]
    for half in range(2):
        wide = st_ref.shape[-1]
        downward = downward + dot_nt(activated[half], st_ref[half].reshape(D, wide))
    normed, rstd = layer_stats(hidden + downward)
    n2_ref[...] = normed
    r2_ref[...] = rstd
    result = (normed * scales_ref[2:3, :] + scales_ref[3:4, :]).astype(jnp.bfloat16)
    out_ref[...] = result
    for index in range(result.shape[0] // piece):
        row = result[index * piece : index * piece + 8].astype(jnp.float32)
        lead_ref[0, index : index + 1, :] = row[:1]


def feed_forward_kernel(
    piece, ctx_ref, x_ref, me_ref, st_ref, scales_ref, bu_ref,
    hb_ref, g_ref, slope_ref, n1_ref, r1_ref, out_ref, n2_ref, r2_ref, lead_ref,
):
    hidden, activated = feed_up(
        ctx_ref[...], x_ref[...], me_ref, scales_ref, bu_ref, (hb_ref, g_ref, slope_ref, n1_ref, r1_ref)
    )
    feed_down(piece, hidden, activated, st_ref, scales_ref, (out_ref, n2_ref, r2_ref, lead_ref))


def add_row(ref, index, value):
    ref[index : index + 1, :] += jnp.sum(value, axis=0, keepdims=True)


def out_back_kernel(
    piece, chunks, cot_ref, lead_ref, n2_ref, r2_ref, scales_ref, g_ref, dr2_ref, vec_ref, grad_ref, turned_ref
):
    step = pl.program_id(0)

    @pl.when(step == 0)
    def _():
        vec_ref[...] = jnp.zeros_like(vec_ref)

    @pl.when(step < chunks)
    def _():
        dout = cot_ref[...].astype(jnp.float32)
        rows = dout.shape[0]
        row = lax.broadcasted_iota(jnp.int32, dout.shape, 0)
        for index in range(rows // piece):
            dout = dout + jnp.where(row == index * piece, lead_ref[0, index : index + 1, :], 0.0)
        normed = n2_ref[...]
        add_row(vec_ref, 0, dout * normed)
        add_row(vec_ref, 1, dout)
        second = layer_back(dout, normed, r2_ref[...], scales_ref[2:3, :])
        add_row(vec_ref, 2, second)
        dr2_ref[...] = second
        turned_ref[:, pl.ds(pl.multiple_of(step * rows, rows), rows)] = second.astype(jnp.bfloat16).T

    @pl.when(step >= chunks)
    def _():
        grad_ref[0] = dot_nn(turned_ref[...], g_ref[...]).astype(jnp.bfloat16)


def no_progress(point):
    pass


def feed_back_kernel(
    chunks, dr2_ref, n1_ref, r1_ref, slope_ref, hb_ref, ctx_ref, me_ref, st_ref, scales_ref,
    dr1_ref, dctx_ref, vec_ref, up_ref, merging_ref, expand_ref,
    dub_ref, turned_h, turned_a, progress=no_progress,
):
    step = pl.program_id(0)
    rows = dr2_ref.shape[0]
    wide = st_ref.shape[2]
    width = me_ref.shape[2] - wide
    tiles = ctx_ref.shape[1]
    tile = expand_ref.shape[2]
    merging_steps = D // tiles

    @pl.when(step == 0)
    def _():
        vec_ref[...] = jnp.zeros_like(vec_ref)
        up_ref[...] = jnp.zeros_like(up_ref)

    progress(0)

    @pl.when(step < chunks)
    def _():
        place = pl.ds(pl.multiple_of(step * rows, rows), rows)
        hidden_back = dr2_ref[...]
        low = hidden_back.astype(jnp.bfloat16)
        turned_h[:, place] = hb_ref[...].T
        for half in range(st_ref.shape[0]):
            at = half * wide
            upward = dot_nn(low, st_ref[half]) * slope_ref[:, at : at + wide].astype(jnp.float32)
            up_ref[0:1, at : at + wide] += jnp.sum(upward, axis=0, keepdims=True)
            upward_low = upward.astype(jnp.bfloat16)
            dub_ref[place, at : at + wide] = upward_low
            hidden_back = hidden_back + dot_nt(upward_low, me_ref[half, :, width:])
            progress(1 + half)
        normed = n1_ref[...]
        add_row(vec_ref, 0, hidden_back * normed)
        add_row(vec_ref, 1, hidden_back)
        first = layer_back(hidden_back, normed, r1_ref[...], scales_ref[0:1, :])
        add_row(vec_ref, 2, first)
        dr1_ref[...] = first
        low = first.astype(jnp.bfloat16)
        turned_a[:, place] = low.T
        for half in range(me_ref.shape[0]):
            dctx_ref[:, half * width : (half + 1) * width] = dot_nn(
                low, me_ref[half, :, :width]
            ).astype(jnp.bfloat16)

    @pl.when(jnp.logical_and(step >= chunks, step < chunks + merging_steps))
    def _():
        merging_ref[0] = dot_nn(turned_a[...], ctx_ref[...]).astype(jnp.bfloat16)

    @pl.when(step >= chunks + merging_steps)
    def _():
        start = (step - chunks - merging_steps) * tile
        right = dub_ref[:, pl.ds(pl.multiple_of(start, tile), tile)]
        expand_ref[0] = dot_nn(turned_h[...], right).astype(jnp.bfloat16)


def attend_back_kernel(
    piece, spans, qkv_ref, dctx_ref, dr1_ref, w_ref, dproj_ref, dx_ref, bias_ref, low_ref,
    progress=no_progress,
):
    step = pl.program_id(0)

    @pl.when(step == 0)
    def _():
        bias_ref[...] = jnp.zeros_like(bias_ref)

    rows = qkv_ref.shape[0]
    width = w_ref.shape[2] // 3
    visible = visible_keys(spans, step, rows, piece, 0)
    point = 0
    total = dr1_ref[...]
    for half in range(w_ref.shape[0]):
        base = half * 3 * width
        for pair in range(width // PAIR):
            at = base + pair * PAIR
            q = qkv_ref[:, at : at + PAIR]
            k = qkv_ref[:, at + width : at + width + PAIR]
            v = qkv_ref[:, at + 2 * width : at + 2 * width + PAIR]
            near = half * width + pair * PAIR
            back = dctx_ref[:, near : near + PAIR]
            parts = []
            for which in range(2):
                scores = dot_nt(own_lanes(k, which) * jnp.bfloat16(score_scale), q)
                scores = jnp.where(visible, scores, masked_value)
                powered = jnp.exp(scores - jnp.max(scores, axis=0, keepdims=True))
                weights = powered * (1.0 / jnp.sum(powered, axis=0, keepdims=True))
                weight_back = dot_nt(own_lanes(v, which), back)
                score_back = weights * (
                    weight_back - jnp.sum(weights * weight_back, axis=0, keepdims=True)
                )
                score_low = (score_back * score_scale).astype(jnp.bfloat16)
                parts.append(
                    (
                        dot_tn(score_low, k),
                        dot_nn(score_low, q),
                        dot_nn(weights.astype(jnp.bfloat16), back),
                    )
                )
            for part in range(3):
                value = join_lanes(parts[0][part], parts[1][part])
                spot = at + part * width
                if part != 1:
                    bias_ref[0:1, spot : spot + PAIR] += jnp.sum(value, axis=0, keepdims=True)
                dproj_ref[:, spot : spot + PAIR] = value.astype(jnp.bfloat16)
            point += 1
            progress(point)
        total = total + dot_nt(dproj_ref[:, base : base + 3 * width], w_ref[half])
    dx_ref[...] = total
    low_ref[step if low_ref.shape[0] > 1 else 0] = total.astype(jnp.bfloat16)


def weight_grad_kernel(left_ref, right_ref, out_ref, turned_ref):
    @pl.when(pl.program_id(0) == 0)
    def _():
        turned_ref[...] = left_ref[...].T

    out_ref[0] = dot_nn(turned_ref[...], right_ref[...]).astype(jnp.bfloat16)


def weight_grad(left, right, groups, tile):
    rows, depth = left.shape
    columns = right.shape[1]
    per = columns // groups // tile
    return pl.pallas_call(
        weight_grad_kernel,
        grid=(columns // tile,),
        in_specs=[
            pl.BlockSpec((rows, depth), lambda i: (0, 0), pipeline_mode=pl.Buffered(1)),
            pl.BlockSpec((rows, tile), lambda i: (0, i)),
        ],
        out_specs=pl.BlockSpec((1, depth, tile), lambda i: (i // per, 0, i % per)),
        out_shape=jax.ShapeDtypeStruct((groups, depth, columns // groups), jnp.bfloat16),
        scratch_shapes=[pltpu.VMEM((depth, rows), jnp.bfloat16)],
        compiler_params=pltpu.CompilerParams(vmem_limit_bytes=big_vmem),
        cost_estimate=pl.CostEstimate(
            flops=2 * rows * depth * columns,
            bytes_accessed=2 * (rows * depth + rows * columns + depth * columns),
            transcendentals=0,
        ),
        name="weight_grad",
    )(left, right)


def contrast_kernel(
    count, own, halves, cls_ref, q_ref, pos_ref, qg_ref, lead_ref, loss_ref,
    mine_ref, all_ref, part_ref, got_ref, stat_ref, term_ref,
    sem_a, sem_b, sem_c, sem_d, sem_e, sem_f, sem_g, sem_h,
):
    me = lax.axis_index("dp")
    half = lax.axis_index("tensor")
    other = 1 - half
    kind = own // 2
    firsts = [cls_ref[0, :kind, :]] + [cls_ref[1 + index, :1, :] for index in range(kind)]
    mine_ref[...] = jnp.concatenate(firsts, axis=0).astype(jnp.bfloat16)
    barrier = pltpu.get_barrier_semaphore()

    @pl.loop(1, count)
    def _(gap):
        pl.semaphore_signal(
            barrier, inc=1, device_id=(lax.rem(me + gap, count), half), device_id_type=MESH
        )

    pl.semaphore_signal(barrier, inc=1, device_id=(me, other), device_id_type=MESH)
    pl.semaphore_wait(barrier, count)

    def push(source, target, sends, lands, gap):
        peer = lax.rem(me + gap, count)
        return pltpu.make_async_remote_copy(
            src_ref=source(peer),
            dst_ref=target.at[me],
            send_sem=sends.at[gap],
            recv_sem=lands.at[me],
            device_id=(peer, half),
            device_id_type=MESH,
        )

    def landed(source, target, sends, lands, gap):
        origin = lax.rem(me + count - gap, count)
        return pltpu.make_async_remote_copy(
            src_ref=target.at[origin],
            dst_ref=target.at[origin],
            send_sem=sends.at[gap],
            recv_sem=lands.at[origin],
            device_id=(origin, half),
            device_id_type=MESH,
        )

    def whole(peer):
        return mine_ref

    @pl.loop(1, count)
    def _(gap):
        push(whole, all_ref, sem_a, sem_b, gap).start()

    all_ref[me] = mine_ref[...]

    @pl.loop(1, count)
    def _(gap):
        landed(whole, all_ref, sem_a, sem_b, gap).wait_recv()

    passages = all_ref[...].astype(jnp.float32).reshape(count * own, D).astype(jnp.bfloat16)
    queries = q_ref[...]
    logits = dot_nt(queries, passages)
    column = lax.broadcasted_iota(jnp.int32, logits.shape, 1)
    near = column % own
    index = (column // own) * (own * halves) + (near // kind) * (kind * halves)
    index = index + half * kind + near % kind
    query = lax.broadcasted_iota(jnp.int32, logits.shape, 0)
    positive = jnp.zeros(logits.shape, jnp.int32)
    for each in range(logits.shape[0]):
        positive = jnp.where(query == each, pos_ref[each], positive)
    chosen = jnp.where(index == positive, 1.0, 0.0)
    highest = jnp.max(logits, axis=1, keepdims=True)
    summed = jnp.sum(jnp.exp(logits - highest), axis=1, keepdims=True)
    picked = jnp.sum(logits * chosen, axis=1, keepdims=True)
    lane = lax.broadcasted_iota(jnp.int32, (logits.shape[0], 128), 1)
    stat_ref[half] = jnp.where(lane == 0, highest, jnp.where(lane == 1, summed, picked))

    def swap(ref, send, land):
        return pltpu.make_async_remote_copy(
            src_ref=ref.at[half],
            dst_ref=ref.at[half],
            send_sem=send,
            recv_sem=land,
            device_id=(me, other),
            device_id_type=MESH,
        )

    def swapped(ref, send, land):
        return pltpu.make_async_remote_copy(
            src_ref=ref.at[other],
            dst_ref=ref.at[other],
            send_sem=send,
            recv_sem=land,
            device_id=(me, other),
            device_id_type=MESH,
        )

    swap(stat_ref, sem_e, sem_f).start()
    swapped(stat_ref, sem_e, sem_f).wait_recv()
    low, high = stat_ref[0], stat_ref[1]
    top = jnp.maximum(low[:, 0:1], high[:, 0:1])
    total = low[:, 1:2] * jnp.exp(low[:, 0:1] - top) + high[:, 1:2] * jnp.exp(high[:, 0:1] - top)
    losses = top + jnp.log(total) - (low[:, 2:3] + high[:, 2:3])
    loss_ref[...] = jnp.broadcast_to(jnp.sum(losses, axis=0, keepdims=True), loss_ref.shape)
    logit_back = (jnp.exp(logits - top) / total - chosen).astype(jnp.bfloat16)
    terms = dot_tn(logit_back, queries)
    part_ref[...] = terms.reshape(count, own, D).astype(jnp.bfloat16)

    def piece(peer):
        return part_ref.at[peer]

    @pl.loop(1, count)
    def _(gap):
        push(piece, got_ref, sem_c, sem_d, gap).start()

    term_ref[half] = dot_nn(logit_back, passages)
    swap(term_ref, sem_g, sem_h).start()
    got_ref[me] = part_ref[me]
    swapped(term_ref, sem_g, sem_h).wait_recv()
    qg_ref[...] = term_ref[0] + term_ref[1]

    @pl.loop(1, count)
    def _(gap):
        landed(piece, got_ref, sem_c, sem_d, gap).wait_recv()

    lead = jnp.sum(got_ref[...].astype(jnp.float32), axis=0)
    lead_ref[...] = jnp.zeros_like(lead_ref)
    lead_ref[0, :kind, :] = lead[:kind]
    for index in range(kind):
        lead_ref[1 + index, :1, :] = lead[kind + index : kind + index + 1]

    @pl.loop(1, count)
    def _(gap):
        push(whole, all_ref, sem_a, sem_b, gap).wait_send()
        push(piece, got_ref, sem_c, sem_d, gap).wait_send()

    swap(stat_ref, sem_e, sem_f).wait_send()
    swap(term_ref, sem_g, sem_h).wait_send()


def contrast(leading, queries, positives):
    count = lax.axis_size("dp")
    halves = lax.axis_size("tensor")
    own = 2 * (leading.shape[0] - 1)
    here = queries.shape[0]
    whole = pl.BlockSpec(memory_space=pltpu.VMEM)
    query_gradient, lead_back, loss = pl.pallas_call(
        functools.partial(contrast_kernel, count, own, halves),
        in_specs=[whole] * 2 + [pl.BlockSpec(memory_space=pltpu.SMEM)],
        out_specs=[whole] * 3,
        out_shape=[
            jax.ShapeDtypeStruct((here, D), jnp.float32),
            jax.ShapeDtypeStruct(leading.shape, jnp.float32),
            jax.ShapeDtypeStruct((8, 128), jnp.float32),
        ],
        scratch_shapes=[
            pltpu.VMEM((own, D), jnp.bfloat16),
            pltpu.VMEM((count, own, D), jnp.bfloat16),
            pltpu.VMEM((count, own, D), jnp.bfloat16),
            pltpu.VMEM((count, own, D), jnp.bfloat16),
            pltpu.VMEM((halves, here, 128), jnp.float32),
            pltpu.VMEM((halves, here, D), jnp.float32),
            pltpu.SemaphoreType.DMA((count,)),
            pltpu.SemaphoreType.DMA((count,)),
            pltpu.SemaphoreType.DMA((count,)),
            pltpu.SemaphoreType.DMA((count,)),
            pltpu.SemaphoreType.DMA,
            pltpu.SemaphoreType.DMA,
            pltpu.SemaphoreType.DMA,
            pltpu.SemaphoreType.DMA,
        ],
        compiler_params=pltpu.CompilerParams(
            collective_id=1, has_side_effects=True, vmem_limit_bytes=big_vmem
        ),
        name="contrast",
    )(leading, queries, positives)
    return query_gradient, lead_back, loss


def total_kernel(bits, value_ref, out_ref, slots, send_sem, recv_sem):
    me = lax.axis_index("dp")
    half = lax.axis_index("tensor")

    def partner(stage):
        if stage == bits:
            return (me, 1 - half)
        gap = 1 << stage
        up = 1 - 2 * lax.rem(me // gap, 2)
        return (me + up * gap, half)

    barrier = pltpu.get_barrier_semaphore()
    for stage in range(bits + 1):
        pl.semaphore_signal(barrier, inc=1, device_id=partner(stage), device_id_type=MESH)
    pl.semaphore_wait(barrier, bits + 1)
    out_ref[...] = value_ref[...]
    slots[0] = value_ref[...]
    copies = []
    for stage in range(bits + 1):
        copy = pltpu.make_async_remote_copy(
            src_ref=slots.at[2 * stage],
            dst_ref=slots.at[2 * stage + 1],
            send_sem=send_sem.at[stage],
            recv_sem=recv_sem.at[stage],
            device_id=partner(stage),
            device_id_type=MESH,
        )
        copy.start()
        copies.append(copy)
        copy.wait_recv()
        summed = slots[2 * stage] + slots[2 * stage + 1]
        if stage < bits:
            slots[2 * stage + 2] = summed
        else:
            out_ref[...] = summed
    for copy in copies:
        copy.wait_send()


def all_total(value):
    bits = (lax.axis_size("dp") - 1).bit_length()
    whole = pl.BlockSpec(memory_space=pltpu.VMEM)
    return pl.pallas_call(
        functools.partial(total_kernel, bits),
        in_specs=[whole],
        out_specs=whole,
        out_shape=jax.ShapeDtypeStruct(value.shape, value.dtype),
        scratch_shapes=[
            pltpu.VMEM((2 * bits + 2,) + value.shape, value.dtype),
            pltpu.SemaphoreType.DMA((bits + 1,)),
            pltpu.SemaphoreType.DMA((bits + 1,)),
        ],
        compiler_params=pltpu.CompilerParams(collective_id=2, has_side_effects=True),
        name="all_total",
    )(value)


def tensor_swap(value):
    return lax.ppermute(value, "tensor", [(0, 1), (1, 0)])


def gathered(own):
    return lax.all_gather(own, ("tensor", "dp"), axis=0, tiled=True).reshape(
        lax.axis_size("tensor"), -1, own.shape[1]
    )


def scattered(whole):
    return lax.psum_scatter(
        whole.reshape(-1, whole.shape[2]), ("tensor", "dp"), scatter_dimension=0, tiled=True
    ).astype(jnp.float32)


def grid_place():
    me = lax.axis_index("dp")
    return lax.axis_index("tensor"), me // 4, lax.rem(me // 2, 2), lax.rem(me, 2)


def at_place(t, z, x, c):
    return (z * 4 + x * 2 + c, t)


def greet_neighbours(cube=False):
    t, z, x, c = grid_place()
    barrier = pltpu.get_barrier_semaphore()
    others = [at_place(t, lax.rem(z + gap, 4), x, c) for gap in range(1, 4)]
    others += [at_place(1 - t, z, x, c), at_place(t, z, 1 - x, c), at_place(t, z, x, 1 - c)]
    if cube:
        others += [at_place(1 - t, z, 1 - x, c), at_place(1 - t, z, x, 1 - c)]
        others += [at_place(t, z, 1 - x, 1 - c), at_place(1 - t, z, 1 - x, 1 - c)]
    for other in others:
        pl.semaphore_signal(barrier, inc=1, device_id=other, device_id_type=MESH)
    pl.semaphore_wait(barrier, len(others))


class Gather:
    count = 19

    def __init__(self, own, buffer, sends, lands, local, index):
        self.own, self.buffer, self.index = own, buffer, index
        self.sends, self.lands, self.local = sends, lands, local
        t, z, x, c = self.place = grid_place()
        even = c == 0
        self.mid = (jnp.where(even, t, 1 - t), jnp.where(even, 1 - x, x))
        self.last = (jnp.where(even, 1 - t, t), jnp.where(even, x, 1 - x))
        self.both = (1 - t, 1 - x)

    def group(self, spot, c):
        return self.buffer.at[spot[0], :, spot[1], c]

    def slot(self, spot, gap):
        _, z, _, c = self.place
        return self.buffer.at[spot[0], lax.rem(z + 4 - gap, 4), spot[1], c]

    def copy(self, source, target, which, device):
        return pltpu.make_async_remote_copy(
            src_ref=source,
            dst_ref=target,
            send_sem=self.sends.at[self.index, which],
            recv_sem=self.lands.at[self.index, which],
            device_id=device,
            device_id_type=MESH,
        )

    def outgoing(self, which):
        t, z, x, c = self.place
        here = (t, x)
        middle = at_place(self.mid[0], z, self.mid[1], c)
        last = at_place(self.last[0], z, self.last[1], c)
        if which < 3:
            device = at_place(t, lax.rem(z + which + 1, 4), x, c)
            return self.copy(self.own, self.slot(here, 0), which, device)
        if which < 5:
            return self.copy(self.own, self.slot(here, 0), which, (middle, last)[which - 3])
        if which < 11:
            slot = self.slot(here, (which - 5) % 3 + 1)
            return self.copy(slot, slot, which, middle if which < 8 else last)
        if which < 15:
            slot = self.slot(self.mid, which - 11)
            return self.copy(slot, slot, which, last)
        group = self.group((here, self.mid, self.last, self.both)[which - 15], c)
        return self.copy(group, group, which, at_place(t, z, x, 1 - c))

    def arrived(self, which):
        t, z, x, c = self.place
        if which < 3:
            target = self.slot((t, x), which + 1)
        elif which < 5:
            target = self.slot((self.mid, self.last)[which - 3], 0)
        elif which < 11:
            target = self.slot(self.mid if which < 8 else self.last, (which - 5) % 3 + 1)
        elif which < 15:
            target = self.slot(self.both, which - 11)
        else:
            target = self.group(((t, x), self.last, self.mid, self.both)[which - 15], 1 - c)
        self.copy(target, target, which, at_place(t, z, x, 1 - c)).wait_recv()

    def keep(self):
        t, z, x, c = self.place
        return pltpu.make_async_copy(self.own, self.slot((t, x), 0), self.local.at[self.index])

    def start(self):
        self.keep().start()
        for which in (0, 2, 1, 3, 4):
            self.outgoing(which).start()

    def line_part(self, gap):
        self.arrived(gap)
        self.outgoing(5 + gap).start()
        self.outgoing(8 + gap).start()

    def line_kept(self):
        self.keep().wait()
        self.outgoing(15).start()

    def line_ready(self):
        for gap in (0, 2, 1):
            self.line_part(gap)
        self.line_kept()

    def middle_ready(self):
        self.arrived(3)
        self.outgoing(11).start()
        for gap in (0, 2, 1):
            self.arrived(5 + gap)
            self.outgoing(12 + gap).start()
        self.outgoing(16).start()

    def last_ready(self):
        for which in (4, 8, 10, 9):
            self.arrived(which)
        self.outgoing(17).start()

    def both_ready(self):
        for which in range(11, 15):
            self.arrived(which)
        self.outgoing(18).start()

    def finish(self):
        for which in range(15, 19):
            self.arrived(which)

    def drain(self):
        for which in range(self.count):
            self.outgoing(which).wait_send()


def forward_gather_kernel(
    piece, chunks, spans, mixing_ref, middle_ref, shrink_ref, offsets_ref, scales_ref, x_ref,
    qkv_ref, ctx_ref, hb_ref, g_ref, slope_ref, n1_ref, r1_ref, out_ref, n2_ref, r2_ref, lead_ref,
    mixing_out, middle_out, shrink_out,
    w_ref, me_ref, st_ref, both_ref, flat_ref, up_ref, ctx_all, g_all, hidden_all,
    sends, lands, local, swap_send, swap_land, stores,
):
    step = pl.program_id(0)
    t, z, x, c = grid_place()
    mixing, middle, shrink = (
        Gather(own, full, sends, lands, local, index)
        for index, (own, full) in enumerate(
            ((mixing_ref, w_ref), (middle_ref, me_ref), (shrink_ref, st_ref))
        )
    )

    def swap(which):
        return pltpu.make_async_remote_copy(
            src_ref=both_ref.at[which],
            dst_ref=both_ref.at[which],
            send_sem=swap_send,
            recv_sem=swap_land,
            device_id=at_place(1 - t, z, x, c),
            device_id_type=MESH,
        )

    def store(index):
        target = (mixing_out, middle_out, shrink_out)[index]
        return pltpu.make_async_copy((w_ref, me_ref, st_ref)[index], target, stores.at[index])

    rows = x_ref.shape[0]
    width = w_ref.shape[5] // 3

    @pl.when(step == 0)
    def _():
        both_ref[t] = offsets_ref[...]
        greet_neighbours()
        mixing.start()
        swap(t).start()
        middle.start()
        shrink.start()
        mixing.line_ready()
        mixing.middle_ready()
        mixing.last_ready()
        middle.line_part(0)
        mixing.both_ready()
        mixing.finish()
        store(0).start()
        middle.line_part(2)
        middle.line_part(1)
        middle.line_kept()
        swap(1 - t).wait_recv()
        for half in range(2):
            flat_ref[half] = jnp.concatenate(
                [both_ref[half, index : index + 1, :] for index in range(both_ref.shape[1])], axis=1
            )
            wide = up_ref.shape[1] // 2
            up_ref[:, half * wide : (half + 1) * wide] = flat_ref[half][:, 2 * width :]

    @pl.when(step == 2)
    def _():
        middle.middle_ready()

    @pl.when(step == chunks - 1)
    def _():
        shrink.line_ready()
        middle.last_ready()

    @pl.when(step == chunks)
    def _():
        middle.both_ready()
        middle.finish()
        store(1).start()

    @pl.when(step == chunks + 1)
    def _():
        shrink.middle_ready()

    @pl.when(step == 2 * chunks - 2)
    def _():
        shrink.last_ready()

    @pl.when(step == 2 * chunks)
    def _():
        shrink.both_ready()
        shrink.finish()
        store(2).start()

    def here(first):
        return pl.ds(pl.multiple_of((step - first) * rows, rows), rows)

    @pl.when(step < chunks)
    def _():
        visible = visible_keys(spans, step, rows, piece, 1)
        for half in range(2):
            weight = w_ref[half].reshape(D, 3 * width)
            bias = flat_ref[half]
            bias = jnp.concatenate(
                [bias[:, :width], jnp.zeros((1, width), jnp.float32), bias[:, width : 2 * width]],
                axis=1,
            )
            attend_half(half, weight, bias, visible, x_ref, qkv_ref, ctx_ref)
        ctx_all[here(0), :] = ctx_ref[...]

    @pl.when(jnp.logical_and(step >= chunks, step < 2 * chunks))
    def _():
        outs = (hb_ref, g_ref, slope_ref, n1_ref, r1_ref)
        place = here(chunks)
        hidden, activated = feed_up(ctx_all[place, :], x_ref[...], me_ref, scales_ref, up_ref, outs)
        hidden_all[place, :] = hidden
        for half in range(2):
            wide = st_ref.shape[5]
            g_all[place, half * wide : (half + 1) * wide] = activated[half]

    @pl.when(step >= 2 * chunks)
    def _():
        place = here(2 * chunks)
        wide = st_ref.shape[5]
        activated = [g_all[place, half * wide : (half + 1) * wide] for half in range(2)]
        outs = (out_ref, n2_ref, r2_ref, lead_ref)
        feed_down(piece, hidden_all[place, :], activated, st_ref, scales_ref, outs)

    @pl.when(step == pl.num_programs(0) - 1)
    def _():
        swap(t).wait_send()
        for each in (mixing, middle, shrink):
            each.drain()
        for index in range(3):
            store(index).wait()


def forward_gather(piece, spans, inputs, owns, offsets, scales, chunk):
    rows = inputs.shape[0]
    chunks = rows // chunk
    halves = lax.axis_size("tensor")
    columns = halves * owns[0].shape[1]
    anywhere = pl.BlockSpec(memory_space=pl.ANY)
    bf16, f32 = jnp.bfloat16, jnp.float32

    def buffer(own):
        return (halves, 4, 2, 2) + own.shape

    def spec(width, first):
        return pl.BlockSpec((chunk, width), lambda i: (jnp.clip(i - first * chunks, 0, chunks - 1), 0))

    shapes = [(columns, bf16, 0), (D, bf16, 0)]
    shapes += [(D, bf16, 1), (FF, bf16, 1), (FF, bf16, 1), (D, f32, 1), (1, f32, 1)]
    shapes += [(D, bf16, 2), (D, f32, 2), (1, f32, 2)]
    outs = pl.pallas_call(
        functools.partial(forward_gather_kernel, piece, chunks),
        grid=(3 * chunks,),
        in_specs=[
            pl.BlockSpec(memory_space=pltpu.SMEM),
            *(full_spec(own.shape) for own in owns),
            full_spec((offsets.shape[0] // 128, 128)),
            full_spec(scales.shape),
            pl.BlockSpec((chunk, D), lambda i: (jnp.minimum(i, 2 * chunks - 1) % chunks, 0)),
        ],
        out_specs=[spec(width, first) for width, _, first in shapes]
        + [pl.BlockSpec((1, 8, D), lambda i: (jnp.maximum(i - 2 * chunks, 0), 0, 0))]
        + [anywhere] * 3,
        out_shape=[jax.ShapeDtypeStruct((rows, width), dtype) for width, dtype, _ in shapes]
        + [jax.ShapeDtypeStruct((chunks, 8, D), f32)]
        + [jax.ShapeDtypeStruct(buffer(own), bf16) for own in owns],
        scratch_shapes=[pltpu.VMEM(buffer(own), bf16) for own in owns]
        + [
            pltpu.VMEM((halves, offsets.shape[0] // 128, 128), f32),
            pltpu.VMEM((halves, 1, offsets.shape[0]), f32),
            pltpu.VMEM((1, FF), f32),
            pltpu.VMEM((rows, D), bf16),
            pltpu.VMEM((rows, FF), bf16),
            pltpu.VMEM((rows, D), f32),
            pltpu.SemaphoreType.DMA((3, Gather.count)),
            pltpu.SemaphoreType.DMA((3, Gather.count)),
            pltpu.SemaphoreType.DMA((3,)),
            pltpu.SemaphoreType.DMA,
            pltpu.SemaphoreType.DMA,
            pltpu.SemaphoreType.DMA((3,)),
        ],
        compiler_params=pltpu.CompilerParams(
            collective_id=3, has_side_effects=True, vmem_limit_bytes=big_vmem
        ),
        name="forward_gather",
    )(spans, *owns, offsets.reshape(-1, 128), scales, inputs)
    fulls = [full.reshape(halves, -1, full.shape[-1]) for full in outs[-3:]]
    return outs[:2], outs[2:-3], fulls


class Scatter:
    def __init__(self, whole, acc, sib, one, two, line, out, sends, lands, local, index):
        self.whole, self.acc, self.sib, self.out, self.index = whole, acc, sib, out, index
        self.one, self.two, self.line = one, two, line
        self.sends, self.lands, self.local = sends, lands, local
        t, z, x, c = self.place = grid_place()
        even = c == 0
        self.first = (jnp.where(even, 1 - t, t), jnp.where(even, x, 1 - x))
        self.second = (jnp.where(even, t, 1 - t), jnp.where(even, 1 - x, x))
        self.order = (2, 1, 0, 3)
        self.spots = (self.first, (1 - t, 1 - x), self.second, (t, x))

    def copy(self, source, target, which, device):
        return pltpu.make_async_remote_copy(
            src_ref=source,
            dst_ref=target,
            send_sem=self.sends.at[self.index, which],
            recv_sem=self.lands.at[self.index, which],
            device_id=device,
            device_id_type=MESH,
        )

    def outgoing(self, which):
        t, z, x, c = self.place
        if which < 4:
            spot = self.spots[self.order[which]]
            return self.copy(
                self.whole.at[spot[0], :, spot[1], 1 - c],
                self.sib.at[spot[0], :, spot[1]],
                which,
                at_place(t, z, x, 1 - c),
            )
        if which < 6:
            spot = self.spots[which - 4]
            device = at_place(self.first[0], z, self.first[1], c)
            return self.copy(self.acc.at[spot[0], :, spot[1]], self.one.at[which - 4], which, device)
        if which == 6:
            spot = self.second
            device = at_place(spot[0], z, spot[1], c)
            return self.copy(self.acc.at[spot[0], :, spot[1]], self.two, which, device)
        there = lax.rem(z + which - 6, 4)
        return self.copy(
            self.acc.at[t, there, x], self.line.at[which - 7], which, at_place(t, there, x, c)
        )

    def arrived(self, which):
        t, z, x, c = self.place
        if which < 4:
            spot = self.spots[which]
            target = self.sib.at[spot[0], :, spot[1]]
        elif which < 6:
            target = self.one.at[which - 4]
        elif which == 6:
            target = self.two
        else:
            target = self.line.at[which - 7]
        self.copy(target, target, which, at_place(t, z, x, 1 - c)).wait_recv()

    def load(self, which):
        c = self.place[3]
        spot = self.spots[which]
        return pltpu.make_async_copy(
            self.whole.at[spot[0], :, spot[1], c],
            self.acc.at[spot[0], :, spot[1]],
            self.local.at[self.index, which],
        )

    def add(self, spot, read):
        @pl.loop(0, 4)
        def _(z):
            low = self.acc[spot[0], z, spot[1]].astype(jnp.float32)
            low = low + read(z).astype(jnp.float32)
            self.acc[spot[0], z, spot[1]] = low.astype(jnp.bfloat16)

    def start(self):
        for which in range(4):
            self.outgoing(which).start()
            self.load(which).start()

    def cores_ready(self):
        for which in range(4):
            spot = self.spots[which]
            self.arrived(which)
            self.load(which).wait()
            self.add(spot, lambda z: self.sib[spot[0], z, spot[1]])
            if which < 2:
                self.outgoing(4 + which).start()

    def first_ready(self):
        self.arrived(5)
        self.add(self.second, lambda z: self.one[1, z])
        self.outgoing(6).start()
        self.arrived(4)
        self.add(self.spots[3], lambda z: self.one[0, z])

    def second_ready(self):
        self.arrived(6)
        self.add(self.spots[3], lambda z: self.two[z])
        for which in range(7, 10):
            self.outgoing(which).start()

    def finish(self):
        t, z, x, c = self.place
        total = self.acc[t, z, x].astype(jnp.float32)
        for which in range(7, 10):
            self.arrived(which)
            total = total + self.line[which - 7].astype(jnp.float32)
        self.out[...] = total
        return jnp.sum(total * total, axis=0, keepdims=True)

    def drain(self):
        for which in range(10):
            self.outgoing(which).wait_send()


class LateScatter(Scatter):
    def __init__(self, *args):
        super().__init__(*args)
        _, _, x, _ = self.place
        self.order = (0, 1, 2, 3)
        self.spots = ((0, 1 - x), (1, 1 - x), (0, x), (1, x))

    def outgoing(self, which):
        t, z, x, c = self.place
        if which < 4:
            return super().outgoing(which)
        if which < 6:
            side = which - 4
            return self.copy(
                self.acc.at[side, :, 1 - x], self.one.at[side], which, at_place(t, z, 1 - x, c)
            )
        if which == 6:
            return self.copy(self.acc.at[1 - t, z, x], self.two, which, at_place(1 - t, z, x, c))
        there = lax.rem(z + which - 6, 4)
        return self.copy(
            self.acc.at[:, there, x], self.line.at[which - 7], which, at_place(t, there, x, c)
        )

    def first_ready(self):
        for side in range(2):
            self.arrived(4 + side)
            self.add((side, self.place[2]), lambda z: self.one[side, z])
        for which in range(7, 10):
            self.outgoing(which).start()

    def second_ready(self):
        t, z, x, _ = self.place
        for which in range(7, 10):
            self.arrived(which)

        def total(side):
            value = self.acc[side, z, x].astype(jnp.float32)
            for which in range(3):
                value = value + self.line[which, side].astype(jnp.float32)
            return value

        self.acc[1 - t, z, x] = total(1 - t).astype(jnp.bfloat16)
        self.outgoing(6).start()
        self.out[...] = total(t)

    def finish(self):
        self.arrived(6)
        total = self.out[...] + self.two[...].astype(jnp.float32)
        self.out[...] = total
        return jnp.sum(total * total, axis=0, keepdims=True)


class Total:
    def __init__(self, slots, line, sends, lands):
        self.slots, self.line, self.sends, self.lands = slots, line, sends, lands
        t, z, x, c = self.place = grid_place()
        self.partners = (at_place(t, z, x, 1 - c), at_place(t, z, 1 - x, c), at_place(1 - t, z, x, c))

    def pair(self, stage):
        return pltpu.make_async_remote_copy(
            src_ref=self.slots.at[2 * stage],
            dst_ref=self.slots.at[2 * stage + 1],
            send_sem=self.sends.at[stage],
            recv_sem=self.lands.at[stage],
            device_id=self.partners[stage],
            device_id_type=MESH,
        )

    def along(self, gap):
        t, z, x, c = self.place
        return pltpu.make_async_remote_copy(
            src_ref=self.line.at[z],
            dst_ref=self.line.at[z],
            send_sem=self.sends.at[2 + gap],
            recv_sem=self.lands.at[2 + gap],
            device_id=at_place(t, lax.rem(z + gap, 4), x, c),
            device_id_type=MESH,
        )

    def landed(self, gap):
        t, z, x, c = self.place
        spot = self.line.at[lax.rem(z + 4 - gap, 4)]
        pltpu.make_async_remote_copy(
            src_ref=spot,
            dst_ref=spot,
            send_sem=self.sends.at[2 + gap],
            recv_sem=self.lands.at[2 + gap],
            device_id=self.partners[0],
            device_id_type=MESH,
        ).wait_recv()

    def start(self, value):
        self.slots[0] = value
        self.pair(0).start()

    def advance(self, stage):
        self.pair(stage).wait_recv()
        summed = self.slots[2 * stage] + self.slots[2 * stage + 1]
        if stage < 2:
            self.slots[2 * stage + 2] = summed
            self.pair(stage + 1).start()
            return
        z = self.place[1]
        self.line[z] = summed
        for gap in range(1, 4):
            self.along(gap).start()

    def finish(self):
        for gap in range(1, 4):
            self.landed(gap)
        return (self.line[0] + self.line[1]) + (self.line[2] + self.line[3])

    def drain(self):
        for stage in range(3):
            self.pair(stage).wait_send()
        for gap in range(1, 4):
            self.along(gap).wait_send()


class Cube:
    def __init__(self, slots, line, sends, lands):
        self.slots, self.line, self.sends, self.lands = slots, line, sends, lands
        self.place = grid_place()

    def turned(self, flip):
        t, _, x, c = self.place
        return (1 - t if flip & 4 else t), (1 - x if flip & 2 else x), (1 - c if flip & 1 else c)

    def copy(self, slot, which, device):
        return pltpu.make_async_remote_copy(
            src_ref=slot,
            dst_ref=slot,
            send_sem=self.sends.at[which],
            recv_sem=self.lands.at[which],
            device_id=device,
            device_id_type=MESH,
        )

    def slot(self, flip):
        t, x, c = self.turned(flip)
        return self.slots.at[t * 4 + x * 2 + c]

    def push(self, flip):
        t, x, c = self.turned(flip)
        return self.copy(self.slot(0), flip - 1, at_place(t, self.place[1], x, c))

    def along(self, gap, back=False):
        t, z, x, c = self.place
        slot = self.line.at[lax.rem(z + 4 - gap, 4) if back else z]
        return self.copy(slot, 6 + gap, at_place(t, lax.rem(z + gap, 4), x, c))

    def total(self, value):
        t, z, x, c = self.place
        self.slots[t * 4 + x * 2 + c] = value
        for flip in range(1, 8):
            self.push(flip).start()
        for flip in range(1, 8):
            self.copy(self.slot(flip), flip - 1, self.place_of(flip)).wait_recv()
        self.line[z] = jnp.sum(self.slots[...], axis=0)
        for gap in range(1, 4):
            self.along(gap).start()
        for gap in range(1, 4):
            self.along(gap, True).wait_recv()
        return (self.line[0] + self.line[1]) + (self.line[2] + self.line[3])

    def place_of(self, flip):
        t, x, c = self.turned(flip)
        return at_place(t, self.place[1], x, c)

    def drain(self):
        for flip in range(1, 8):
            self.push(flip).wait_send()
        for gap in range(1, 4):
            self.along(gap).wait_send()


def scatter_buffers(whole, columns, late=False):
    halves = lax.axis_size("tensor")
    rows = whole.shape[1] // lax.axis_size("dp")
    two, line = ((), (3, halves)) if late else ((4,), (3,))
    shapes = ((halves, 4, 2), (halves, 4, 2), (2, 4), two, line)
    return [pltpu.VMEM(shape + (rows, columns), jnp.bfloat16) for shape in shapes]


def scatter_parts(pieces, buffers, sems, kind=Scatter):
    return [
        kind(
            whole.at[:, :, :, :, :, first : first + columns],
            *buffers[5 * index : 5 * index + 5],
            out.at[:, first : first + columns],
            *sems,
            index,
        )
        for index, (whole, out, first, columns) in enumerate(pieces)
    ]


def scatter_sems(count):
    return [
        pltpu.SemaphoreType.DMA((count, 10)),
        pltpu.SemaphoreType.DMA((count, 10)),
        pltpu.SemaphoreType.DMA((count, 4)),
    ]


def scatter_input(whole):
    return whole.reshape(lax.axis_size("tensor"), 4, 2, 2, -1, whole.shape[2])


def scatter_shape(whole):
    return jax.ShapeDtypeStruct((whole.shape[1] // lax.axis_size("dp"), whole.shape[2]), jnp.float32)


def push_partner(source, target, index, sends, lands):
    t, z, x, c = grid_place()
    return pltpu.make_async_remote_copy(
        src_ref=source.at[index],
        dst_ref=target.at[index],
        send_sem=sends.at[index],
        recv_sem=lands.at[index],
        device_id=at_place(1 - t, z, x, c),
        device_id_type=MESH,
    )


class Plan:
    def __init__(self, actions, times):
        self.at, self.rest = {}, []
        points = sorted(times.items(), key=lambda item: item[1])
        at = 0
        for due, action in sorted(actions, key=lambda item: item[0]):
            while at < len(points) and points[at][1] < due:
                at += 1
            if at < len(points):
                self.at.setdefault(points[at][0], []).append(action)
            else:
                self.rest.append(action)

    def run(self, point):
        for (step, where), actions in self.at.items():
            if where == point:

                @pl.when(pl.program_id(0) == step)
                def _():
                    for action in actions:
                        action()

    def finish(self):
        for action in self.rest:
            action()


def scatter_actions(parts, ready, link, ended=lambda part: part.finish):
    actions = []
    for index, part in enumerate(parts):
        due = ready + link * index
        actions += [
            (due, part.cores_ready),
            (due + link + 2, part.first_ready),
            (due + 2 * link + 4, part.second_ready),
            (due + 2 * link + 7, ended(part)),
        ]
    return actions


def feed_back_scatter_kernel(chunks, early, columns, whole_ref, tail_ref, *refs):
    ins, outs, (tail_out, out_ref) = refs[:9], refs[9:15], refs[15:17]
    scratch, rest = refs[17:20], refs[20:]
    count = whole_ref.shape[5] // columns
    buffers, sems, (sends, lands) = rest[: 5 * count], rest[5 * count : 5 * count + 3], rest[5 * count + 3 :]
    parts = scatter_parts(
        [(whole_ref, out_ref, index * columns, columns) for index in range(count)], buffers, sems, LateScatter
    )

    def begin():
        greet_neighbours()
        for part in parts:
            part.start()
        for index in range(early):
            push_partner(tail_ref.at[chunks - early :], tail_out, index, sends, lands).start()

    actions = [(0, begin)] + scatter_actions(parts, 8, 6.6)
    steps = chunks + D // ins[5].shape[1] + 2 * (ins[7].shape[2] // outs[5].shape[2])
    times = {(step, 0): 4 + 5.3 * step for step in range(chunks)}
    times |= {(step, 0): 30.5 + 1.7 * (step - chunks) for step in range(chunks, steps)}
    times |= {(step, 1 + half): 6 + 5.3 * step + 2 * half for step in range(chunks) for half in range(2)}
    times[(0, 0)] = 0
    plan = Plan(actions, times)
    feed_back_kernel(chunks, *ins, *outs, *scratch, plan.run)

    @pl.when(pl.program_id(0) == pl.num_programs(0) - 1)
    def _():
        plan.finish()
        for part in parts:
            part.drain()
        for index in range(early):
            push_partner(tail_ref.at[chunks - early :], tail_out, index, sends, lands).wait()


def attend_last_kernel(piece, chunks, columns, spans, one_ref, two_ref, *refs):
    ins, left_ref, done_ref, first_ref, second_ref, upward_ref, loss_ref = refs[:4], *refs[4:10]
    dx_ref, low_out, one_out, two_out, last_out, total_ref, norm_ref = refs[10:17]
    dproj_ref, bias_ref, turned_ref, grad_ref, square_ref, low_ref, sends, lands = refs[17:25]
    rest = refs[25:]
    count = one_ref.shape[5] // columns + 1
    late = scatter_parts(
        [(one_ref, one_out, index * columns, columns) for index in range(count - 1)]
        + [(two_ref, two_out, 0, columns)],
        rest[: 5 * count],
        rest[5 * count : 5 * count + 3],
        LateScatter,
    )
    rest = rest[5 * count + 3 :]
    tail = grad_ref.shape[5] // columns
    last = scatter_parts(
        [(grad_ref, last_out, index * columns, columns) for index in range(tail)],
        rest[: 5 * tail],
        rest[5 * tail : 5 * tail + 3],
    )
    rest = rest[5 * tail + 3 :]
    vector, norm = Total(*rest[:4]), Cube(*rest[4:])
    step = pl.program_id(0)

    def begin():
        greet_neighbours(True)
        for part in late:
            part.start()
        square_ref[...] = jnp.zeros_like(square_ref)
        turned_ref[...] = left_ref[...].T

    def ended(part):
        def action():
            square_ref[0:1, :] += part.finish()

        return action

    actions = [(0, begin)] + scatter_actions(late, 8, 6.6, ended)
    actions += scatter_actions(last, 46, 5, ended)
    actions += [(46.5, lambda: vector.advance(0)), (50, lambda: vector.advance(1)), (57, lambda: vector.advance(2))]
    times = {(step, point): 4 + 7.3 * step + 1.15 * point for step in range(chunks) for point in range(7)}
    times |= {(chunks + tile, 0): 41 + 2.0 * tile for tile in range(2 * tail)}
    times[(0, 0)] = 0
    plan = Plan(actions, times)
    plan.run(0)

    @pl.when(step < chunks)
    def _():
        rows = dx_ref.shape[0]
        here = dproj_ref.at[pl.ds(pl.multiple_of(step * rows, rows), rows), :]
        attend_back_kernel(piece, spans, *ins, here, dx_ref, bias_ref, low_ref, plan.run)

    for index in range(chunks):

        @pl.when(step == index)
        def _():
            if index == chunks - 1:
                base = bias_ref.shape[1] // 2
                wide = upward_ref.shape[1] // 2
                lines = [first_ref[0:2, :], second_ref[0:2, :], first_ref[2:3, :], second_ref[2:3, :]]
                for half in range(2):
                    at = half * base
                    pair = [bias_ref[0:1, at : at + columns]]
                    pair += [bias_ref[0:1, at + 2 * columns : at + 3 * columns]]
                    lines.append(jnp.concatenate(pair, axis=1))
                    lines += [
                        upward_ref[0:1, half * wide + first : half * wide + first + D]
                        for first in range(0, wide, D)
                    ]
                column = lax.broadcasted_iota(jnp.int32, (1, D), 1)
                lines.append(jnp.where(column == 1, loss_ref[0:1, 0:1], 0.0))
                lines.append(jnp.zeros((3, D), jnp.float32))
                pack = jnp.concatenate(lines, axis=0)
                vector.start(pack)
            push_partner(low_ref, low_out, index, sends, lands).start()

    @pl.when(step >= chunks)
    def _():
        tile = step - chunks
        half, piece_index = lax.rem(tile, 2), lax.div(tile, 2)
        start = pl.multiple_of((half * tail + piece_index) * columns, columns)
        grad = dot_nn(turned_ref[...], dproj_ref[:, pl.ds(start, columns)]).astype(jnp.bfloat16)
        start = pl.multiple_of(piece_index * columns, columns)
        grad_ref[half, :, :, :, :, pl.ds(start, columns)] = grad.reshape(
            grad_ref.shape[1:5] + (columns,)
        )

    for index, part in enumerate(last):

        @pl.when(step == chunks + 2 * index + 1)
        def _():
            part.start()

    @pl.when(step == pl.num_programs(0) - 1)
    def _():
        plan.finish()
        total_ref[...] = vector.finish()
        squares = jnp.sum(square_ref[...]) + jnp.sum(done_ref[...] * done_ref[...])
        norm_ref[...] = norm.total(jnp.full(norm_ref.shape, squares))
        for each in late + last + [vector, norm]:
            each.drain()
        for index in range(chunks):
            push_partner(low_ref, low_out, index, sends, lands).wait()


def adam(weight, moment, square, average, gradient, rate, scalars):
    factor, first_fix, second_fix = scalars
    clipped = gradient * factor
    first = first_decay * moment + (1.0 - first_decay) * clipped
    second = second_decay * square + (1.0 - second_decay) * clipped * clipped
    master = weight - rate * (
        first / first_fix / (jnp.sqrt(second / second_fix) + adam_eps) + decay_weight * weight
    )
    smooth = smooth_decay * average + (1.0 - smooth_decay) * master
    return master, first, second, smooth


def finish_kernel(chunk, chunks, rates, passages, halves, *refs):
    out_own, out_head, out_tail, dx_own, dx_other = refs[:5]
    large, grads = refs[5:21], refs[21:25]
    scales_refs, offsets_refs, total_ref, norm_ref, step_ref = refs[25:29], refs[29:33], *refs[33:36]
    short_out, long_out, short_dx, long_dx = refs[36:40]
    large_outs, scales_outs, offsets_outs, figures_ref = refs[40:56], refs[56:60], refs[60:64], refs[64]
    scratch = refs[65:]
    ins, outs = scratch[:16], scratch[16:32]
    rows_ref, own_ref, low_ref, wide_ref, in_sems, out_sems, block_sems, wide_sems, load_sems = scratch[32:]
    place = lax.axis_index("tensor")
    longs = chunks - 1

    def rows(first, count):
        return pl.ds(pl.multiple_of(first * chunk, chunk), count * chunk)

    ahead = out_head.shape[0] // chunk
    other = 1 - place
    brought = [
        pltpu.make_async_copy(source, target, load_sems.at[k])
        for k, (source, target) in enumerate(
            (
                (dx_other, low_ref),
                (out_own, rows_ref.at[rows(0, chunks)]),
                (out_head, rows_ref.at[rows(chunks, ahead)]),
                (out_tail, rows_ref.at[rows(chunks + ahead, chunks - ahead)]),
                (dx_own, own_ref),
            )
        )
    ]
    for load in brought:
        load.start()
    loads = [pltpu.make_async_copy(large[k], ins[k], in_sems.at[k]) for k in range(16)]
    for load in loads:
        load.start()
    blocks = [
        (rows_ref.at[rows(0, 1)], short_out.at[rows(place, 1)]),
        (rows_ref.at[rows(1, longs)], long_out.at[rows(place * longs, longs)]),
        (rows_ref.at[rows(chunks, 1)], short_out.at[rows(other, 1)]),
        (rows_ref.at[rows(chunks + 1, longs)], long_out.at[rows(other * longs, longs)]),
        (own_ref.at[rows(0, 1)], short_dx.at[rows(place, 1)]),
        (own_ref.at[rows(1, longs)], long_dx.at[rows(place * longs, longs)]),
    ]
    copies = [
        pltpu.make_async_copy(source, target, block_sems.at[k])
        for k, (source, target) in enumerate(blocks)
    ]
    brought[0].wait()
    for index in range(chunks):
        wide_ref[index] = low_ref[rows(index, 1), :].astype(jnp.float32)
        target = short_dx.at[rows(other, 1)]
        if index > 0:
            target = long_dx.at[rows(other * longs + index - 1, 1)]
        copy = pltpu.make_async_copy(wide_ref.at[index], target, wide_sems.at[index])
        copy.start()
        copies.append(copy)
    for load in brought[1:]:
        load.wait()
    for copy in copies[:6]:
        copy.start()

    sums = total_ref[...]
    row = lax.broadcasted_iota(jnp.int32, sums.shape, 0)
    column = lax.broadcasted_iota(jnp.int32, sums.shape, 1)

    def whole_sum(value):
        return jnp.sum(jnp.sum(value, axis=1, keepdims=True), axis=0, keepdims=True)

    squares = norm_ref[0:1, 0:1] + whole_sum(jnp.where(row < 12, sums * sums, 0.0))
    loss = whole_sum(jnp.where(jnp.logical_and(row == 12, column == 1), sums, 0.0))
    norm = jnp.sqrt(squares)
    factor = clip_limit / jnp.maximum(norm, clip_limit)
    steps = jnp.full((1, 1), step_ref[0], jnp.int32).astype(jnp.float32)
    first_fix = 1.0 - jnp.exp(steps * math.log(first_decay))
    second_fix = 1.0 - jnp.exp(steps * math.log(second_decay))
    scalars = (factor, first_fix, second_fix)
    figure = lax.broadcasted_iota(jnp.int32, figures_ref.shape, 0)
    figures_ref[...] = jnp.where(figure == 0, norm, loss / (halves * passages))
    for each in range(4):
        values = []
        for k in range(4 * each, 4 * each + 4):
            loads[k].wait()
            values.append(ins[k][...])
        gradient = grads[each][...]
        if values[0].ndim == 3:
            width = values[0].shape[2]
            gradient = jnp.stack([gradient[:, k * width : (k + 1) * width] for k in range(3)])
        fixed = [one.reshape((1,) * values[0].ndim) for one in scalars]
        new = adam(*values, gradient, rates[each], fixed)
        for part in range(4):
            k = 4 * each + part
            outs[k][...] = new[part]
            copy = pltpu.make_async_copy(outs[k], large_outs[k], out_sems.at[k])
            copy.start()
            copies.append(copy)
    new = adam(*(ref[...] for ref in scales_refs), sums[:6], rates[4], scalars)
    for ref, value in zip(scales_outs, new):
        ref[...] = value
    mine = jnp.where(place == 0, sums[6:9], sums[9:12])
    width = offsets_refs[0].shape[1]
    mine = jnp.concatenate(
        [mine[r : r + 1, c : c + width] for r in range(3) for c in range(0, D, width)], axis=0
    )
    new = adam(*(ref[...] for ref in offsets_refs), mine, rates[5], scalars)
    for ref, value in zip(offsets_outs, new):
        ref[...] = value
    for copy in copies:
        copy.wait()


def finish(chunk, halves_of_rows, large, grads, scales, offsets, total, norm, step_count, passages):
    chunks = halves_of_rows[0].shape[0] // chunk
    halves = lax.axis_size("tensor")
    anywhere = pl.BlockSpec(memory_space=pl.ANY)
    vmem = pl.BlockSpec(memory_space=pltpu.VMEM)
    smem = pl.BlockSpec(memory_space=pltpu.SMEM)
    f32, bf16 = jnp.float32, jnp.bfloat16
    rates = (1.0 / math.sqrt(D), 8.0 / math.sqrt(D), 1.0 / math.sqrt(D), 1.0 / math.sqrt(FF), 0.3, 0.3)
    offsets = [each.reshape(-1, 128) for each in offsets]
    shaped = [jax.ShapeDtypeStruct(each.shape, f32) for each in (*large, *scales, *offsets)]
    both = [
        jax.ShapeDtypeStruct((halves * count * chunk, D), dtype)
        for dtype in (bf16, f32)
        for count in (1, chunks - 1)
    ]
    outs = pl.pallas_call(
        functools.partial(finish_kernel, chunk, chunks, rates, passages, halves),
        in_specs=[anywhere] * 21 + [vmem] * 14 + [smem],
        out_specs=[anywhere] * 20 + [vmem] * 9,
        out_shape=both + shaped + [jax.ShapeDtypeStruct((8, 128), f32)],
        scratch_shapes=[pltpu.VMEM(each.shape, f32) for each in large] * 2
        + [
            pltpu.VMEM((halves * chunks * chunk, D), bf16),
            pltpu.VMEM((chunks * chunk, D), f32),
            pltpu.VMEM((chunks * chunk, D), bf16),
            pltpu.VMEM((chunks, chunk, D), f32),
            pltpu.SemaphoreType.DMA((16,)),
            pltpu.SemaphoreType.DMA((16,)),
            pltpu.SemaphoreType.DMA((6,)),
            pltpu.SemaphoreType.DMA((chunks,)),
            pltpu.SemaphoreType.DMA((5,)),
        ],
        compiler_params=pltpu.CompilerParams(vmem_limit_bytes=big_vmem),
        name="finish",
    )(*halves_of_rows, *large, *grads, *scales, *offsets, total, norm, step_count)
    return outs[:4], outs[4:20], outs[20:24], [each.reshape(-1) for each in outs[24:28]], outs[28]


def row_spec(rows, columns):
    return pl.BlockSpec((rows, columns), lambda i: (i, 0))


def full_spec(shape):
    return pl.BlockSpec(shape, lambda i: (0,) * len(shape), pipeline_mode=pl.Buffered(1))


def shards(
    short_tokens,
    long_tokens,
    short_cotangent,
    long_cotangent,
    short_lengths,
    long_lengths,
    queries,
    positives,
    step_count,
    mixing_weight,
    mixing_moment,
    mixing_square,
    mixing_average,
    merging_weight,
    merging_moment,
    merging_square,
    merging_average,
    expand_weight,
    expand_moment,
    expand_square,
    expand_average,
    shrink_weight,
    shrink_moment,
    shrink_square,
    shrink_average,
    scales_weight,
    scales_moment,
    scales_square,
    scales_average,
    offsets_weight,
    offsets_moment,
    offsets_square,
    offsets_average,
):
    halves = lax.axis_size("tensor")
    place = lax.axis_index("tensor")
    short_span = short_tokens.shape[1]
    long_span = long_tokens.shape[1]
    shorts = short_tokens.shape[0] // halves
    longs = long_tokens.shape[0] // halves
    chunk = long_span
    piece = short_span
    assert shorts * short_span == chunk and shorts == longs
    chunks = longs + 1
    rows = chunks * chunk
    width = mixing_weight.shape[2]
    wide = expand_weight.shape[1]

    def own_half(short_all, long_all):
        return jnp.concatenate(
            [
                lax.dynamic_slice_in_dim(short_all, place * shorts, shorts).reshape(-1, D),
                lax.dynamic_slice_in_dim(long_all, place * longs, longs).reshape(-1, D),
            ],
            axis=0,
        )

    fast = lax.axis_size("dp") == 16 and halves == 2
    mixing_own = mixing_weight.astype(jnp.bfloat16).reshape(-1, 3 * width)
    middle_own = jnp.concatenate([merging_weight.T, expand_weight], axis=1).astype(jnp.bfloat16)
    shrink_own = shrink_weight.T.astype(jnp.bfloat16)
    short_limits = lax.dynamic_slice_in_dim(short_lengths, place * shorts, shorts)
    long_limits = lax.dynamic_slice_in_dim(long_lengths, place * longs, longs)
    spans = jnp.concatenate(
        [
            short_limits[None, :],
            long_limits[:, None] - piece * jnp.arange(chunk // piece, dtype=jnp.int32)[None, :],
        ],
        axis=0,
    )
    inputs = own_half(short_tokens, long_tokens)
    cotangent = own_half(short_cotangent, long_cotangent)
    bf16, f32 = jnp.bfloat16, jnp.float32

    def shaped(columns, dtype):
        return jax.ShapeDtypeStruct((rows, columns), dtype)

    smem = pl.BlockSpec(memory_space=pltpu.SMEM)
    params = pltpu.CompilerParams(vmem_limit_bytes=big_vmem)
    mixing_columns = halves * 3 * width
    scores_flops = 2 * rows * chunk * PAIR * (halves * width // HEAD_DIM)
    if fast:
        (qkv, context), feed, (mixing_full, middle_full, shrink_full) = forward_gather(
            piece,
            spans,
            inputs,
            (mixing_own, middle_own, shrink_own),
            offsets_weight,
            scales_weight,
            chunk,
        )
    else:
        mixing_full, middle_full, shrink_full = (
            gathered(own) for own in (mixing_own, middle_own, shrink_own)
        )
        offsets_other = tensor_swap(offsets_weight)
        offsets_both = jnp.where(
            place == 0,
            jnp.stack([offsets_weight, offsets_other]),
            jnp.stack([offsets_other, offsets_weight]),
        )
        mixing_bias = jnp.concatenate(
            [
                offsets_both[:, :width],
                jnp.zeros((halves, width), jnp.float32),
                offsets_both[:, width : 2 * width],
            ],
            axis=1,
        ).reshape(1, -1)
        qkv, context = pl.pallas_call(
            functools.partial(attend_forward_kernel, piece),
            grid=(chunks,),
            in_specs=[
                smem,
                row_spec(chunk, D),
                full_spec(mixing_full.shape),
                full_spec(mixing_bias.shape),
            ],
            out_specs=[row_spec(chunk, mixing_columns), row_spec(chunk, D)],
            out_shape=[shaped(mixing_columns, bf16), shaped(D, bf16)],
            compiler_params=params,
            cost_estimate=pl.CostEstimate(
                flops=2 * rows * D * mixing_columns + 6 * scores_flops,
                bytes_accessed=16 * 1024 * 1024,
                transcendentals=rows * chunk * 12,
            ),
            name="attend_forward",
        )(spans, inputs, mixing_full, mixing_bias)
        upward_bias = offsets_both[:, 2 * width :].reshape(1, -1)
        feed_ins = [context, inputs, middle_full, shrink_full, scales_weight, upward_bias]
        feed_in_specs = [
            row_spec(chunk, D),
            row_spec(chunk, D),
            full_spec(middle_full.shape),
            full_spec(shrink_full.shape),
            full_spec(scales_weight.shape),
            full_spec(upward_bias.shape),
        ]
        feed_out_specs = [
            row_spec(chunk, D),
            row_spec(chunk, FF),
            row_spec(chunk, FF),
            row_spec(chunk, D),
            row_spec(chunk, 1),
            row_spec(chunk, D),
            row_spec(chunk, D),
            row_spec(chunk, 1),
            pl.BlockSpec((1, 8, D), lambda i: (i, 0, 0)),
        ]
        feed_outs = [
            shaped(D, bf16),
            shaped(FF, bf16),
            shaped(FF, bf16),
            shaped(D, f32),
            shaped(1, f32),
            shaped(D, bf16),
            shaped(D, f32),
            shaped(1, f32),
            jax.ShapeDtypeStruct((chunks, 8, D), f32),
        ]
        feed_cost = pl.CostEstimate(
            flops=2 * rows * D * (D + 2 * FF),
            bytes_accessed=48 * 1024 * 1024,
            transcendentals=2 * rows * FF,
        )
        feed = pl.pallas_call(
            functools.partial(feed_forward_kernel, piece),
            grid=(chunks,),
            in_specs=feed_in_specs,
            out_specs=feed_out_specs,
            out_shape=feed_outs,
            compiler_params=params,
            cost_estimate=feed_cost,
            name="feed_forward",
        )(*feed_ins)
    anywhere = pl.BlockSpec(memory_space=pl.ANY)
    (
        hidden_low,
        activated,
        slope,
        normed_first,
        rstd_first,
        output,
        normed_second,
        rstd_second,
        leading,
    ) = feed
    query_gradient, lead_rows, loss_rows = contrast(leading, queries, positives)
    ahead = 2
    if fast:
        output_head = lax.optimization_barrier((output[: ahead * chunk], lead_rows))[0]
        output_head = tensor_swap(output_head)
    tile = 512
    per = wide // tile

    def chunk_spec(columns):
        return pl.BlockSpec((chunk, columns), lambda i: (jnp.minimum(i, chunks - 1), 0))

    second_back, second_grad, shrink_grad = pl.pallas_call(
        functools.partial(out_back_kernel, piece, chunks),
        grid=(chunks + FF // tile,),
        in_specs=[
            chunk_spec(D),
            pl.BlockSpec((1, 8, D), lambda i: (jnp.minimum(i, chunks - 1), 0, 0)),
            chunk_spec(D),
            chunk_spec(1),
            full_spec(scales_weight.shape),
            pl.BlockSpec((rows, tile), lambda i: (0, jnp.maximum(i - chunks, 0))),
        ],
        out_specs=[
            chunk_spec(D),
            pl.BlockSpec((8, D), lambda i: (0, 0)),
            pl.BlockSpec(
                (1, D, tile),
                lambda i: (jnp.maximum(i - chunks, 0) // per, 0, jnp.maximum(i - chunks, 0) % per),
            ),
        ],
        out_shape=[
            shaped(D, f32),
            jax.ShapeDtypeStruct((8, D), f32),
            jax.ShapeDtypeStruct((halves, D, wide), bf16),
        ],
        scratch_shapes=[pltpu.VMEM((D, rows), bf16)],
        compiler_params=params,
        cost_estimate=pl.CostEstimate(
            flops=2 * rows * D * FF, bytes_accessed=32 * 1024 * 1024, transcendentals=0
        ),
        name="out_back",
    )(cotangent, lead_rows, normed_second, rstd_second, scales_weight, activated)
    back_ins = [
        second_back,
        normed_first,
        rstd_first,
        slope,
        hidden_low,
        context,
        middle_full,
        shrink_full,
        scales_weight,
    ]
    merging_tiles = D // width
    back_steps = chunks + merging_tiles + FF // tile

    def merging_at(i):
        return jnp.clip(i - chunks, 0, merging_tiles - 1)

    def expand_at(i):
        return jnp.maximum(i - chunks - merging_tiles, 0)

    back_in_specs = [
        chunk_spec(D),
        chunk_spec(D),
        chunk_spec(1),
        chunk_spec(FF),
        chunk_spec(D),
        pl.BlockSpec((rows, width), lambda i: (0, merging_at(i))),
        full_spec(middle_full.shape),
        full_spec(shrink_full.shape),
        full_spec(scales_weight.shape),
    ]
    back_out_specs = [
        chunk_spec(D),
        chunk_spec(D),
        pl.BlockSpec((8, D), lambda i: (0, 0)),
        pl.BlockSpec((8, FF), lambda i: (0, 0)),
        pl.BlockSpec((1, D, width), lambda i: (merging_at(i), 0, 0)),
        pl.BlockSpec((1, D, tile), lambda i: (expand_at(i) // per, 0, expand_at(i) % per)),
    ]
    back_outs = [
        shaped(D, f32),
        shaped(D, bf16),
        jax.ShapeDtypeStruct((8, D), f32),
        jax.ShapeDtypeStruct((8, FF), f32),
        jax.ShapeDtypeStruct((halves, D, width), bf16),
        jax.ShapeDtypeStruct((halves, D, wide), bf16),
    ]
    back_scratch = [
        pltpu.VMEM((rows, FF), bf16),
        pltpu.VMEM((D, rows), bf16),
        pltpu.VMEM((D, rows), bf16),
    ]
    back_cost = pl.CostEstimate(
        flops=2 * rows * D * (2 * D + 3 * FF), bytes_accessed=48 * 1024 * 1024, transcendentals=0
    )
    if fast:
        shrink_grad, output_head = lax.optimization_barrier((shrink_grad, output_head))
        tail = output.reshape(chunks, chunk, D)
        *back, output_tail, shrink_sum = pl.pallas_call(
            functools.partial(feed_back_scatter_kernel, chunks, chunks - ahead, width),
            grid=(back_steps,),
            in_specs=[anywhere, full_spec(tail.shape)] + back_in_specs,
            out_specs=back_out_specs + [anywhere, full_spec(scatter_shape(shrink_grad).shape)],
            out_shape=back_outs
            + [jax.ShapeDtypeStruct((chunks - ahead, chunk, D), bf16), scatter_shape(shrink_grad)],
            scratch_shapes=back_scratch
            + scatter_buffers(shrink_grad, width, True) * (wide // width)
            + scatter_sems(wide // width)
            + [pltpu.SemaphoreType.DMA((chunks - ahead,))] * 2,
            compiler_params=pltpu.CompilerParams(
                collective_id=5, has_side_effects=True, vmem_limit_bytes=big_vmem
            ),
            cost_estimate=back_cost,
            name="feed_back_scatter",
        )(scatter_input(shrink_grad), tail, *back_ins)
    else:
        back = pl.pallas_call(
            functools.partial(feed_back_kernel, chunks),
            grid=(back_steps,),
            in_specs=back_in_specs,
            out_specs=back_out_specs,
            out_shape=back_outs,
            scratch_shapes=back_scratch,
            compiler_params=params,
            cost_estimate=back_cost,
            name="feed_back",
        )(*back_ins)
        shrink_sum = scattered(shrink_grad)
        output_head = tensor_swap(output[: ahead * chunk])
        output_tail = tensor_swap(output[ahead * chunk :])
    first_back, context_back, first_grad, upward_grad, merging_grad, expand_grad = back
    pair_ins = [qkv, context_back, first_back, mixing_full]
    pair_in_specs = [
        chunk_spec(mixing_columns),
        chunk_spec(D),
        chunk_spec(D),
        full_spec(mixing_full.shape),
    ]
    pair_cost = pl.CostEstimate(
        flops=2 * rows * D * mixing_columns + 15 * scores_flops,
        bytes_accessed=24 * 1024 * 1024,
        transcendentals=rows * chunk * 12,
    )
    lane = lax.broadcasted_iota(jnp.int32, (1, D), 1)
    losses = jnp.where(lane == 1, loss_rows[0, 0], 0.0)

    def stacked(bias_both, scalars):
        scalars = jnp.pad(scalars, ((0, 3), (0, 0)))
        offsets_grad = jnp.concatenate([bias_both, upward_grad[0].reshape(halves, wide)], axis=1)
        vectors = [first_grad[:2], second_grad[:2], first_grad[2:3], second_grad[2:3]]
        return jnp.concatenate(vectors + [offsets_grad.reshape(-1, D), scalars], axis=0)

    if fast:
        parts = (expand_grad, merging_grad)
        late_count, last_count = wide // width + 1, 3
        last_whole = jax.ShapeDtypeStruct((halves, D, 3 * width), bf16)
        vector = jax.ShapeDtypeStruct((16, D), f32)
        more = (inputs, shrink_sum, first_grad, second_grad, upward_grad, loss_rows)
        small = (8, 128)
        out_shape = [
            shaped(D, f32),
            jax.ShapeDtypeStruct((chunks, chunk, D), bf16),
            scatter_shape(expand_grad),
            scatter_shape(merging_grad),
            scatter_shape(last_whole),
            jax.ShapeDtypeStruct(vector.shape, f32),
            jax.ShapeDtypeStruct(small, f32),
        ]
        input_back, input_other, expand_sum, merging_sum, mixing_sum, summed, squares_all = (
            pl.pallas_call(
                functools.partial(attend_last_kernel, piece, chunks, width),
                grid=(chunks + 2 * last_count,),
                in_specs=[smem, anywhere, anywhere]
                + pair_in_specs
                + [full_spec(each.shape) for each in more],
                out_specs=[chunk_spec(D), anywhere]
                + [full_spec(each.shape) for each in out_shape[2:]],
                out_shape=out_shape,
                scratch_shapes=[
                    pltpu.VMEM((rows, mixing_columns), bf16),
                    pltpu.VMEM((8, mixing_columns), f32),
                    pltpu.VMEM((D, rows), bf16),
                    pltpu.VMEM((halves, 4, 2, 2, D // 16, 3 * width), bf16),
                    pltpu.VMEM((8, width), f32),
                    pltpu.VMEM((chunks, chunk, D), bf16),
                    pltpu.SemaphoreType.DMA((chunks,)),
                    pltpu.SemaphoreType.DMA((chunks,)),
                ]
                + scatter_buffers(expand_grad, width, True) * late_count
                + scatter_sems(late_count)
                + scatter_buffers(last_whole, width) * last_count
                + scatter_sems(last_count)
                + [
                    pltpu.VMEM((6,) + vector.shape, f32),
                    pltpu.VMEM((4,) + vector.shape, f32),
                    pltpu.SemaphoreType.DMA((6,)),
                    pltpu.SemaphoreType.DMA((6,)),
                    pltpu.VMEM((8,) + small, f32),
                    pltpu.VMEM((4,) + small, f32),
                    pltpu.SemaphoreType.DMA((10,)),
                    pltpu.SemaphoreType.DMA((10,)),
                ],
                compiler_params=pltpu.CompilerParams(
                    collective_id=6, has_side_effects=True, vmem_limit_bytes=big_vmem
                ),
                cost_estimate=pair_cost,
                name="attend_last",
            )(
                spans,
                *(scatter_input(part) for part in parts),
                *pair_ins,
                *more,
            )
        )
    else:
        projected_back, input_back, bias_grad, input_low = pl.pallas_call(
            functools.partial(attend_back_kernel, piece),
            grid=(chunks,),
            in_specs=[smem] + pair_in_specs,
            out_specs=[
                row_spec(chunk, mixing_columns),
                row_spec(chunk, D),
                pl.BlockSpec((8, mixing_columns), lambda i: (0, 0)),
                pl.BlockSpec((1, chunk, D), lambda i: (i, 0, 0)),
            ],
            out_shape=[
                shaped(mixing_columns, bf16),
                shaped(D, f32),
                jax.ShapeDtypeStruct((8, mixing_columns), f32),
                jax.ShapeDtypeStruct((chunks, chunk, D), bf16),
            ],
            compiler_params=params,
            cost_estimate=pair_cost,
            name="attend_back",
        )(spans, *pair_ins)
        expand_sum, merging_sum = scattered(expand_grad), scattered(merging_grad)
        input_other = tensor_swap(input_low)
        mixing_sum = scattered(weight_grad(inputs, projected_back, halves, 384))
        sums = (shrink_sum, expand_sum, merging_sum, mixing_sum)
        squares_part = sum(jnp.sum(each * each) for each in sums)
        bias_both = bias_grad[0].reshape(halves, 3, width)
        bias_both = jnp.concatenate([bias_both[:, 0], bias_both[:, 2]], axis=1)
        summed = all_total(stacked(bias_both, jnp.where(lane == 0, squares_part, losses)))
        squares_all = jnp.full((8, 128), summed[12, 0])
    grads = (mixing_sum, merging_sum, expand_sum, shrink_sum)

    def turn(value):
        return value.transpose(1, 0, 2)

    large = (
        turn(mixing_weight),
        turn(mixing_moment),
        turn(mixing_square),
        turn(mixing_average),
        merging_weight.T,
        merging_moment.T,
        merging_square.T,
        merging_average.T,
        expand_weight,
        expand_moment,
        expand_square,
        expand_average,
        shrink_weight.T,
        shrink_moment.T,
        shrink_square.T,
        shrink_average.T,
    )
    both, large_new, scales_new, offsets_new, figures = finish(
        chunk,
        (output, output_head, output_tail.reshape(-1, D), input_back, input_other.reshape(rows, D)),
        large,
        grads,
        (scales_weight, scales_moment, scales_square, scales_average),
        (offsets_weight, offsets_moment, offsets_square, offsets_average),
        summed,
        squares_all,
        step_count,
        queries.shape[0] * lax.axis_size("dp"),
    )
    return (
        (
            both[0].reshape(short_tokens.shape),
            both[1].reshape(long_tokens.shape),
            both[2].reshape(short_tokens.shape),
            both[3].reshape(long_tokens.shape),
            query_gradient,
            figures[1, :1],
            figures[0, :1],
        )
        + tuple(turn(each) for each in large_new[:4])
        + tuple(each.T for each in large_new[4:8])
        + tuple(large_new[8:12])
        + tuple(each.T for each in large_new[12:])
        + tuple(scales_new)
        + tuple(offsets_new)
    )


def solution(mesh):
    placed = (
        P("dp", None, None),
        P("dp", None, None),
        P("dp", None, None),
        P("dp", None, None),
        P("dp"),
        P("dp"),
        P("dp", None),
        P("dp"),
        P(),
        P("dp", None, "tensor"),
        P("dp", None, "tensor"),
        P("dp", None, "tensor"),
        P("dp", None, "tensor"),
        P("tensor", "dp"),
        P("tensor", "dp"),
        P("tensor", "dp"),
        P("tensor", "dp"),
        P("dp", "tensor"),
        P("dp", "tensor"),
        P("dp", "tensor"),
        P("dp", "tensor"),
        P("tensor", "dp"),
        P("tensor", "dp"),
        P("tensor", "dp"),
        P("tensor", "dp"),
        P(),
        P(),
        P(),
        P(),
        P("tensor"),
        P("tensor"),
        P("tensor"),
        P("tensor"),
    )
    return jax.shard_map(
        shards,
        mesh=mesh,
        in_specs=placed,
        out_specs=(
            P("dp", None, None),
            P("dp", None, None),
            P("dp", None, None),
            P("dp", None, None),
            P("dp", None),
            P(),
            P(),
            P("dp", None, "tensor"),
            P("dp", None, "tensor"),
            P("dp", None, "tensor"),
            P("dp", None, "tensor"),
            P("tensor", "dp"),
            P("tensor", "dp"),
            P("tensor", "dp"),
            P("tensor", "dp"),
            P("dp", "tensor"),
            P("dp", "tensor"),
            P("dp", "tensor"),
            P("dp", "tensor"),
            P("tensor", "dp"),
            P("tensor", "dp"),
            P("tensor", "dp"),
            P("tensor", "dp"),
            P(),
            P(),
            P(),
            P(),
            P("tensor"),
            P("tensor"),
            P("tensor"),
            P("tensor"),
        ),
        check_vma=False,
    )
```

```python
import functools
import math

import jax
import jax.numpy as jnp
from jax import lax
from jax.experimental import pallas as pl
from jax.experimental.pallas import tpu as pltpu
from jax.sharding import PartitionSpec as P

D = 768
FF = 3072
HEAD_DIM = 64
PAIR = 2 * HEAD_DIM
MESH = pl.DeviceIdType.MESH

norm_eps = 1e-05
score_scale = 0.125
masked_value = -1e30
first_decay = 0.5
second_decay = 0.75
smooth_decay = 0.75
decay_weight = 0.01
adam_eps = 1e-08
clip_limit = 1.0
inverse_root_two = 0.7071067811865476
inverse_root_tau = 0.3989422804014327
big_vmem = 56 * 1024 * 1024


def dot_nn(a, b):
    return lax.dot_general(a, b, (((1,), (0,)), ((), ())), preferred_element_type=jnp.float32)


def dot_nt(a, b):
    return lax.dot_general(a, b, (((1,), (1,)), ((), ())), preferred_element_type=jnp.float32)


def dot_tn(a, b):
    return lax.dot_general(a, b, (((0,), (0,)), ((), ())), preferred_element_type=jnp.float32)


def layer_stats(resid):
    centre = resid - jnp.mean(resid, axis=-1, keepdims=True)
    rstd = lax.rsqrt(jnp.mean(centre * centre, axis=-1, keepdims=True) + norm_eps)
    return (centre * rstd, rstd)


def layer_back(gradient, normed, rstd, gain):
    scaled = gradient * gain
    return rstd * (
        scaled
        - jnp.mean(scaled, axis=-1, keepdims=True)
        - normed * jnp.mean(scaled * normed, axis=-1, keepdims=True)
    )


def visible_keys(spans, step, rows, piece, key_axis):
    shape = (rows, 1) if key_axis == 0 else (1, rows)
    place = lax.broadcasted_iota(jnp.int32, shape, key_axis)
    segment = place // piece
    limit = jnp.zeros(shape, jnp.int32)
    for index in range(rows // piece):
        limit = jnp.where(segment == index, spans[step, index], limit)
    key_valid = (place % piece) < limit
    first = lax.broadcasted_iota(jnp.int32, (rows, rows), 0) // piece
    second = lax.broadcasted_iota(jnp.int32, (rows, rows), 1) // piece
    return jnp.logical_and(jnp.logical_or(first == second, step > 0), key_valid)


def own_lanes(value, which):
    lane = lax.broadcasted_iota(jnp.int32, value.shape, 1)
    return jnp.where((lane // HEAD_DIM) == which, value, jnp.zeros_like(value))


def join_lanes(low, high):
    lane = lax.broadcasted_iota(jnp.int32, low.shape, 1)
    return jnp.where(lane < HEAD_DIM, low, high)


def attend_half(half, weight, bias, visible, x, qkv_ref, ctx_ref):
    width = weight.shape[1] // 3
    base = half * 3 * width
    projected = dot_nn(x, weight) + bias
    qkv_ref[:, base : base + 3 * width] = projected.astype(jnp.bfloat16)
    for pair in range(width // PAIR):
        at = base + pair * PAIR
        q = qkv_ref[:, at : at + PAIR] * jnp.bfloat16(score_scale)
        k = qkv_ref[:, at + width : at + width + PAIR]
        v = qkv_ref[:, at + 2 * width : at + 2 * width + PAIR]
        parts = []
        for which in range(2):
            scores = jnp.where(visible, dot_nt(own_lanes(q, which), k), masked_value)
            powered = jnp.exp(scores - jnp.max(scores, axis=-1, keepdims=True))
            weights = powered * (1.0 / jnp.sum(powered, axis=-1, keepdims=True))
            parts.append(dot_nn(weights.astype(jnp.bfloat16), v))
        at = half * width + pair * PAIR
        ctx_ref[:, at : at + PAIR] = join_lanes(*parts).astype(jnp.bfloat16)


def attend_forward_kernel(piece, spans, x_ref, w_ref, bias_ref, qkv_ref, ctx_ref):
    step = pl.program_id(0)
    rows = x_ref.shape[0]
    width = w_ref.shape[2] // 3
    visible = visible_keys(spans, step, rows, piece, 1)
    for half in range(w_ref.shape[0]):
        bias = bias_ref[:, half * 3 * width : (half + 1) * 3 * width]
        attend_half(half, w_ref[half], bias, visible, x_ref[...], qkv_ref, ctx_ref)


def feed_up(context, inputs, me_ref, scales_ref, bu_ref, outs):
    hb_ref, g_ref, slope_ref, n1_ref, r1_ref = outs
    wide = bu_ref.shape[1] // 2
    width = me_ref.shape[-1] - wide
    attention = scales_ref[4:5, :]

    def weight(half, columns):
        place = (half,) + (slice(None),) * (len(me_ref.shape) - 2) + (columns,)
        return me_ref[place].reshape(D, -1)

    for half in range(2):
        attention = attention + dot_nt(
            context[:, half * width : (half + 1) * width], weight(half, slice(0, width))
        )
    normed, rstd = layer_stats(inputs.astype(jnp.float32) + attention)
    n1_ref[...] = normed
    r1_ref[...] = rstd
    hidden = normed * scales_ref[0:1, :] + scales_ref[1:2, :]
    hidden_low = hidden.astype(jnp.bfloat16)
    hb_ref[...] = hidden_low
    activated = []
    for half in range(2):
        at = half * wide
        upward = dot_nn(hidden_low, weight(half, slice(width, width + wide))) + bu_ref[:, at : at + wide]
        cumulative = 0.5 * (1.0 + lax.erf(upward * inverse_root_two))
        density = jnp.exp(-0.5 * upward * upward) * inverse_root_tau
        activated.append((upward * cumulative).astype(jnp.bfloat16))
        g_ref[:, at : at + wide] = activated[half]
        slope_ref[:, at : at + wide] = (cumulative + upward * density).astype(jnp.bfloat16)
    return hidden, activated


def feed_down(piece, hidden, activated, st_ref, scales_ref, outs):
    out_ref, n2_ref, r2_ref, lead_ref = outs
    downward = scales_ref[5:6, :]
    for half in range(2):
        wide = st_ref.shape[-1]
        downward = downward + dot_nt(activated[half], st_ref[half].reshape(D, wide))
    normed, rstd = layer_stats(hidden + downward)
    n2_ref[...] = normed
    r2_ref[...] = rstd
    result = (normed * scales_ref[2:3, :] + scales_ref[3:4, :]).astype(jnp.bfloat16)
    out_ref[...] = result
    for index in range(result.shape[0] // piece):
        row = result[index * piece : index * piece + 8].astype(jnp.float32)
        lead_ref[0, index : index + 1, :] = row[:1]


def feed_forward_kernel(
    piece, ctx_ref, x_ref, me_ref, st_ref, scales_ref, bu_ref,
    hb_ref, g_ref, slope_ref, n1_ref, r1_ref, out_ref, n2_ref, r2_ref, lead_ref,
):
    hidden, activated = feed_up(
        ctx_ref[...], x_ref[...], me_ref, scales_ref, bu_ref, (hb_ref, g_ref, slope_ref, n1_ref, r1_ref)
    )
    feed_down(piece, hidden, activated, st_ref, scales_ref, (out_ref, n2_ref, r2_ref, lead_ref))


def add_row(ref, index, value):
    ref[index : index + 1, :] += jnp.sum(value, axis=0, keepdims=True)


def out_back_kernel(
    piece, chunks, short_ref, long_ref, lead_ref, n2_ref, r2_ref, scales_ref, g_ref, dr2_ref, vec_ref, grad_ref, turned_ref
):
    step = pl.program_id(0)

    @pl.when(step == 0)
    def _():
        vec_ref[...] = jnp.zeros_like(vec_ref)

    @pl.when(step < chunks)
    def _():
        dout = jnp.where(step == 0, short_ref[...], long_ref[...]).astype(jnp.float32)
        rows = dout.shape[0]
        row = lax.broadcasted_iota(jnp.int32, dout.shape, 0)
        for index in range(rows // piece):
            dout = dout + jnp.where(row == index * piece, lead_ref[0, index : index + 1, :], 0.0)
        normed = n2_ref[...]
        add_row(vec_ref, 0, dout * normed)
        add_row(vec_ref, 1, dout)
        second = layer_back(dout, normed, r2_ref[...], scales_ref[2:3, :])
        add_row(vec_ref, 2, second)
        dr2_ref[...] = second
        turned_ref[:, pl.ds(pl.multiple_of(step * rows, rows), rows)] = second.astype(jnp.bfloat16).T

    @pl.when(step >= chunks)
    def _():
        grad_ref[0] = dot_nn(turned_ref[...], g_ref[...]).astype(jnp.bfloat16)


def no_progress(point):
    pass


def feed_back_kernel(
    chunks, dr2_ref, n1_ref, r1_ref, slope_ref, hb_ref, ctx_ref, me_ref, st_ref, scales_ref,
    dr1_ref, dctx_ref, vec_ref, up_ref, merging_ref, expand_ref,
    dub_ref, turned_h, turned_a, progress=no_progress,
):
    step = pl.program_id(0)
    rows = dr2_ref.shape[0]
    wide = st_ref.shape[2]
    width = me_ref.shape[2] - wide
    tiles = ctx_ref.shape[1]
    tile = expand_ref.shape[2]
    merging_steps = D // tiles

    @pl.when(step == 0)
    def _():
        vec_ref[...] = jnp.zeros_like(vec_ref)
        up_ref[...] = jnp.zeros_like(up_ref)

    progress(0)

    @pl.when(step < chunks)
    def _():
        place = pl.ds(pl.multiple_of(step * rows, rows), rows)
        hidden_back = dr2_ref[...]
        low = hidden_back.astype(jnp.bfloat16)
        turned_h[:, place] = hb_ref[...].T
        for half in range(st_ref.shape[0]):
            at = half * wide
            upward = dot_nn(low, st_ref[half]) * slope_ref[:, at : at + wide].astype(jnp.float32)
            up_ref[0:1, at : at + wide] += jnp.sum(upward, axis=0, keepdims=True)
            upward_low = upward.astype(jnp.bfloat16)
            dub_ref[place, at : at + wide] = upward_low
            hidden_back = hidden_back + dot_nt(upward_low, me_ref[half, :, width:])
            progress(1 + half)
        normed = n1_ref[...]
        add_row(vec_ref, 0, hidden_back * normed)
        add_row(vec_ref, 1, hidden_back)
        first = layer_back(hidden_back, normed, r1_ref[...], scales_ref[0:1, :])
        add_row(vec_ref, 2, first)
        dr1_ref[...] = first
        low = first.astype(jnp.bfloat16)
        turned_a[:, place] = low.T
        for half in range(me_ref.shape[0]):
            dctx_ref[:, half * width : (half + 1) * width] = dot_nn(
                low, me_ref[half, :, :width]
            ).astype(jnp.bfloat16)

    @pl.when(jnp.logical_and(step >= chunks, step < chunks + merging_steps))
    def _():
        merging_ref[0] = dot_nn(turned_a[...], ctx_ref[...]).astype(jnp.bfloat16)

    @pl.when(step >= chunks + merging_steps)
    def _():
        start = (step - chunks - merging_steps) * tile
        right = dub_ref[:, pl.ds(pl.multiple_of(start, tile), tile)]
        expand_ref[0] = dot_nn(turned_h[...], right).astype(jnp.bfloat16)


def attend_back_kernel(
    piece, spans, qkv_ref, dctx_ref, dr1_ref, w_ref, dproj_ref, dx_ref, bias_ref, low_ref,
    progress=no_progress,
):
    step = pl.program_id(0)

    @pl.when(step == 0)
    def _():
        bias_ref[...] = jnp.zeros_like(bias_ref)

    rows = qkv_ref.shape[0]
    width = w_ref.shape[2] // 3
    visible = visible_keys(spans, step, rows, piece, 0)
    point = 0
    total = dr1_ref[...]
    for half in range(w_ref.shape[0]):
        base = half * 3 * width
        for pair in range(width // PAIR):
            at = base + pair * PAIR
            q = qkv_ref[:, at : at + PAIR]
            k = qkv_ref[:, at + width : at + width + PAIR]
            v = qkv_ref[:, at + 2 * width : at + 2 * width + PAIR]
            near = half * width + pair * PAIR
            back = dctx_ref[:, near : near + PAIR]
            parts = []
            for which in range(2):
                scores = dot_nt(own_lanes(k, which) * jnp.bfloat16(score_scale), q)
                scores = jnp.where(visible, scores, masked_value)
                powered = jnp.exp(scores - jnp.max(scores, axis=0, keepdims=True))
                weights = powered * (1.0 / jnp.sum(powered, axis=0, keepdims=True))
                weight_back = dot_nt(own_lanes(v, which), back)
                score_back = weights * (
                    weight_back - jnp.sum(weights * weight_back, axis=0, keepdims=True)
                )
                score_low = (score_back * score_scale).astype(jnp.bfloat16)
                parts.append(
                    (
                        dot_tn(score_low, k),
                        dot_nn(score_low, q),
                        dot_nn(weights.astype(jnp.bfloat16), back),
                    )
                )
            for part in range(3):
                value = join_lanes(parts[0][part], parts[1][part])
                spot = at + part * width
                if part != 1:
                    bias_ref[0:1, spot : spot + PAIR] += jnp.sum(value, axis=0, keepdims=True)
                dproj_ref[:, spot : spot + PAIR] = value.astype(jnp.bfloat16)
            point += 1
            progress(point)
        total = total + dot_nt(dproj_ref[:, base : base + 3 * width], w_ref[half])
    dx_ref[...] = total
    low_ref[step if low_ref.shape[0] > 1 else 0] = total.astype(jnp.bfloat16)


def weight_grad_kernel(left_ref, right_ref, out_ref, turned_ref):
    @pl.when(pl.program_id(0) == 0)
    def _():
        turned_ref[...] = left_ref[...].T

    out_ref[0] = dot_nn(turned_ref[...], right_ref[...]).astype(jnp.bfloat16)


def weight_grad(left, right, groups, tile):
    rows, depth = left.shape
    columns = right.shape[1]
    per = columns // groups // tile
    return pl.pallas_call(
        weight_grad_kernel,
        grid=(columns // tile,),
        in_specs=[
            pl.BlockSpec((rows, depth), lambda i: (0, 0), pipeline_mode=pl.Buffered(1)),
            pl.BlockSpec((rows, tile), lambda i: (0, i)),
        ],
        out_specs=pl.BlockSpec((1, depth, tile), lambda i: (i // per, 0, i % per)),
        out_shape=jax.ShapeDtypeStruct((groups, depth, columns // groups), jnp.bfloat16),
        scratch_shapes=[pltpu.VMEM((depth, rows), jnp.bfloat16)],
        compiler_params=pltpu.CompilerParams(vmem_limit_bytes=big_vmem),
        cost_estimate=pl.CostEstimate(
            flops=2 * rows * depth * columns,
            bytes_accessed=2 * (rows * depth + rows * columns + depth * columns),
            transcendentals=0,
        ),
        name="weight_grad",
    )(left, right)


def contrast_kernel(
    count, own, halves, cls_ref, q_ref, pos_ref, qg_ref, lead_ref, loss_ref,
    mine_ref, all_ref, part_ref, got_ref, stat_ref, term_ref,
    sem_a, sem_b, sem_c, sem_d, sem_e, sem_f, sem_g, sem_h,
):
    me = lax.axis_index("dp")
    half = lax.axis_index("tensor")
    other = 1 - half
    kind = own // 2
    firsts = [cls_ref[0, :kind, :]] + [cls_ref[1 + index, :1, :] for index in range(kind)]
    mine_ref[...] = jnp.concatenate(firsts, axis=0).astype(jnp.bfloat16)
    barrier = pltpu.get_barrier_semaphore()

    @pl.loop(1, count)
    def _(gap):
        pl.semaphore_signal(
            barrier, inc=1, device_id=(lax.rem(me + gap, count), half), device_id_type=MESH
        )

    pl.semaphore_signal(barrier, inc=1, device_id=(me, other), device_id_type=MESH)
    pl.semaphore_wait(barrier, count)

    def push(source, target, sends, lands, gap):
        peer = lax.rem(me + gap, count)
        return pltpu.make_async_remote_copy(
            src_ref=source(peer),
            dst_ref=target.at[me],
            send_sem=sends.at[gap],
            recv_sem=lands.at[me],
            device_id=(peer, half),
            device_id_type=MESH,
        )

    def landed(source, target, sends, lands, gap):
        origin = lax.rem(me + count - gap, count)
        return pltpu.make_async_remote_copy(
            src_ref=target.at[origin],
            dst_ref=target.at[origin],
            send_sem=sends.at[gap],
            recv_sem=lands.at[origin],
            device_id=(origin, half),
            device_id_type=MESH,
        )

    def whole(peer):
        return mine_ref

    @pl.loop(1, count)
    def _(gap):
        push(whole, all_ref, sem_a, sem_b, gap).start()

    all_ref[me] = mine_ref[...]

    @pl.loop(1, count)
    def _(gap):
        landed(whole, all_ref, sem_a, sem_b, gap).wait_recv()

    passages = all_ref[...].astype(jnp.float32).reshape(count * own, D).astype(jnp.bfloat16)
    queries = q_ref[...]
    logits = dot_nt(queries, passages)
    column = lax.broadcasted_iota(jnp.int32, logits.shape, 1)
    near = column % own
    index = (column // own) * (own * halves) + (near // kind) * (kind * halves)
    index = index + half * kind + near % kind
    query = lax.broadcasted_iota(jnp.int32, logits.shape, 0)
    positive = jnp.zeros(logits.shape, jnp.int32)
    for each in range(logits.shape[0]):
        positive = jnp.where(query == each, pos_ref[each], positive)
    chosen = jnp.where(index == positive, 1.0, 0.0)
    highest = jnp.max(logits, axis=1, keepdims=True)
    summed = jnp.sum(jnp.exp(logits - highest), axis=1, keepdims=True)
    picked = jnp.sum(logits * chosen, axis=1, keepdims=True)
    lane = lax.broadcasted_iota(jnp.int32, (logits.shape[0], 128), 1)
    stat_ref[half] = jnp.where(lane == 0, highest, jnp.where(lane == 1, summed, picked))

    def swap(ref, send, land):
        return pltpu.make_async_remote_copy(
            src_ref=ref.at[half],
            dst_ref=ref.at[half],
            send_sem=send,
            recv_sem=land,
            device_id=(me, other),
            device_id_type=MESH,
        )

    def swapped(ref, send, land):
        return pltpu.make_async_remote_copy(
            src_ref=ref.at[other],
            dst_ref=ref.at[other],
            send_sem=send,
            recv_sem=land,
            device_id=(me, other),
            device_id_type=MESH,
        )

    swap(stat_ref, sem_e, sem_f).start()
    swapped(stat_ref, sem_e, sem_f).wait_recv()
    low, high = stat_ref[0], stat_ref[1]
    top = jnp.maximum(low[:, 0:1], high[:, 0:1])
    total = low[:, 1:2] * jnp.exp(low[:, 0:1] - top) + high[:, 1:2] * jnp.exp(high[:, 0:1] - top)
    losses = top + jnp.log(total) - (low[:, 2:3] + high[:, 2:3])
    loss_ref[...] = jnp.broadcast_to(jnp.sum(losses, axis=0, keepdims=True), loss_ref.shape)
    logit_back = (jnp.exp(logits - top) / total - chosen).astype(jnp.bfloat16)
    terms = dot_tn(logit_back, queries)
    part_ref[...] = terms.reshape(count, own, D).astype(jnp.bfloat16)

    def piece(peer):
        return part_ref.at[peer]

    @pl.loop(1, count)
    def _(gap):
        push(piece, got_ref, sem_c, sem_d, gap).start()

    term_ref[half] = dot_nn(logit_back, passages)
    swap(term_ref, sem_g, sem_h).start()
    got_ref[me] = part_ref[me]
    swapped(term_ref, sem_g, sem_h).wait_recv()
    qg_ref[...] = term_ref[0] + term_ref[1]

    @pl.loop(1, count)
    def _(gap):
        landed(piece, got_ref, sem_c, sem_d, gap).wait_recv()

    lead = jnp.sum(got_ref[...].astype(jnp.float32), axis=0)
    lead_ref[...] = jnp.zeros_like(lead_ref)
    lead_ref[0, :kind, :] = lead[:kind]
    for index in range(kind):
        lead_ref[1 + index, :1, :] = lead[kind + index : kind + index + 1]

    @pl.loop(1, count)
    def _(gap):
        push(whole, all_ref, sem_a, sem_b, gap).wait_send()
        push(piece, got_ref, sem_c, sem_d, gap).wait_send()

    swap(stat_ref, sem_e, sem_f).wait_send()
    swap(term_ref, sem_g, sem_h).wait_send()


def contrast(leading, queries, positives):
    count = lax.axis_size("dp")
    halves = lax.axis_size("tensor")
    own = 2 * (leading.shape[0] - 1)
    here = queries.shape[0]
    whole = pl.BlockSpec(memory_space=pltpu.VMEM)
    query_gradient, lead_back, loss = pl.pallas_call(
        functools.partial(contrast_kernel, count, own, halves),
        in_specs=[whole] * 2 + [pl.BlockSpec(memory_space=pltpu.SMEM)],
        out_specs=[whole] * 3,
        out_shape=[
            jax.ShapeDtypeStruct((here, D), jnp.float32),
            jax.ShapeDtypeStruct(leading.shape, jnp.float32),
            jax.ShapeDtypeStruct((8, 128), jnp.float32),
        ],
        scratch_shapes=[
            pltpu.VMEM((own, D), jnp.bfloat16),
            pltpu.VMEM((count, own, D), jnp.bfloat16),
            pltpu.VMEM((count, own, D), jnp.bfloat16),
            pltpu.VMEM((count, own, D), jnp.bfloat16),
            pltpu.VMEM((halves, here, 128), jnp.float32),
            pltpu.VMEM((halves, here, D), jnp.float32),
            pltpu.SemaphoreType.DMA((count,)),
            pltpu.SemaphoreType.DMA((count,)),
            pltpu.SemaphoreType.DMA((count,)),
            pltpu.SemaphoreType.DMA((count,)),
            pltpu.SemaphoreType.DMA,
            pltpu.SemaphoreType.DMA,
            pltpu.SemaphoreType.DMA,
            pltpu.SemaphoreType.DMA,
        ],
        compiler_params=pltpu.CompilerParams(
            collective_id=1, has_side_effects=True, vmem_limit_bytes=big_vmem
        ),
        name="contrast",
    )(leading, queries, positives)
    return query_gradient, lead_back, loss


def total_kernel(bits, value_ref, out_ref, slots, send_sem, recv_sem):
    me = lax.axis_index("dp")
    half = lax.axis_index("tensor")

    def partner(stage):
        if stage == bits:
            return (me, 1 - half)
        gap = 1 << stage
        up = 1 - 2 * lax.rem(me // gap, 2)
        return (me + up * gap, half)

    barrier = pltpu.get_barrier_semaphore()
    for stage in range(bits + 1):
        pl.semaphore_signal(barrier, inc=1, device_id=partner(stage), device_id_type=MESH)
    pl.semaphore_wait(barrier, bits + 1)
    out_ref[...] = value_ref[...]
    slots[0] = value_ref[...]
    copies = []
    for stage in range(bits + 1):
        copy = pltpu.make_async_remote_copy(
            src_ref=slots.at[2 * stage],
            dst_ref=slots.at[2 * stage + 1],
            send_sem=send_sem.at[stage],
            recv_sem=recv_sem.at[stage],
            device_id=partner(stage),
            device_id_type=MESH,
        )
        copy.start()
        copies.append(copy)
        copy.wait_recv()
        summed = slots[2 * stage] + slots[2 * stage + 1]
        if stage < bits:
            slots[2 * stage + 2] = summed
        else:
            out_ref[...] = summed
    for copy in copies:
        copy.wait_send()


def all_total(value):
    bits = (lax.axis_size("dp") - 1).bit_length()
    whole = pl.BlockSpec(memory_space=pltpu.VMEM)
    return pl.pallas_call(
        functools.partial(total_kernel, bits),
        in_specs=[whole],
        out_specs=whole,
        out_shape=jax.ShapeDtypeStruct(value.shape, value.dtype),
        scratch_shapes=[
            pltpu.VMEM((2 * bits + 2,) + value.shape, value.dtype),
            pltpu.SemaphoreType.DMA((bits + 1,)),
            pltpu.SemaphoreType.DMA((bits + 1,)),
        ],
        compiler_params=pltpu.CompilerParams(collective_id=2, has_side_effects=True),
        name="all_total",
    )(value)


def tensor_swap(value):
    return lax.ppermute(value, "tensor", [(0, 1), (1, 0)])


def gathered(own):
    return lax.all_gather(own, ("tensor", "dp"), axis=0, tiled=True).reshape(
        lax.axis_size("tensor"), -1, own.shape[1]
    )


def scattered(whole):
    return lax.psum_scatter(
        whole.reshape(-1, whole.shape[2]), ("tensor", "dp"), scatter_dimension=0, tiled=True
    ).astype(jnp.float32)


def grid_place():
    me = lax.axis_index("dp")
    return lax.axis_index("tensor"), me // 4, lax.rem(me // 2, 2), lax.rem(me, 2)


def at_place(t, z, x, c):
    return (z * 4 + x * 2 + c, t)


def greet_neighbours(cube=False):
    t, z, x, c = grid_place()
    barrier = pltpu.get_barrier_semaphore()
    others = [at_place(t, lax.rem(z + gap, 4), x, c) for gap in range(1, 4)]
    others += [at_place(1 - t, z, x, c), at_place(t, z, 1 - x, c), at_place(t, z, x, 1 - c)]
    if cube:
        others += [at_place(1 - t, z, 1 - x, c), at_place(1 - t, z, x, 1 - c)]
        others += [at_place(t, z, 1 - x, 1 - c), at_place(1 - t, z, 1 - x, 1 - c)]
    for other in others:
        pl.semaphore_signal(barrier, inc=1, device_id=other, device_id_type=MESH)
    pl.semaphore_wait(barrier, len(others))


class Gather:
    count = 19

    def __init__(self, own, buffer, sends, lands, local, index):
        self.own, self.buffer, self.index = own, buffer, index
        self.sends, self.lands, self.local = sends, lands, local
        t, z, x, c = self.place = grid_place()
        even = c == 0
        self.mid = (jnp.where(even, t, 1 - t), jnp.where(even, 1 - x, x))
        self.last = (jnp.where(even, 1 - t, t), jnp.where(even, x, 1 - x))
        self.both = (1 - t, 1 - x)

    def group(self, spot, c):
        return self.buffer.at[spot[0], :, spot[1], c]

    def slot(self, spot, gap):
        _, z, _, c = self.place
        return self.buffer.at[spot[0], lax.rem(z + 4 - gap, 4), spot[1], c]

    def copy(self, source, target, which, device):
        return pltpu.make_async_remote_copy(
            src_ref=source,
            dst_ref=target,
            send_sem=self.sends.at[self.index, which],
            recv_sem=self.lands.at[self.index, which],
            device_id=device,
            device_id_type=MESH,
        )

    def outgoing(self, which):
        t, z, x, c = self.place
        here = (t, x)
        middle = at_place(self.mid[0], z, self.mid[1], c)
        last = at_place(self.last[0], z, self.last[1], c)
        if which < 3:
            device = at_place(t, lax.rem(z + which + 1, 4), x, c)
            return self.copy(self.own, self.slot(here, 0), which, device)
        if which < 5:
            return self.copy(self.own, self.slot(here, 0), which, (middle, last)[which - 3])
        if which < 11:
            slot = self.slot(here, (which - 5) % 3 + 1)
            return self.copy(slot, slot, which, middle if which < 8 else last)
        if which < 15:
            slot = self.slot(self.mid, which - 11)
            return self.copy(slot, slot, which, last)
        group = self.group((here, self.mid, self.last, self.both)[which - 15], c)
        return self.copy(group, group, which, at_place(t, z, x, 1 - c))

    def arrived(self, which):
        t, z, x, c = self.place
        if which < 3:
            target = self.slot((t, x), which + 1)
        elif which < 5:
            target = self.slot((self.mid, self.last)[which - 3], 0)
        elif which < 11:
            target = self.slot(self.mid if which < 8 else self.last, (which - 5) % 3 + 1)
        elif which < 15:
            target = self.slot(self.both, which - 11)
        else:
            target = self.group(((t, x), self.last, self.mid, self.both)[which - 15], 1 - c)
        self.copy(target, target, which, at_place(t, z, x, 1 - c)).wait_recv()

    def keep(self):
        t, z, x, c = self.place
        return pltpu.make_async_copy(self.own, self.slot((t, x), 0), self.local.at[self.index])

    def start(self):
        self.keep().start()
        for which in (0, 2, 1, 3, 4):
            self.outgoing(which).start()

    def line_part(self, gap):
        self.arrived(gap)
        self.outgoing(5 + gap).start()
        self.outgoing(8 + gap).start()

    def line_kept(self):
        self.keep().wait()
        self.outgoing(15).start()

    def line_ready(self):
        for gap in (0, 2, 1):
            self.line_part(gap)
        self.line_kept()

    def middle_ready(self):
        self.arrived(3)
        self.outgoing(11).start()
        for gap in (0, 2, 1):
            self.arrived(5 + gap)
            self.outgoing(12 + gap).start()
        self.outgoing(16).start()

    def last_ready(self):
        for which in (4, 8, 10, 9):
            self.arrived(which)
        self.outgoing(17).start()

    def both_ready(self):
        for which in range(11, 15):
            self.arrived(which)
        self.outgoing(18).start()

    def finish(self):
        for which in range(15, 19):
            self.arrived(which)

    def drain(self):
        for which in range(self.count):
            self.outgoing(which).wait_send()


def forward_gather_kernel(
    piece, chunks, spans, mixing_ref, middle_ref, shrink_ref, offsets_ref, scales_ref, short_ref, long_ref,
    qkv_ref, ctx_ref, hb_ref, g_ref, slope_ref, n1_ref, r1_ref, out_ref, n2_ref, r2_ref, lead_ref,
    mixing_out, middle_out, shrink_out,
    w_ref, me_ref, st_ref, both_ref, flat_ref, up_ref, ctx_all, g_all, hidden_all,
    sends, lands, local, swap_send, swap_land, stores,
):
    step = pl.program_id(0)
    t, z, x, c = grid_place()
    mixing, middle, shrink = (
        Gather(own, full, sends, lands, local, index)
        for index, (own, full) in enumerate(
            ((mixing_ref, w_ref), (middle_ref, me_ref), (shrink_ref, st_ref))
        )
    )

    def swap(which):
        return pltpu.make_async_remote_copy(
            src_ref=both_ref.at[which],
            dst_ref=both_ref.at[which],
            send_sem=swap_send,
            recv_sem=swap_land,
            device_id=at_place(1 - t, z, x, c),
            device_id_type=MESH,
        )

    def store(index):
        target = (mixing_out, middle_out, shrink_out)[index]
        return pltpu.make_async_copy((w_ref, me_ref, st_ref)[index], target, stores.at[index])

    rows = long_ref.shape[0]
    width = w_ref.shape[5] // 3

    def tokens(first):
        return jnp.where(step == first, short_ref[...], long_ref[...])


    @pl.when(step == 0)
    def _():
        both_ref[t] = offsets_ref[...]
        greet_neighbours()
        mixing.start()
        swap(t).start()
        middle.start()
        shrink.start()
        mixing.line_ready()
        mixing.middle_ready()
        mixing.last_ready()
        middle.line_part(0)
        mixing.both_ready()
        mixing.finish()
        store(0).start()
        middle.line_part(2)
        middle.line_part(1)
        middle.line_kept()
        swap(1 - t).wait_recv()
        for half in range(2):
            flat_ref[half] = jnp.concatenate(
                [both_ref[half, index : index + 1, :] for index in range(both_ref.shape[1])], axis=1
            )
            wide = up_ref.shape[1] // 2
            up_ref[:, half * wide : (half + 1) * wide] = flat_ref[half][:, 2 * width :]

    @pl.when(step == 2)
    def _():
        middle.middle_ready()

    @pl.when(step == chunks - 1)
    def _():
        shrink.line_ready()
        middle.last_ready()

    @pl.when(step == chunks)
    def _():
        middle.both_ready()
        middle.finish()
        store(1).start()

    @pl.when(step == chunks + 1)
    def _():
        shrink.middle_ready()

    @pl.when(step == 2 * chunks - 2)
    def _():
        shrink.last_ready()

    @pl.when(step == 2 * chunks)
    def _():
        shrink.both_ready()
        shrink.finish()
        store(2).start()

    def here(first):
        return pl.ds(pl.multiple_of((step - first) * rows, rows), rows)

    @pl.when(step < chunks)
    def _():
        visible = visible_keys(spans, step, rows, piece, 1)
        for half in range(2):
            weight = w_ref[half].reshape(D, 3 * width)
            bias = flat_ref[half]
            bias = jnp.concatenate(
                [bias[:, :width], jnp.zeros((1, width), jnp.float32), bias[:, width : 2 * width]],
                axis=1,
            )
            attend_half(half, weight, bias, visible, tokens(0), qkv_ref, ctx_ref)
        ctx_all[here(0), :] = ctx_ref[...]

    @pl.when(jnp.logical_and(step >= chunks, step < 2 * chunks))
    def _():
        outs = (hb_ref, g_ref, slope_ref, n1_ref, r1_ref)
        place = here(chunks)
        hidden, activated = feed_up(ctx_all[place, :], tokens(chunks), me_ref, scales_ref, up_ref, outs)
        hidden_all[place, :] = hidden
        for half in range(2):
            wide = st_ref.shape[5]
            g_all[place, half * wide : (half + 1) * wide] = activated[half]

    @pl.when(step >= 2 * chunks)
    def _():
        place = here(2 * chunks)
        wide = st_ref.shape[5]
        activated = [g_all[place, half * wide : (half + 1) * wide] for half in range(2)]
        outs = (out_ref, n2_ref, r2_ref, lead_ref)
        feed_down(piece, hidden_all[place, :], activated, st_ref, scales_ref, outs)

    @pl.when(step == pl.num_programs(0) - 1)
    def _():
        swap(t).wait_send()
        for each in (mixing, middle, shrink):
            each.drain()
        for index in range(3):
            store(index).wait()


def forward_gather(piece, spans, short_rows, long_rows, owns, offsets, scales, chunk, chunks):
    rows = chunks * chunk
    halves = lax.axis_size("tensor")
    columns = halves * owns[0].shape[1]
    anywhere = pl.BlockSpec(memory_space=pl.ANY)
    bf16, f32 = jnp.bfloat16, jnp.float32

    def buffer(own):
        return (halves, 4, 2, 2) + own.shape

    def spec(width, first):
        return pl.BlockSpec((chunk, width), lambda i: (jnp.clip(i - first * chunks, 0, chunks - 1), 0))

    shapes = [(columns, bf16, 0), (D, bf16, 0)]
    shapes += [(D, bf16, 1), (FF, bf16, 1), (FF, bf16, 1), (D, f32, 1), (1, f32, 1)]
    shapes += [(D, bf16, 2), (D, f32, 2), (1, f32, 2)]
    outs = pl.pallas_call(
        functools.partial(forward_gather_kernel, piece, chunks),
        grid=(3 * chunks,),
        in_specs=[
            pl.BlockSpec(memory_space=pltpu.SMEM),
            *(full_spec(own.shape) for own in owns),
            full_spec((offsets.shape[0] // 128, 128)),
            full_spec(scales.shape),
            *half_specs(chunk, chunks, lambda i: jnp.minimum(i, 2 * chunks - 1) % chunks),
        ],
        out_specs=[spec(width, first) for width, _, first in shapes]
        + [pl.BlockSpec((1, 8, D), lambda i: (jnp.maximum(i - 2 * chunks, 0), 0, 0))]
        + [anywhere] * 3,
        out_shape=[jax.ShapeDtypeStruct((rows, width), dtype) for width, dtype, _ in shapes]
        + [jax.ShapeDtypeStruct((chunks, 8, D), f32)]
        + [jax.ShapeDtypeStruct(buffer(own), bf16) for own in owns],
        scratch_shapes=[pltpu.VMEM(buffer(own), bf16) for own in owns]
        + [
            pltpu.VMEM((halves, offsets.shape[0] // 128, 128), f32),
            pltpu.VMEM((halves, 1, offsets.shape[0]), f32),
            pltpu.VMEM((1, FF), f32),
            pltpu.VMEM((rows, D), bf16),
            pltpu.VMEM((rows, FF), bf16),
            pltpu.VMEM((rows, D), f32),
            pltpu.SemaphoreType.DMA((3, Gather.count)),
            pltpu.SemaphoreType.DMA((3, Gather.count)),
            pltpu.SemaphoreType.DMA((3,)),
            pltpu.SemaphoreType.DMA,
            pltpu.SemaphoreType.DMA,
            pltpu.SemaphoreType.DMA((3,)),
        ],
        compiler_params=pltpu.CompilerParams(
            collective_id=3, has_side_effects=True, vmem_limit_bytes=big_vmem
        ),
        name="forward_gather",
    )(spans, *owns, offsets.reshape(-1, 128), scales, short_rows, long_rows)
    fulls = [full.reshape(halves, -1, full.shape[-1]) for full in outs[-3:]]
    return outs[:2], outs[2:-3], fulls


class Scatter:
    def __init__(self, whole, acc, sib, one, two, line, out, sends, lands, local, index):
        self.whole, self.acc, self.sib, self.out, self.index = whole, acc, sib, out, index
        self.one, self.two, self.line = one, two, line
        self.sends, self.lands, self.local = sends, lands, local
        t, z, x, c = self.place = grid_place()
        even = c == 0
        self.first = (jnp.where(even, 1 - t, t), jnp.where(even, x, 1 - x))
        self.second = (jnp.where(even, t, 1 - t), jnp.where(even, 1 - x, x))
        self.order = (2, 1, 0, 3)
        self.spots = (self.first, (1 - t, 1 - x), self.second, (t, x))

    def copy(self, source, target, which, device):
        return pltpu.make_async_remote_copy(
            src_ref=source,
            dst_ref=target,
            send_sem=self.sends.at[self.index, which],
            recv_sem=self.lands.at[self.index, which],
            device_id=device,
            device_id_type=MESH,
        )

    def outgoing(self, which):
        t, z, x, c = self.place
        if which < 4:
            spot = self.spots[self.order[which]]
            return self.copy(
                self.whole.at[spot[0], :, spot[1], 1 - c],
                self.sib.at[spot[0], :, spot[1]],
                which,
                at_place(t, z, x, 1 - c),
            )
        if which < 6:
            spot = self.spots[which - 4]
            device = at_place(self.first[0], z, self.first[1], c)
            return self.copy(self.acc.at[spot[0], :, spot[1]], self.one.at[which - 4], which, device)
        if which == 6:
            spot = self.second
            device = at_place(spot[0], z, spot[1], c)
            return self.copy(self.acc.at[spot[0], :, spot[1]], self.two, which, device)
        there = lax.rem(z + which - 6, 4)
        return self.copy(
            self.acc.at[t, there, x], self.line.at[which - 7], which, at_place(t, there, x, c)
        )

    def arrived(self, which):
        t, z, x, c = self.place
        if which < 4:
            spot = self.spots[which]
            target = self.sib.at[spot[0], :, spot[1]]
        elif which < 6:
            target = self.one.at[which - 4]
        elif which == 6:
            target = self.two
        else:
            target = self.line.at[which - 7]
        self.copy(target, target, which, at_place(t, z, x, 1 - c)).wait_recv()

    def load(self, which):
        c = self.place[3]
        spot = self.spots[which]
        return pltpu.make_async_copy(
            self.whole.at[spot[0], :, spot[1], c],
            self.acc.at[spot[0], :, spot[1]],
            self.local.at[self.index, which],
        )

    def add(self, spot, read):
        @pl.loop(0, 4)
        def _(z):
            low = self.acc[spot[0], z, spot[1]].astype(jnp.float32)
            low = low + read(z).astype(jnp.float32)
            self.acc[spot[0], z, spot[1]] = low.astype(jnp.bfloat16)

    def start(self):
        for which in range(4):
            self.outgoing(which).start()
            self.load(which).start()

    def cores_ready(self):
        for which in range(4):
            spot = self.spots[which]
            self.arrived(which)
            self.load(which).wait()
            self.add(spot, lambda z: self.sib[spot[0], z, spot[1]])
            if which < 2:
                self.outgoing(4 + which).start()

    def first_ready(self):
        self.arrived(5)
        self.add(self.second, lambda z: self.one[1, z])
        self.outgoing(6).start()
        self.arrived(4)
        self.add(self.spots[3], lambda z: self.one[0, z])

    def second_ready(self):
        self.arrived(6)
        self.add(self.spots[3], lambda z: self.two[z])
        for which in range(7, 10):
            self.outgoing(which).start()

    def finish(self):
        t, z, x, c = self.place
        total = self.acc[t, z, x].astype(jnp.float32)
        for which in range(7, 10):
            self.arrived(which)
            total = total + self.line[which - 7].astype(jnp.float32)
        self.out[...] = total
        return jnp.sum(total * total, axis=0, keepdims=True)

    def drain(self):
        for which in range(10):
            self.outgoing(which).wait_send()


class LateScatter(Scatter):
    def __init__(self, *args):
        super().__init__(*args)
        _, _, x, _ = self.place
        self.order = (0, 1, 2, 3)
        self.spots = ((0, 1 - x), (1, 1 - x), (0, x), (1, x))

    def outgoing(self, which):
        t, z, x, c = self.place
        if which < 4:
            return super().outgoing(which)
        if which < 6:
            side = which - 4
            return self.copy(
                self.acc.at[side, :, 1 - x], self.one.at[side], which, at_place(t, z, 1 - x, c)
            )
        if which == 6:
            return self.copy(self.acc.at[1 - t, z, x], self.two, which, at_place(1 - t, z, x, c))
        there = lax.rem(z + which - 6, 4)
        return self.copy(
            self.acc.at[:, there, x], self.line.at[which - 7], which, at_place(t, there, x, c)
        )

    def first_ready(self):
        for side in range(2):
            self.arrived(4 + side)
            self.add((side, self.place[2]), lambda z: self.one[side, z])
        for which in range(7, 10):
            self.outgoing(which).start()

    def second_ready(self):
        t, z, x, _ = self.place
        for which in range(7, 10):
            self.arrived(which)

        def total(side):
            value = self.acc[side, z, x].astype(jnp.float32)
            for which in range(3):
                value = value + self.line[which, side].astype(jnp.float32)
            return value

        self.acc[1 - t, z, x] = total(1 - t).astype(jnp.bfloat16)
        self.outgoing(6).start()
        self.out[...] = total(t)

    def finish(self):
        self.arrived(6)
        total = self.out[...] + self.two[...].astype(jnp.float32)
        self.out[...] = total
        return jnp.sum(total * total, axis=0, keepdims=True)


class Total:
    def __init__(self, slots, line, sends, lands):
        self.slots, self.line, self.sends, self.lands = slots, line, sends, lands
        t, z, x, c = self.place = grid_place()
        self.partners = (at_place(t, z, x, 1 - c), at_place(t, z, 1 - x, c), at_place(1 - t, z, x, c))

    def pair(self, stage):
        return pltpu.make_async_remote_copy(
            src_ref=self.slots.at[2 * stage],
            dst_ref=self.slots.at[2 * stage + 1],
            send_sem=self.sends.at[stage],
            recv_sem=self.lands.at[stage],
            device_id=self.partners[stage],
            device_id_type=MESH,
        )

    def along(self, gap):
        t, z, x, c = self.place
        return pltpu.make_async_remote_copy(
            src_ref=self.line.at[z],
            dst_ref=self.line.at[z],
            send_sem=self.sends.at[2 + gap],
            recv_sem=self.lands.at[2 + gap],
            device_id=at_place(t, lax.rem(z + gap, 4), x, c),
            device_id_type=MESH,
        )

    def landed(self, gap):
        t, z, x, c = self.place
        spot = self.line.at[lax.rem(z + 4 - gap, 4)]
        pltpu.make_async_remote_copy(
            src_ref=spot,
            dst_ref=spot,
            send_sem=self.sends.at[2 + gap],
            recv_sem=self.lands.at[2 + gap],
            device_id=self.partners[0],
            device_id_type=MESH,
        ).wait_recv()

    def start(self, value):
        self.slots[0] = value
        self.pair(0).start()

    def advance(self, stage):
        self.pair(stage).wait_recv()
        summed = self.slots[2 * stage] + self.slots[2 * stage + 1]
        if stage < 2:
            self.slots[2 * stage + 2] = summed
            self.pair(stage + 1).start()
            return
        z = self.place[1]
        self.line[z] = summed
        for gap in range(1, 4):
            self.along(gap).start()

    def finish(self):
        for gap in range(1, 4):
            self.landed(gap)
        return (self.line[0] + self.line[1]) + (self.line[2] + self.line[3])

    def drain(self):
        for stage in range(3):
            self.pair(stage).wait_send()
        for gap in range(1, 4):
            self.along(gap).wait_send()


class Cube:
    def __init__(self, slots, line, sends, lands):
        self.slots, self.line, self.sends, self.lands = slots, line, sends, lands
        self.place = grid_place()

    def turned(self, flip):
        t, _, x, c = self.place
        return (1 - t if flip & 4 else t), (1 - x if flip & 2 else x), (1 - c if flip & 1 else c)

    def copy(self, slot, which, device):
        return pltpu.make_async_remote_copy(
            src_ref=slot,
            dst_ref=slot,
            send_sem=self.sends.at[which],
            recv_sem=self.lands.at[which],
            device_id=device,
            device_id_type=MESH,
        )

    def slot(self, flip):
        t, x, c = self.turned(flip)
        return self.slots.at[t * 4 + x * 2 + c]

    def push(self, flip):
        t, x, c = self.turned(flip)
        return self.copy(self.slot(0), flip - 1, at_place(t, self.place[1], x, c))

    def along(self, gap, back=False):
        t, z, x, c = self.place
        slot = self.line.at[lax.rem(z + 4 - gap, 4) if back else z]
        return self.copy(slot, 6 + gap, at_place(t, lax.rem(z + gap, 4), x, c))

    def total(self, value):
        t, z, x, c = self.place
        self.slots[t * 4 + x * 2 + c] = value
        for flip in range(1, 8):
            self.push(flip).start()
        for flip in range(1, 8):
            self.copy(self.slot(flip), flip - 1, self.place_of(flip)).wait_recv()
        self.line[z] = jnp.sum(self.slots[...], axis=0)
        for gap in range(1, 4):
            self.along(gap).start()
        for gap in range(1, 4):
            self.along(gap, True).wait_recv()
        return (self.line[0] + self.line[1]) + (self.line[2] + self.line[3])

    def place_of(self, flip):
        t, x, c = self.turned(flip)
        return at_place(t, self.place[1], x, c)

    def drain(self):
        for flip in range(1, 8):
            self.push(flip).wait_send()
        for gap in range(1, 4):
            self.along(gap).wait_send()


def scatter_buffers(whole, columns, late=False):
    halves = lax.axis_size("tensor")
    rows = whole.shape[1] // lax.axis_size("dp")
    two, line = ((), (3, halves)) if late else ((4,), (3,))
    shapes = ((halves, 4, 2), (halves, 4, 2), (2, 4), two, line)
    return [pltpu.VMEM(shape + (rows, columns), jnp.bfloat16) for shape in shapes]


def scatter_parts(pieces, buffers, sems, kind=Scatter):
    return [
        kind(
            whole.at[:, :, :, :, :, first : first + columns],
            *buffers[5 * index : 5 * index + 5],
            out.at[:, first : first + columns],
            *sems,
            index,
        )
        for index, (whole, out, first, columns) in enumerate(pieces)
    ]


def scatter_sems(count):
    return [
        pltpu.SemaphoreType.DMA((count, 10)),
        pltpu.SemaphoreType.DMA((count, 10)),
        pltpu.SemaphoreType.DMA((count, 4)),
    ]


def scatter_input(whole):
    return whole.reshape(lax.axis_size("tensor"), 4, 2, 2, -1, whole.shape[2])


def scatter_shape(whole):
    return jax.ShapeDtypeStruct((whole.shape[1] // lax.axis_size("dp"), whole.shape[2]), jnp.float32)


def push_partner(source, target, index, sends, lands):
    t, z, x, c = grid_place()
    return pltpu.make_async_remote_copy(
        src_ref=source.at[index],
        dst_ref=target.at[index],
        send_sem=sends.at[index],
        recv_sem=lands.at[index],
        device_id=at_place(1 - t, z, x, c),
        device_id_type=MESH,
    )


class Plan:
    def __init__(self, actions, times):
        self.at, self.rest = {}, []
        points = sorted(times.items(), key=lambda item: item[1])
        at = 0
        for due, action in sorted(actions, key=lambda item: item[0]):
            while at < len(points) and points[at][1] < due:
                at += 1
            if at < len(points):
                self.at.setdefault(points[at][0], []).append(action)
            else:
                self.rest.append(action)

    def run(self, point):
        for (step, where), actions in self.at.items():
            if where == point:

                @pl.when(pl.program_id(0) == step)
                def _():
                    for action in actions:
                        action()

    def finish(self):
        for action in self.rest:
            action()


def scatter_actions(parts, ready, link, ended=lambda part: part.finish):
    actions = []
    for index, part in enumerate(parts):
        due = ready + link * index
        actions += [
            (due, part.cores_ready),
            (due + link + 2, part.first_ready),
            (due + 2 * link + 4, part.second_ready),
            (due + 2 * link + 7, ended(part)),
        ]
    return actions


def feed_back_scatter_kernel(chunks, early, columns, whole_ref, tail_ref, *refs):
    ins, outs, (tail_out, out_ref) = refs[:9], refs[9:15], refs[15:17]
    scratch, rest = refs[17:20], refs[20:]
    count = whole_ref.shape[5] // columns
    buffers, sems, (sends, lands) = rest[: 5 * count], rest[5 * count : 5 * count + 3], rest[5 * count + 3 :]
    parts = scatter_parts(
        [(whole_ref, out_ref, index * columns, columns) for index in range(count)], buffers, sems, LateScatter
    )

    def begin():
        greet_neighbours()
        for part in parts:
            part.start()
        for index in range(early):
            push_partner(tail_ref.at[chunks - early :], tail_out, index, sends, lands).start()

    actions = [(0, begin)] + scatter_actions(parts, 8, 6.6)
    steps = chunks + D // ins[5].shape[1] + 2 * (ins[7].shape[2] // outs[5].shape[2])
    times = {(step, 0): 4 + 5.3 * step for step in range(chunks)}
    times |= {(step, 0): 30.5 + 1.7 * (step - chunks) for step in range(chunks, steps)}
    times |= {(step, 1 + half): 6 + 5.3 * step + 2 * half for step in range(chunks) for half in range(2)}
    times[(0, 0)] = 0
    plan = Plan(actions, times)
    feed_back_kernel(chunks, *ins, *outs, *scratch, plan.run)

    @pl.when(pl.program_id(0) == pl.num_programs(0) - 1)
    def _():
        plan.finish()
        for part in parts:
            part.drain()
        for index in range(early):
            push_partner(tail_ref.at[chunks - early :], tail_out, index, sends, lands).wait()


def attend_last_kernel(piece, chunks, columns, spans, one_ref, two_ref, *refs):
    ins, short_ref, long_ref, done_ref = refs[:4], *refs[4:7]
    first_ref, second_ref, upward_ref, loss_ref = refs[7:11]
    refs = refs[1:]
    dx_ref, low_out, one_out, two_out, last_out, total_ref, norm_ref = refs[10:17]
    dproj_ref, bias_ref, turned_ref, grad_ref, square_ref, low_ref, sends, lands = refs[17:25]
    rest = refs[25:]
    count = one_ref.shape[5] // columns + 1
    late = scatter_parts(
        [(one_ref, one_out, index * columns, columns) for index in range(count - 1)]
        + [(two_ref, two_out, 0, columns)],
        rest[: 5 * count],
        rest[5 * count : 5 * count + 3],
        LateScatter,
    )
    rest = rest[5 * count + 3 :]
    tail = grad_ref.shape[5] // columns
    last = scatter_parts(
        [(grad_ref, last_out, index * columns, columns) for index in range(tail)],
        rest[: 5 * tail],
        rest[5 * tail : 5 * tail + 3],
    )
    rest = rest[5 * tail + 3 :]
    vector, norm = Total(*rest[:4]), Cube(*rest[4:])
    step = pl.program_id(0)

    def begin():
        greet_neighbours(True)
        for part in late:
            part.start()
        square_ref[...] = jnp.zeros_like(square_ref)
        turned_ref[:, : short_ref.shape[0]] = short_ref[...].T
        turned_ref[:, short_ref.shape[0] :] = long_ref[...].T

    def ended(part):
        def action():
            square_ref[0:1, :] += part.finish()

        return action

    actions = [(0, begin)] + scatter_actions(late, 8, 6.6, ended)
    actions += scatter_actions(last, 46, 5, ended)
    actions += [(46.5, lambda: vector.advance(0)), (50, lambda: vector.advance(1)), (57, lambda: vector.advance(2))]
    times = {(step, point): 4 + 7.3 * step + 1.15 * point for step in range(chunks) for point in range(7)}
    times |= {(chunks + tile, 0): 41 + 2.0 * tile for tile in range(2 * tail)}
    times[(0, 0)] = 0
    plan = Plan(actions, times)
    plan.run(0)

    @pl.when(step < chunks)
    def _():
        rows = dx_ref.shape[0]
        here = dproj_ref.at[pl.ds(pl.multiple_of(step * rows, rows), rows), :]
        attend_back_kernel(piece, spans, *ins, here, dx_ref, bias_ref, low_ref, plan.run)

    for index in range(chunks):

        @pl.when(step == index)
        def _():
            if index == chunks - 1:
                base = bias_ref.shape[1] // 2
                wide = upward_ref.shape[1] // 2
                lines = [first_ref[0:2, :], second_ref[0:2, :], first_ref[2:3, :], second_ref[2:3, :]]
                for half in range(2):
                    at = half * base
                    pair = [bias_ref[0:1, at : at + columns]]
                    pair += [bias_ref[0:1, at + 2 * columns : at + 3 * columns]]
                    lines.append(jnp.concatenate(pair, axis=1))
                    lines += [
                        upward_ref[0:1, half * wide + first : half * wide + first + D]
                        for first in range(0, wide, D)
                    ]
                column = lax.broadcasted_iota(jnp.int32, (1, D), 1)
                lines.append(jnp.where(column == 1, loss_ref[0:1, 0:1], 0.0))
                lines.append(jnp.zeros((3, D), jnp.float32))
                pack = jnp.concatenate(lines, axis=0)
                vector.start(pack)
            push_partner(low_ref, low_out, index, sends, lands).start()

    @pl.when(step >= chunks)
    def _():
        tile = step - chunks
        half, piece_index = lax.rem(tile, 2), lax.div(tile, 2)
        start = pl.multiple_of((half * tail + piece_index) * columns, columns)
        grad = dot_nn(turned_ref[...], dproj_ref[:, pl.ds(start, columns)]).astype(jnp.bfloat16)
        start = pl.multiple_of(piece_index * columns, columns)
        grad_ref[half, :, :, :, :, pl.ds(start, columns)] = grad.reshape(
            grad_ref.shape[1:5] + (columns,)
        )

    for index, part in enumerate(last):

        @pl.when(step == chunks + 2 * index + 1)
        def _():
            part.start()

    @pl.when(step == pl.num_programs(0) - 1)
    def _():
        plan.finish()
        total_ref[...] = vector.finish()
        squares = jnp.sum(square_ref[...]) + jnp.sum(done_ref[...] * done_ref[...])
        norm_ref[...] = norm.total(jnp.full(norm_ref.shape, squares))
        for each in late + last + [vector, norm]:
            each.drain()
        for index in range(chunks):
            push_partner(low_ref, low_out, index, sends, lands).wait()


def adam(weight, moment, square, average, gradient, rate, scalars):
    factor, first_fix, second_fix = scalars
    clipped = gradient * factor
    first = first_decay * moment + (1.0 - first_decay) * clipped
    second = second_decay * square + (1.0 - second_decay) * clipped * clipped
    master = weight - rate * (
        first / first_fix / (jnp.sqrt(second / second_fix) + adam_eps) + decay_weight * weight
    )
    smooth = smooth_decay * average + (1.0 - smooth_decay) * master
    return master, first, second, smooth


def finish_kernel(chunk, chunks, rates, passages, halves, *refs):
    out_own, out_head, out_tail, dx_own, dx_other = refs[:5]
    large, grads = refs[5:21], refs[21:25]
    scales_refs, offsets_refs, total_ref, norm_ref, step_ref = refs[25:29], refs[29:33], *refs[33:36]
    short_out, long_out, short_dx, long_dx = refs[36:40]
    large_outs, scales_outs, offsets_outs, figures_ref = refs[40:56], refs[56:60], refs[60:64], refs[64]
    scratch = refs[65:]
    ins, outs = scratch[:16], scratch[16:32]
    rows_ref, own_ref, low_ref, wide_ref, in_sems, out_sems, block_sems, wide_sems, load_sems = scratch[32:]
    place = lax.axis_index("tensor")
    longs = chunks - 1

    def rows(first, count):
        return pl.ds(pl.multiple_of(first * chunk, chunk), count * chunk)

    ahead = out_head.shape[0] // chunk
    other = 1 - place
    brought = [
        pltpu.make_async_copy(source, target, load_sems.at[k])
        for k, (source, target) in enumerate(
            (
                (dx_other, low_ref),
                (out_own, rows_ref.at[rows(0, chunks)]),
                (out_head, rows_ref.at[rows(chunks, ahead)]),
                (out_tail, rows_ref.at[rows(chunks + ahead, chunks - ahead)]),
                (dx_own, own_ref),
            )
        )
    ]
    for load in brought:
        load.start()
    loads = [pltpu.make_async_copy(large[k], ins[k], in_sems.at[k]) for k in range(16)]
    for load in loads:
        load.start()
    blocks = [
        (rows_ref.at[rows(0, 1)], short_out.at[rows(place, 1)]),
        (rows_ref.at[rows(1, longs)], long_out.at[rows(place * longs, longs)]),
        (rows_ref.at[rows(chunks, 1)], short_out.at[rows(other, 1)]),
        (rows_ref.at[rows(chunks + 1, longs)], long_out.at[rows(other * longs, longs)]),
        (own_ref.at[rows(0, 1)], short_dx.at[rows(place, 1)]),
        (own_ref.at[rows(1, longs)], long_dx.at[rows(place * longs, longs)]),
    ]
    copies = [
        pltpu.make_async_copy(source, target, block_sems.at[k])
        for k, (source, target) in enumerate(blocks)
    ]
    brought[0].wait()
    for index in range(chunks):
        wide_ref[index] = low_ref[rows(index, 1), :].astype(jnp.float32)
        target = short_dx.at[rows(other, 1)]
        if index > 0:
            target = long_dx.at[rows(other * longs + index - 1, 1)]
        copy = pltpu.make_async_copy(wide_ref.at[index], target, wide_sems.at[index])
        copy.start()
        copies.append(copy)
    for load in brought[1:]:
        load.wait()
    for copy in copies[:6]:
        copy.start()

    sums = total_ref[...]
    row = lax.broadcasted_iota(jnp.int32, sums.shape, 0)
    column = lax.broadcasted_iota(jnp.int32, sums.shape, 1)

    def whole_sum(value):
        return jnp.sum(jnp.sum(value, axis=1, keepdims=True), axis=0, keepdims=True)

    squares = norm_ref[0:1, 0:1] + whole_sum(jnp.where(row < 12, sums * sums, 0.0))
    loss = whole_sum(jnp.where(jnp.logical_and(row == 12, column == 1), sums, 0.0))
    norm = jnp.sqrt(squares)
    factor = clip_limit / jnp.maximum(norm, clip_limit)
    steps = jnp.full((1, 1), step_ref[0], jnp.int32).astype(jnp.float32)
    first_fix = 1.0 - jnp.exp(steps * math.log(first_decay))
    second_fix = 1.0 - jnp.exp(steps * math.log(second_decay))
    scalars = (factor, first_fix, second_fix)
    figure = lax.broadcasted_iota(jnp.int32, figures_ref.shape, 0)
    figures_ref[...] = jnp.where(figure == 0, norm, loss / (halves * passages))
    for each in range(4):
        values = []
        for k in range(4 * each, 4 * each + 4):
            loads[k].wait()
            values.append(ins[k][...])
        gradient = grads[each][...]
        if values[0].ndim == 3:
            width = values[0].shape[2]
            gradient = jnp.stack([gradient[:, k * width : (k + 1) * width] for k in range(3)])
        fixed = [one.reshape((1,) * values[0].ndim) for one in scalars]
        new = adam(*values, gradient, rates[each], fixed)
        for part in range(4):
            k = 4 * each + part
            outs[k][...] = new[part]
            copy = pltpu.make_async_copy(outs[k], large_outs[k], out_sems.at[k])
            copy.start()
            copies.append(copy)
    new = adam(*(ref[...] for ref in scales_refs), sums[:6], rates[4], scalars)
    for ref, value in zip(scales_outs, new):
        ref[...] = value
    mine = jnp.where(place == 0, sums[6:9], sums[9:12])
    width = offsets_refs[0].shape[1]
    mine = jnp.concatenate(
        [mine[r : r + 1, c : c + width] for r in range(3) for c in range(0, D, width)], axis=0
    )
    new = adam(*(ref[...] for ref in offsets_refs), mine, rates[5], scalars)
    for ref, value in zip(offsets_outs, new):
        ref[...] = value
    for copy in copies:
        copy.wait()


def finish(chunk, halves_of_rows, large, grads, scales, offsets, total, norm, step_count, passages):
    chunks = halves_of_rows[0].shape[0] // chunk
    halves = lax.axis_size("tensor")
    anywhere = pl.BlockSpec(memory_space=pl.ANY)
    vmem = pl.BlockSpec(memory_space=pltpu.VMEM)
    smem = pl.BlockSpec(memory_space=pltpu.SMEM)
    f32, bf16 = jnp.float32, jnp.bfloat16
    rates = (1.0 / math.sqrt(D), 8.0 / math.sqrt(D), 1.0 / math.sqrt(D), 1.0 / math.sqrt(FF), 0.3, 0.3)
    offsets = [each.reshape(-1, 128) for each in offsets]
    shaped = [jax.ShapeDtypeStruct(each.shape, f32) for each in (*large, *scales, *offsets)]
    both = [
        jax.ShapeDtypeStruct((halves * count * chunk, D), dtype)
        for dtype in (bf16, f32)
        for count in (1, chunks - 1)
    ]
    outs = pl.pallas_call(
        functools.partial(finish_kernel, chunk, chunks, rates, passages, halves),
        in_specs=[anywhere] * 21 + [vmem] * 14 + [smem],
        out_specs=[anywhere] * 20 + [vmem] * 9,
        out_shape=both + shaped + [jax.ShapeDtypeStruct((8, 128), f32)],
        scratch_shapes=[pltpu.VMEM(each.shape, f32) for each in large] * 2
        + [
            pltpu.VMEM((halves * chunks * chunk, D), bf16),
            pltpu.VMEM((chunks * chunk, D), f32),
            pltpu.VMEM((chunks * chunk, D), bf16),
            pltpu.VMEM((chunks, chunk, D), f32),
            pltpu.SemaphoreType.DMA((16,)),
            pltpu.SemaphoreType.DMA((16,)),
            pltpu.SemaphoreType.DMA((6,)),
            pltpu.SemaphoreType.DMA((chunks,)),
            pltpu.SemaphoreType.DMA((5,)),
        ],
        compiler_params=pltpu.CompilerParams(vmem_limit_bytes=big_vmem),
        name="finish",
    )(*halves_of_rows, *large, *grads, *scales, *offsets, total, norm, step_count)
    return outs[:4], outs[4:20], outs[20:24], [each.reshape(-1) for each in outs[24:28]], outs[28]


def half_specs(chunk, chunks, at):
    def long_at(i):
        return (lax.axis_index("tensor") * (chunks - 1) + jnp.maximum(at(i) - 1, 0), 0)

    return [
        pl.BlockSpec((chunk, D), lambda i: (lax.axis_index("tensor"), 0)),
        pl.BlockSpec((chunk, D), long_at),
    ]


def row_spec(rows, columns):
    return pl.BlockSpec((rows, columns), lambda i: (i, 0))


def full_spec(shape):
    return pl.BlockSpec(shape, lambda i: (0,) * len(shape), pipeline_mode=pl.Buffered(1))


def shards(
    short_tokens,
    long_tokens,
    short_cotangent,
    long_cotangent,
    short_lengths,
    long_lengths,
    queries,
    positives,
    step_count,
    mixing_weight,
    mixing_moment,
    mixing_square,
    mixing_average,
    merging_weight,
    merging_moment,
    merging_square,
    merging_average,
    expand_weight,
    expand_moment,
    expand_square,
    expand_average,
    shrink_weight,
    shrink_moment,
    shrink_square,
    shrink_average,
    scales_weight,
    scales_moment,
    scales_square,
    scales_average,
    offsets_weight,
    offsets_moment,
    offsets_square,
    offsets_average,
):
    halves = lax.axis_size("tensor")
    place = lax.axis_index("tensor")
    short_span = short_tokens.shape[1]
    long_span = long_tokens.shape[1]
    shorts = short_tokens.shape[0] // halves
    longs = long_tokens.shape[0] // halves
    chunk = long_span
    piece = short_span
    assert shorts * short_span == chunk and shorts == longs
    chunks = longs + 1
    rows = chunks * chunk
    width = mixing_weight.shape[2]
    wide = expand_weight.shape[1]

    def own_half(short_all, long_all):
        return jnp.concatenate(
            [
                lax.dynamic_slice_in_dim(short_all, place * shorts, shorts).reshape(-1, D),
                lax.dynamic_slice_in_dim(long_all, place * longs, longs).reshape(-1, D),
            ],
            axis=0,
        )

    fast = lax.axis_size("dp") == 16 and halves == 2
    mixing_own = mixing_weight.astype(jnp.bfloat16).reshape(-1, 3 * width)
    middle_own = jnp.concatenate([merging_weight.T, expand_weight], axis=1).astype(jnp.bfloat16)
    shrink_own = shrink_weight.T.astype(jnp.bfloat16)
    short_limits = lax.dynamic_slice_in_dim(short_lengths, place * shorts, shorts)
    long_limits = lax.dynamic_slice_in_dim(long_lengths, place * longs, longs)
    spans = jnp.concatenate(
        [
            short_limits[None, :],
            long_limits[:, None] - piece * jnp.arange(chunk // piece, dtype=jnp.int32)[None, :],
        ],
        axis=0,
    )
    inputs = own_half(short_tokens, long_tokens)
    bf16, f32 = jnp.bfloat16, jnp.float32

    def shaped(columns, dtype):
        return jax.ShapeDtypeStruct((rows, columns), dtype)

    smem = pl.BlockSpec(memory_space=pltpu.SMEM)
    params = pltpu.CompilerParams(vmem_limit_bytes=big_vmem)
    mixing_columns = halves * 3 * width
    scores_flops = 2 * rows * chunk * PAIR * (halves * width // HEAD_DIM)
    if fast:
        (qkv, context), feed, (mixing_full, middle_full, shrink_full) = forward_gather(
            piece,
            spans,
            short_tokens.reshape(-1, D),
            long_tokens.reshape(-1, D),
            (mixing_own, middle_own, shrink_own),
            offsets_weight,
            scales_weight,
            chunk,
            chunks,
        )
    else:
        mixing_full, middle_full, shrink_full = (
            gathered(own) for own in (mixing_own, middle_own, shrink_own)
        )
        offsets_other = tensor_swap(offsets_weight)
        offsets_both = jnp.where(
            place == 0,
            jnp.stack([offsets_weight, offsets_other]),
            jnp.stack([offsets_other, offsets_weight]),
        )
        mixing_bias = jnp.concatenate(
            [
                offsets_both[:, :width],
                jnp.zeros((halves, width), jnp.float32),
                offsets_both[:, width : 2 * width],
            ],
            axis=1,
        ).reshape(1, -1)
        qkv, context = pl.pallas_call(
            functools.partial(attend_forward_kernel, piece),
            grid=(chunks,),
            in_specs=[
                smem,
                row_spec(chunk, D),
                full_spec(mixing_full.shape),
                full_spec(mixing_bias.shape),
            ],
            out_specs=[row_spec(chunk, mixing_columns), row_spec(chunk, D)],
            out_shape=[shaped(mixing_columns, bf16), shaped(D, bf16)],
            compiler_params=params,
            cost_estimate=pl.CostEstimate(
                flops=2 * rows * D * mixing_columns + 6 * scores_flops,
                bytes_accessed=16 * 1024 * 1024,
                transcendentals=rows * chunk * 12,
            ),
            name="attend_forward",
        )(spans, inputs, mixing_full, mixing_bias)
        upward_bias = offsets_both[:, 2 * width :].reshape(1, -1)
        feed_ins = [context, inputs, middle_full, shrink_full, scales_weight, upward_bias]
        feed_in_specs = [
            row_spec(chunk, D),
            row_spec(chunk, D),
            full_spec(middle_full.shape),
            full_spec(shrink_full.shape),
            full_spec(scales_weight.shape),
            full_spec(upward_bias.shape),
        ]
        feed_out_specs = [
            row_spec(chunk, D),
            row_spec(chunk, FF),
            row_spec(chunk, FF),
            row_spec(chunk, D),
            row_spec(chunk, 1),
            row_spec(chunk, D),
            row_spec(chunk, D),
            row_spec(chunk, 1),
            pl.BlockSpec((1, 8, D), lambda i: (i, 0, 0)),
        ]
        feed_outs = [
            shaped(D, bf16),
            shaped(FF, bf16),
            shaped(FF, bf16),
            shaped(D, f32),
            shaped(1, f32),
            shaped(D, bf16),
            shaped(D, f32),
            shaped(1, f32),
            jax.ShapeDtypeStruct((chunks, 8, D), f32),
        ]
        feed_cost = pl.CostEstimate(
            flops=2 * rows * D * (D + 2 * FF),
            bytes_accessed=48 * 1024 * 1024,
            transcendentals=2 * rows * FF,
        )
        feed = pl.pallas_call(
            functools.partial(feed_forward_kernel, piece),
            grid=(chunks,),
            in_specs=feed_in_specs,
            out_specs=feed_out_specs,
            out_shape=feed_outs,
            compiler_params=params,
            cost_estimate=feed_cost,
            name="feed_forward",
        )(*feed_ins)
    anywhere = pl.BlockSpec(memory_space=pl.ANY)
    (
        hidden_low,
        activated,
        slope,
        normed_first,
        rstd_first,
        output,
        normed_second,
        rstd_second,
        leading,
    ) = feed
    query_gradient, lead_rows, loss_rows = contrast(leading, queries, positives)
    ahead = 2
    if fast:
        output_head = lax.optimization_barrier((output[: ahead * chunk], lead_rows))[0]
        output_head = tensor_swap(output_head)
    tile = 512
    per = wide // tile

    def chunk_spec(columns):
        return pl.BlockSpec((chunk, columns), lambda i: (jnp.minimum(i, chunks - 1), 0))

    second_back, second_grad, shrink_grad = pl.pallas_call(
        functools.partial(out_back_kernel, piece, chunks),
        grid=(chunks + FF // tile,),
        in_specs=[
            *half_specs(chunk, chunks, lambda i: jnp.minimum(i, chunks - 1)),
            pl.BlockSpec((1, 8, D), lambda i: (jnp.minimum(i, chunks - 1), 0, 0)),
            chunk_spec(D),
            chunk_spec(1),
            full_spec(scales_weight.shape),
            pl.BlockSpec((rows, tile), lambda i: (0, jnp.maximum(i - chunks, 0))),
        ],
        out_specs=[
            chunk_spec(D),
            pl.BlockSpec((8, D), lambda i: (0, 0)),
            pl.BlockSpec(
                (1, D, tile),
                lambda i: (jnp.maximum(i - chunks, 0) // per, 0, jnp.maximum(i - chunks, 0) % per),
            ),
        ],
        out_shape=[
            shaped(D, f32),
            jax.ShapeDtypeStruct((8, D), f32),
            jax.ShapeDtypeStruct((halves, D, wide), bf16),
        ],
        scratch_shapes=[pltpu.VMEM((D, rows), bf16)],
        compiler_params=params,
        cost_estimate=pl.CostEstimate(
            flops=2 * rows * D * FF, bytes_accessed=32 * 1024 * 1024, transcendentals=0
        ),
        name="out_back",
    )(
        short_cotangent.reshape(-1, D),
        long_cotangent.reshape(-1, D),
        lead_rows, normed_second, rstd_second, scales_weight, activated)
    back_ins = [
        second_back,
        normed_first,
        rstd_first,
        slope,
        hidden_low,
        context,
        middle_full,
        shrink_full,
        scales_weight,
    ]
    merging_tiles = D // width
    back_steps = chunks + merging_tiles + FF // tile

    def merging_at(i):
        return jnp.clip(i - chunks, 0, merging_tiles - 1)

    def expand_at(i):
        return jnp.maximum(i - chunks - merging_tiles, 0)

    back_in_specs = [
        chunk_spec(D),
        chunk_spec(D),
        chunk_spec(1),
        chunk_spec(FF),
        chunk_spec(D),
        pl.BlockSpec((rows, width), lambda i: (0, merging_at(i))),
        full_spec(middle_full.shape),
        full_spec(shrink_full.shape),
        full_spec(scales_weight.shape),
    ]
    back_out_specs = [
        chunk_spec(D),
        chunk_spec(D),
        pl.BlockSpec((8, D), lambda i: (0, 0)),
        pl.BlockSpec((8, FF), lambda i: (0, 0)),
        pl.BlockSpec((1, D, width), lambda i: (merging_at(i), 0, 0)),
        pl.BlockSpec((1, D, tile), lambda i: (expand_at(i) // per, 0, expand_at(i) % per)),
    ]
    back_outs = [
        shaped(D, f32),
        shaped(D, bf16),
        jax.ShapeDtypeStruct((8, D), f32),
        jax.ShapeDtypeStruct((8, FF), f32),
        jax.ShapeDtypeStruct((halves, D, width), bf16),
        jax.ShapeDtypeStruct((halves, D, wide), bf16),
    ]
    back_scratch = [
        pltpu.VMEM((rows, FF), bf16),
        pltpu.VMEM((D, rows), bf16),
        pltpu.VMEM((D, rows), bf16),
    ]
    back_cost = pl.CostEstimate(
        flops=2 * rows * D * (2 * D + 3 * FF), bytes_accessed=48 * 1024 * 1024, transcendentals=0
    )
    if fast:
        shrink_grad, output_head = lax.optimization_barrier((shrink_grad, output_head))
        tail = output.reshape(chunks, chunk, D)
        *back, output_tail, shrink_sum = pl.pallas_call(
            functools.partial(feed_back_scatter_kernel, chunks, chunks - ahead, width),
            grid=(back_steps,),
            in_specs=[anywhere, full_spec(tail.shape)] + back_in_specs,
            out_specs=back_out_specs + [anywhere, full_spec(scatter_shape(shrink_grad).shape)],
            out_shape=back_outs
            + [jax.ShapeDtypeStruct((chunks - ahead, chunk, D), bf16), scatter_shape(shrink_grad)],
            scratch_shapes=back_scratch
            + scatter_buffers(shrink_grad, width, True) * (wide // width)
            + scatter_sems(wide // width)
            + [pltpu.SemaphoreType.DMA((chunks - ahead,))] * 2,
            compiler_params=pltpu.CompilerParams(
                collective_id=5, has_side_effects=True, vmem_limit_bytes=big_vmem
            ),
            cost_estimate=back_cost,
            name="feed_back_scatter",
        )(scatter_input(shrink_grad), tail, *back_ins)
    else:
        back = pl.pallas_call(
            functools.partial(feed_back_kernel, chunks),
            grid=(back_steps,),
            in_specs=back_in_specs,
            out_specs=back_out_specs,
            out_shape=back_outs,
            scratch_shapes=back_scratch,
            compiler_params=params,
            cost_estimate=back_cost,
            name="feed_back",
        )(*back_ins)
        shrink_sum = scattered(shrink_grad)
        output_head = tensor_swap(output[: ahead * chunk])
        output_tail = tensor_swap(output[ahead * chunk :])
    first_back, context_back, first_grad, upward_grad, merging_grad, expand_grad = back
    pair_ins = [qkv, context_back, first_back, mixing_full]
    pair_in_specs = [
        chunk_spec(mixing_columns),
        chunk_spec(D),
        chunk_spec(D),
        full_spec(mixing_full.shape),
    ]
    pair_cost = pl.CostEstimate(
        flops=2 * rows * D * mixing_columns + 15 * scores_flops,
        bytes_accessed=24 * 1024 * 1024,
        transcendentals=rows * chunk * 12,
    )
    lane = lax.broadcasted_iota(jnp.int32, (1, D), 1)
    losses = jnp.where(lane == 1, loss_rows[0, 0], 0.0)

    def stacked(bias_both, scalars):
        scalars = jnp.pad(scalars, ((0, 3), (0, 0)))
        offsets_grad = jnp.concatenate([bias_both, upward_grad[0].reshape(halves, wide)], axis=1)
        vectors = [first_grad[:2], second_grad[:2], first_grad[2:3], second_grad[2:3]]
        return jnp.concatenate(vectors + [offsets_grad.reshape(-1, D), scalars], axis=0)

    if fast:
        parts = (expand_grad, merging_grad)
        late_count, last_count = wide // width + 1, 3
        last_whole = jax.ShapeDtypeStruct((halves, D, 3 * width), bf16)
        vector = jax.ShapeDtypeStruct((16, D), f32)
        more = (shrink_sum, first_grad, second_grad, upward_grad, loss_rows)
        small = (8, 128)
        out_shape = [
            shaped(D, f32),
            jax.ShapeDtypeStruct((chunks, chunk, D), bf16),
            scatter_shape(expand_grad),
            scatter_shape(merging_grad),
            scatter_shape(last_whole),
            jax.ShapeDtypeStruct(vector.shape, f32),
            jax.ShapeDtypeStruct(small, f32),
        ]
        input_back, input_other, expand_sum, merging_sum, mixing_sum, summed, squares_all = (
            pl.pallas_call(
                functools.partial(attend_last_kernel, piece, chunks, width),
                grid=(chunks + 2 * last_count,),
                in_specs=[smem, anywhere, anywhere]
                + pair_in_specs
                + [
                    pl.BlockSpec((count * chunk, D), lambda i: (lax.axis_index("tensor"), 0), pipeline_mode=pl.Buffered(1))
                    for count in (1, chunks - 1)
                ]
                + [full_spec(each.shape) for each in more],
                out_specs=[chunk_spec(D), anywhere]
                + [full_spec(each.shape) for each in out_shape[2:]],
                out_shape=out_shape,
                scratch_shapes=[
                    pltpu.VMEM((rows, mixing_columns), bf16),
                    pltpu.VMEM((8, mixing_columns), f32),
                    pltpu.VMEM((D, rows), bf16),
                    pltpu.VMEM((halves, 4, 2, 2, D // 16, 3 * width), bf16),
                    pltpu.VMEM((8, width), f32),
                    pltpu.VMEM((chunks, chunk, D), bf16),
                    pltpu.SemaphoreType.DMA((chunks,)),
                    pltpu.SemaphoreType.DMA((chunks,)),
                ]
                + scatter_buffers(expand_grad, width, True) * late_count
                + scatter_sems(late_count)
                + scatter_buffers(last_whole, width) * last_count
                + scatter_sems(last_count)
                + [
                    pltpu.VMEM((6,) + vector.shape, f32),
                    pltpu.VMEM((4,) + vector.shape, f32),
                    pltpu.SemaphoreType.DMA((6,)),
                    pltpu.SemaphoreType.DMA((6,)),
                    pltpu.VMEM((8,) + small, f32),
                    pltpu.VMEM((4,) + small, f32),
                    pltpu.SemaphoreType.DMA((10,)),
                    pltpu.SemaphoreType.DMA((10,)),
                ],
                compiler_params=pltpu.CompilerParams(
                    collective_id=6, has_side_effects=True, vmem_limit_bytes=big_vmem
                ),
                cost_estimate=pair_cost,
                name="attend_last",
            )(
                spans,
                *(scatter_input(part) for part in parts),
                *pair_ins,
                short_tokens.reshape(-1, D),
                long_tokens.reshape(-1, D),
                *more,
            )
        )
    else:
        projected_back, input_back, bias_grad, input_low = pl.pallas_call(
            functools.partial(attend_back_kernel, piece),
            grid=(chunks,),
            in_specs=[smem] + pair_in_specs,
            out_specs=[
                row_spec(chunk, mixing_columns),
                row_spec(chunk, D),
                pl.BlockSpec((8, mixing_columns), lambda i: (0, 0)),
                pl.BlockSpec((1, chunk, D), lambda i: (i, 0, 0)),
            ],
            out_shape=[
                shaped(mixing_columns, bf16),
                shaped(D, f32),
                jax.ShapeDtypeStruct((8, mixing_columns), f32),
                jax.ShapeDtypeStruct((chunks, chunk, D), bf16),
            ],
            compiler_params=params,
            cost_estimate=pair_cost,
            name="attend_back",
        )(spans, *pair_ins)
        expand_sum, merging_sum = scattered(expand_grad), scattered(merging_grad)
        input_other = tensor_swap(input_low)
        mixing_sum = scattered(weight_grad(inputs, projected_back, halves, 384))
        sums = (shrink_sum, expand_sum, merging_sum, mixing_sum)
        squares_part = sum(jnp.sum(each * each) for each in sums)
        bias_both = bias_grad[0].reshape(halves, 3, width)
        bias_both = jnp.concatenate([bias_both[:, 0], bias_both[:, 2]], axis=1)
        summed = all_total(stacked(bias_both, jnp.where(lane == 0, squares_part, losses)))
        squares_all = jnp.full((8, 128), summed[12, 0])
    grads = (mixing_sum, merging_sum, expand_sum, shrink_sum)

    def turn(value):
        return value.transpose(1, 0, 2)

    large = (
        turn(mixing_weight),
        turn(mixing_moment),
        turn(mixing_square),
        turn(mixing_average),
        merging_weight.T,
        merging_moment.T,
        merging_square.T,
        merging_average.T,
        expand_weight,
        expand_moment,
        expand_square,
        expand_average,
        shrink_weight.T,
        shrink_moment.T,
        shrink_square.T,
        shrink_average.T,
    )
    both, large_new, scales_new, offsets_new, figures = finish(
        chunk,
        (output, output_head, output_tail.reshape(-1, D), input_back, input_other.reshape(rows, D)),
        large,
        grads,
        (scales_weight, scales_moment, scales_square, scales_average),
        (offsets_weight, offsets_moment, offsets_square, offsets_average),
        summed,
        squares_all,
        step_count,
        queries.shape[0] * lax.axis_size("dp"),
    )
    return (
        (
            both[0].reshape(short_tokens.shape),
            both[1].reshape(long_tokens.shape),
            both[2].reshape(short_tokens.shape),
            both[3].reshape(long_tokens.shape),
            query_gradient,
            figures[1, :1],
            figures[0, :1],
        )
        + tuple(turn(each) for each in large_new[:4])
        + tuple(each.T for each in large_new[4:8])
        + tuple(large_new[8:12])
        + tuple(each.T for each in large_new[12:])
        + tuple(scales_new)
        + tuple(offsets_new)
    )


def solution(mesh):
    placed = (
        P("dp", None, None),
        P("dp", None, None),
        P("dp", None, None),
        P("dp", None, None),
        P("dp"),
        P("dp"),
        P("dp", None),
        P("dp"),
        P(),
        P("dp", None, "tensor"),
        P("dp", None, "tensor"),
        P("dp", None, "tensor"),
        P("dp", None, "tensor"),
        P("tensor", "dp"),
        P("tensor", "dp"),
        P("tensor", "dp"),
        P("tensor", "dp"),
        P("dp", "tensor"),
        P("dp", "tensor"),
        P("dp", "tensor"),
        P("dp", "tensor"),
        P("tensor", "dp"),
        P("tensor", "dp"),
        P("tensor", "dp"),
        P("tensor", "dp"),
        P(),
        P(),
        P(),
        P(),
        P("tensor"),
        P("tensor"),
        P("tensor"),
        P("tensor"),
    )
    return jax.shard_map(
        shards,
        mesh=mesh,
        in_specs=placed,
        out_specs=(
            P("dp", None, None),
            P("dp", None, None),
            P("dp", None, None),
            P("dp", None, None),
            P("dp", None),
            P(),
            P(),
            P("dp", None, "tensor"),
            P("dp", None, "tensor"),
            P("dp", None, "tensor"),
            P("dp", None, "tensor"),
            P("tensor", "dp"),
            P("tensor", "dp"),
            P("tensor", "dp"),
            P("tensor", "dp"),
            P("dp", "tensor"),
            P("dp", "tensor"),
            P("dp", "tensor"),
            P("dp", "tensor"),
            P("tensor", "dp"),
            P("tensor", "dp"),
            P("tensor", "dp"),
            P("tensor", "dp"),
            P(),
            P(),
            P(),
            P(),
            P("tensor"),
            P("tensor"),
            P("tensor"),
            P("tensor"),
        ),
        check_vma=False,
    )
```

```python
import functools
import math

import jax
import jax.numpy as jnp
from jax import lax
from jax.experimental import pallas as pl
from jax.experimental.pallas import tpu as pltpu
from jax.sharding import PartitionSpec as P

D = 768
FF = 3072
HEAD_DIM = 64
PAIR = 2 * HEAD_DIM
MESH = pl.DeviceIdType.MESH

norm_eps = 1e-05
score_scale = 0.125
masked_value = -1e30
first_decay = 0.5
second_decay = 0.75
smooth_decay = 0.75
decay_weight = 0.01
adam_eps = 1e-08
clip_limit = 1.0
inverse_root_two = 0.7071067811865476
inverse_root_tau = 0.3989422804014327
big_vmem = 56 * 1024 * 1024


def dot_nn(a, b):
    return lax.dot_general(a, b, (((1,), (0,)), ((), ())), preferred_element_type=jnp.float32)


def dot_nt(a, b):
    return lax.dot_general(a, b, (((1,), (1,)), ((), ())), preferred_element_type=jnp.float32)


def dot_tn(a, b):
    return lax.dot_general(a, b, (((0,), (0,)), ((), ())), preferred_element_type=jnp.float32)


def layer_stats(resid):
    centre = resid - jnp.mean(resid, axis=-1, keepdims=True)
    rstd = lax.rsqrt(jnp.mean(centre * centre, axis=-1, keepdims=True) + norm_eps)
    return (centre * rstd, rstd)


def layer_back(gradient, normed, rstd, gain):
    scaled = gradient * gain
    return rstd * (
        scaled
        - jnp.mean(scaled, axis=-1, keepdims=True)
        - normed * jnp.mean(scaled * normed, axis=-1, keepdims=True)
    )


def visible_keys(spans, step, rows, piece, key_axis):
    shape = (rows, 1) if key_axis == 0 else (1, rows)
    place = lax.broadcasted_iota(jnp.int32, shape, key_axis)
    segment = place // piece
    limit = jnp.zeros(shape, jnp.int32)
    for index in range(rows // piece):
        limit = jnp.where(segment == index, spans[step, index], limit)
    key_valid = (place % piece) < limit
    first = lax.broadcasted_iota(jnp.int32, (rows, rows), 0) // piece
    second = lax.broadcasted_iota(jnp.int32, (rows, rows), 1) // piece
    return jnp.logical_and(jnp.logical_or(first == second, step > 0), key_valid)


def own_lanes(value, which):
    lane = lax.broadcasted_iota(jnp.int32, value.shape, 1)
    return jnp.where((lane // HEAD_DIM) == which, value, jnp.zeros_like(value))


def join_lanes(low, high):
    lane = lax.broadcasted_iota(jnp.int32, low.shape, 1)
    return jnp.where(lane < HEAD_DIM, low, high)


def attend_half(half, weight, bias, visible, x, qkv_ref, ctx_ref):
    width = weight.shape[1] // 3
    base = half * 3 * width
    projected = dot_nn(x, weight) + bias
    qkv_ref[:, base : base + 3 * width] = projected.astype(jnp.bfloat16)
    for pair in range(width // PAIR):
        at = base + pair * PAIR
        q = qkv_ref[:, at : at + PAIR] * jnp.bfloat16(score_scale)
        k = qkv_ref[:, at + width : at + width + PAIR]
        v = qkv_ref[:, at + 2 * width : at + 2 * width + PAIR]
        parts = []
        for which in range(2):
            scores = jnp.where(visible, dot_nt(own_lanes(q, which), k), masked_value)
            powered = jnp.exp(scores - jnp.max(scores, axis=-1, keepdims=True))
            weights = powered * (1.0 / jnp.sum(powered, axis=-1, keepdims=True))
            parts.append(dot_nn(weights.astype(jnp.bfloat16), v))
        at = half * width + pair * PAIR
        ctx_ref[:, at : at + PAIR] = join_lanes(*parts).astype(jnp.bfloat16)


def attend_forward_kernel(piece, spans, x_ref, w_ref, bias_ref, qkv_ref, ctx_ref):
    step = pl.program_id(0)
    rows = x_ref.shape[0]
    width = w_ref.shape[2] // 3
    visible = visible_keys(spans, step, rows, piece, 1)
    for half in range(w_ref.shape[0]):
        bias = bias_ref[:, half * 3 * width : (half + 1) * 3 * width]
        attend_half(half, w_ref[half], bias, visible, x_ref[...], qkv_ref, ctx_ref)


def feed_up(context, inputs, me_ref, scales_ref, bu_ref, outs):
    hb_ref, g_ref, slope_ref, n1_ref, r1_ref = outs
    wide = bu_ref.shape[1] // 2
    width = me_ref.shape[-1] - wide
    attention = scales_ref[4:5, :]

    def weight(half, columns):
        place = (half,) + (slice(None),) * (len(me_ref.shape) - 2) + (columns,)
        return me_ref[place].reshape(D, -1)

    for half in range(2):
        attention = attention + dot_nt(
            context[:, half * width : (half + 1) * width], weight(half, slice(0, width))
        )
    normed, rstd = layer_stats(inputs.astype(jnp.float32) + attention)
    n1_ref[...] = normed
    r1_ref[...] = rstd
    hidden = normed * scales_ref[0:1, :] + scales_ref[1:2, :]
    hidden_low = hidden.astype(jnp.bfloat16)
    hb_ref[...] = hidden_low
    activated = []
    for half in range(2):
        at = half * wide
        upward = dot_nn(hidden_low, weight(half, slice(width, width + wide))) + bu_ref[:, at : at + wide]
        cumulative = 0.5 * (1.0 + lax.erf(upward * inverse_root_two))
        density = jnp.exp(-0.5 * upward * upward) * inverse_root_tau
        activated.append((upward * cumulative).astype(jnp.bfloat16))
        g_ref[:, at : at + wide] = activated[half]
        slope_ref[:, at : at + wide] = (cumulative + upward * density).astype(jnp.bfloat16)
    return hidden, activated


def feed_down(piece, hidden, activated, st_ref, scales_ref, outs):
    out_ref, n2_ref, r2_ref, lead_ref = outs
    downward = scales_ref[5:6, :]
    for half in range(2):
        wide = st_ref.shape[-1]
        downward = downward + dot_nt(activated[half], st_ref[half].reshape(D, wide))
    normed, rstd = layer_stats(hidden + downward)
    n2_ref[...] = normed
    r2_ref[...] = rstd
    result = (normed * scales_ref[2:3, :] + scales_ref[3:4, :]).astype(jnp.bfloat16)
    out_ref[...] = result
    for index in range(result.shape[0] // piece):
        row = result[index * piece : index * piece + 8].astype(jnp.float32)
        lead_ref[0, index : index + 1, :] = row[:1]


def feed_forward_kernel(
    piece, ctx_ref, x_ref, me_ref, st_ref, scales_ref, bu_ref,
    hb_ref, g_ref, slope_ref, n1_ref, r1_ref, out_ref, n2_ref, r2_ref, lead_ref,
):
    hidden, activated = feed_up(
        ctx_ref[...], x_ref[...], me_ref, scales_ref, bu_ref, (hb_ref, g_ref, slope_ref, n1_ref, r1_ref)
    )
    feed_down(piece, hidden, activated, st_ref, scales_ref, (out_ref, n2_ref, r2_ref, lead_ref))


def add_row(ref, index, value):
    ref[index : index + 1, :] += jnp.sum(value, axis=0, keepdims=True)


def out_back_kernel(
    piece, chunks, short_ref, long_ref, lead_ref, n2_ref, r2_ref, scales_ref, g_ref, dr2_ref, vec_ref, grad_ref, turned_ref
):
    step = pl.program_id(0)

    @pl.when(step == 0)
    def _():
        vec_ref[...] = jnp.zeros_like(vec_ref)

    @pl.when(step < chunks)
    def _():
        dout = jnp.where(step == 0, short_ref[...], long_ref[...]).astype(jnp.float32)
        rows = dout.shape[0]
        row = lax.broadcasted_iota(jnp.int32, dout.shape, 0)
        for index in range(rows // piece):
            dout = dout + jnp.where(row == index * piece, lead_ref[0, index : index + 1, :], 0.0)
        normed = n2_ref[...]
        add_row(vec_ref, 0, dout * normed)
        add_row(vec_ref, 1, dout)
        second = layer_back(dout, normed, r2_ref[...], scales_ref[2:3, :])
        add_row(vec_ref, 2, second)
        dr2_ref[...] = second
        turned_ref[:, pl.ds(pl.multiple_of(step * rows, rows), rows)] = second.astype(jnp.bfloat16).T

    @pl.when(step >= chunks)
    def _():
        grad_ref[0] = dot_nn(turned_ref[...], g_ref[...]).astype(jnp.bfloat16)


def no_progress(point):
    pass


def feed_back_kernel(
    chunks, dr2_ref, n1_ref, r1_ref, slope_ref, hb_ref, ctx_ref, me_ref, st_ref, scales_ref,
    dr1_ref, dctx_ref, vec_ref, up_ref, merging_ref, expand_ref,
    dub_ref, turned_h, turned_a, progress=no_progress,
):
    step = pl.program_id(0)
    rows = dr2_ref.shape[0]
    wide = st_ref.shape[2]
    width = me_ref.shape[2] - wide
    tiles = ctx_ref.shape[1]
    tile = expand_ref.shape[2]
    merging_steps = D // tiles

    @pl.when(step == 0)
    def _():
        vec_ref[...] = jnp.zeros_like(vec_ref)
        up_ref[...] = jnp.zeros_like(up_ref)

    progress(0)

    @pl.when(step < chunks)
    def _():
        place = pl.ds(pl.multiple_of(step * rows, rows), rows)
        hidden_back = dr2_ref[...]
        low = hidden_back.astype(jnp.bfloat16)
        turned_h[:, place] = hb_ref[...].T
        for half in range(st_ref.shape[0]):
            at = half * wide
            upward = dot_nn(low, st_ref[half]) * slope_ref[:, at : at + wide].astype(jnp.float32)
            up_ref[0:1, at : at + wide] += jnp.sum(upward, axis=0, keepdims=True)
            upward_low = upward.astype(jnp.bfloat16)
            dub_ref[place, at : at + wide] = upward_low
            hidden_back = hidden_back + dot_nt(upward_low, me_ref[half, :, width:])
            progress(1 + half)
        normed = n1_ref[...]
        add_row(vec_ref, 0, hidden_back * normed)
        add_row(vec_ref, 1, hidden_back)
        first = layer_back(hidden_back, normed, r1_ref[...], scales_ref[0:1, :])
        add_row(vec_ref, 2, first)
        dr1_ref[...] = first
        low = first.astype(jnp.bfloat16)
        turned_a[:, place] = low.T
        for half in range(me_ref.shape[0]):
            dctx_ref[:, half * width : (half + 1) * width] = dot_nn(
                low, me_ref[half, :, :width]
            ).astype(jnp.bfloat16)

    @pl.when(jnp.logical_and(step >= chunks, step < chunks + merging_steps))
    def _():
        merging_ref[0] = dot_nn(turned_a[...], ctx_ref[...]).astype(jnp.bfloat16)

    @pl.when(step >= chunks + merging_steps)
    def _():
        start = (step - chunks - merging_steps) * tile
        right = dub_ref[:, pl.ds(pl.multiple_of(start, tile), tile)]
        expand_ref[0] = dot_nn(turned_h[...], right).astype(jnp.bfloat16)


def attend_back_kernel(
    piece, spans, qkv_ref, dctx_ref, dr1_ref, w_ref, dproj_ref, dx_ref, bias_ref, low_ref,
    progress=no_progress,
):
    step = pl.program_id(0)

    @pl.when(step == 0)
    def _():
        bias_ref[...] = jnp.zeros_like(bias_ref)

    rows = qkv_ref.shape[0]
    width = w_ref.shape[2] // 3
    visible = visible_keys(spans, step, rows, piece, 0)
    point = 0
    total = dr1_ref[...]
    for half in range(w_ref.shape[0]):
        base = half * 3 * width
        for pair in range(width // PAIR):
            at = base + pair * PAIR
            q = qkv_ref[:, at : at + PAIR]
            k = qkv_ref[:, at + width : at + width + PAIR]
            v = qkv_ref[:, at + 2 * width : at + 2 * width + PAIR]
            near = half * width + pair * PAIR
            back = dctx_ref[:, near : near + PAIR]
            parts = []
            for which in range(2):
                scores = dot_nt(own_lanes(k, which) * jnp.bfloat16(score_scale), q)
                scores = jnp.where(visible, scores, masked_value)
                powered = jnp.exp(scores - jnp.max(scores, axis=0, keepdims=True))
                weights = powered * (1.0 / jnp.sum(powered, axis=0, keepdims=True))
                weight_back = dot_nt(own_lanes(v, which), back)
                score_back = weights * (
                    weight_back - jnp.sum(weights * weight_back, axis=0, keepdims=True)
                )
                score_low = (score_back * score_scale).astype(jnp.bfloat16)
                parts.append(
                    (
                        dot_tn(score_low, k),
                        dot_nn(score_low, q),
                        dot_nn(weights.astype(jnp.bfloat16), back),
                    )
                )
            for part in range(3):
                value = join_lanes(parts[0][part], parts[1][part])
                spot = at + part * width
                if part != 1:
                    bias_ref[0:1, spot : spot + PAIR] += jnp.sum(value, axis=0, keepdims=True)
                dproj_ref[:, spot : spot + PAIR] = value.astype(jnp.bfloat16)
            point += 1
            progress(point)
        total = total + dot_nt(dproj_ref[:, base : base + 3 * width], w_ref[half])
    dx_ref[...] = total
    low_ref[step if low_ref.shape[0] > 1 else 0] = total.astype(jnp.bfloat16)


def weight_grad_kernel(left_ref, right_ref, out_ref, turned_ref):
    @pl.when(pl.program_id(0) == 0)
    def _():
        turned_ref[...] = left_ref[...].T

    out_ref[0] = dot_nn(turned_ref[...], right_ref[...]).astype(jnp.bfloat16)


def weight_grad(left, right, groups, tile):
    rows, depth = left.shape
    columns = right.shape[1]
    per = columns // groups // tile
    return pl.pallas_call(
        weight_grad_kernel,
        grid=(columns // tile,),
        in_specs=[
            pl.BlockSpec((rows, depth), lambda i: (0, 0), pipeline_mode=pl.Buffered(1)),
            pl.BlockSpec((rows, tile), lambda i: (0, i)),
        ],
        out_specs=pl.BlockSpec((1, depth, tile), lambda i: (i // per, 0, i % per)),
        out_shape=jax.ShapeDtypeStruct((groups, depth, columns // groups), jnp.bfloat16),
        scratch_shapes=[pltpu.VMEM((depth, rows), jnp.bfloat16)],
        compiler_params=pltpu.CompilerParams(vmem_limit_bytes=big_vmem),
        cost_estimate=pl.CostEstimate(
            flops=2 * rows * depth * columns,
            bytes_accessed=2 * (rows * depth + rows * columns + depth * columns),
            transcendentals=0,
        ),
        name="weight_grad",
    )(left, right)


def contrast_kernel(
    count, own, halves, cls_ref, q_ref, pos_ref, qg_ref, lead_ref, loss_ref,
    mine_ref, all_ref, part_ref, got_ref, stat_ref, term_ref,
    sem_a, sem_b, sem_c, sem_d, sem_e, sem_f, sem_g, sem_h,
):
    me = lax.axis_index("dp")
    half = lax.axis_index("tensor")
    other = 1 - half
    kind = own // 2
    firsts = [cls_ref[0, :kind, :]] + [cls_ref[1 + index, :1, :] for index in range(kind)]
    mine_ref[...] = jnp.concatenate(firsts, axis=0).astype(jnp.bfloat16)
    barrier = pltpu.get_barrier_semaphore()

    @pl.loop(1, count)
    def _(gap):
        pl.semaphore_signal(
            barrier, inc=1, device_id=(lax.rem(me + gap, count), half), device_id_type=MESH
        )

    pl.semaphore_signal(barrier, inc=1, device_id=(me, other), device_id_type=MESH)
    pl.semaphore_wait(barrier, count)

    def push(source, target, sends, lands, gap):
        peer = lax.rem(me + gap, count)
        return pltpu.make_async_remote_copy(
            src_ref=source(peer),
            dst_ref=target.at[me],
            send_sem=sends.at[gap],
            recv_sem=lands.at[me],
            device_id=(peer, half),
            device_id_type=MESH,
        )

    def landed(source, target, sends, lands, gap):
        origin = lax.rem(me + count - gap, count)
        return pltpu.make_async_remote_copy(
            src_ref=target.at[origin],
            dst_ref=target.at[origin],
            send_sem=sends.at[gap],
            recv_sem=lands.at[origin],
            device_id=(origin, half),
            device_id_type=MESH,
        )

    def whole(peer):
        return mine_ref

    @pl.loop(1, count)
    def _(gap):
        push(whole, all_ref, sem_a, sem_b, gap).start()

    all_ref[me] = mine_ref[...]

    @pl.loop(1, count)
    def _(gap):
        landed(whole, all_ref, sem_a, sem_b, gap).wait_recv()

    passages = all_ref[...].astype(jnp.float32).reshape(count * own, D).astype(jnp.bfloat16)
    queries = q_ref[...]
    logits = dot_nt(queries, passages)
    column = lax.broadcasted_iota(jnp.int32, logits.shape, 1)
    near = column % own
    index = (column // own) * (own * halves) + (near // kind) * (kind * halves)
    index = index + half * kind + near % kind
    query = lax.broadcasted_iota(jnp.int32, logits.shape, 0)
    positive = jnp.zeros(logits.shape, jnp.int32)
    for each in range(logits.shape[0]):
        positive = jnp.where(query == each, pos_ref[each], positive)
    chosen = jnp.where(index == positive, 1.0, 0.0)
    highest = jnp.max(logits, axis=1, keepdims=True)
    summed = jnp.sum(jnp.exp(logits - highest), axis=1, keepdims=True)
    picked = jnp.sum(logits * chosen, axis=1, keepdims=True)
    lane = lax.broadcasted_iota(jnp.int32, (logits.shape[0], 128), 1)
    stat_ref[half] = jnp.where(lane == 0, highest, jnp.where(lane == 1, summed, picked))

    def swap(ref, send, land):
        return pltpu.make_async_remote_copy(
            src_ref=ref.at[half],
            dst_ref=ref.at[half],
            send_sem=send,
            recv_sem=land,
            device_id=(me, other),
            device_id_type=MESH,
        )

    def swapped(ref, send, land):
        return pltpu.make_async_remote_copy(
            src_ref=ref.at[other],
            dst_ref=ref.at[other],
            send_sem=send,
            recv_sem=land,
            device_id=(me, other),
            device_id_type=MESH,
        )

    swap(stat_ref, sem_e, sem_f).start()
    swapped(stat_ref, sem_e, sem_f).wait_recv()
    low, high = stat_ref[0], stat_ref[1]
    top = jnp.maximum(low[:, 0:1], high[:, 0:1])
    total = low[:, 1:2] * jnp.exp(low[:, 0:1] - top) + high[:, 1:2] * jnp.exp(high[:, 0:1] - top)
    losses = top + jnp.log(total) - (low[:, 2:3] + high[:, 2:3])
    loss_ref[...] = jnp.broadcast_to(jnp.sum(losses, axis=0, keepdims=True), loss_ref.shape)
    logit_back = (jnp.exp(logits - top) / total - chosen).astype(jnp.bfloat16)
    terms = dot_tn(logit_back, queries)
    part_ref[...] = terms.reshape(count, own, D).astype(jnp.bfloat16)

    def piece(peer):
        return part_ref.at[peer]

    @pl.loop(1, count)
    def _(gap):
        push(piece, got_ref, sem_c, sem_d, gap).start()

    term_ref[half] = dot_nn(logit_back, passages)
    swap(term_ref, sem_g, sem_h).start()
    got_ref[me] = part_ref[me]
    swapped(term_ref, sem_g, sem_h).wait_recv()
    qg_ref[...] = term_ref[0] + term_ref[1]

    @pl.loop(1, count)
    def _(gap):
        landed(piece, got_ref, sem_c, sem_d, gap).wait_recv()

    lead = jnp.sum(got_ref[...].astype(jnp.float32), axis=0)
    lead_ref[...] = jnp.zeros_like(lead_ref)
    lead_ref[0, :kind, :] = lead[:kind]
    for index in range(kind):
        lead_ref[1 + index, :1, :] = lead[kind + index : kind + index + 1]

    @pl.loop(1, count)
    def _(gap):
        push(whole, all_ref, sem_a, sem_b, gap).wait_send()
        push(piece, got_ref, sem_c, sem_d, gap).wait_send()

    swap(stat_ref, sem_e, sem_f).wait_send()
    swap(term_ref, sem_g, sem_h).wait_send()


def contrast(leading, queries, positives):
    count = lax.axis_size("dp")
    halves = lax.axis_size("tensor")
    own = 2 * (leading.shape[0] - 1)
    here = queries.shape[0]
    whole = pl.BlockSpec(memory_space=pltpu.VMEM)
    query_gradient, lead_back, loss = pl.pallas_call(
        functools.partial(contrast_kernel, count, own, halves),
        in_specs=[whole] * 2 + [pl.BlockSpec(memory_space=pltpu.SMEM)],
        out_specs=[whole] * 3,
        out_shape=[
            jax.ShapeDtypeStruct((here, D), jnp.float32),
            jax.ShapeDtypeStruct(leading.shape, jnp.float32),
            jax.ShapeDtypeStruct((8, 128), jnp.float32),
        ],
        scratch_shapes=[
            pltpu.VMEM((own, D), jnp.bfloat16),
            pltpu.VMEM((count, own, D), jnp.bfloat16),
            pltpu.VMEM((count, own, D), jnp.bfloat16),
            pltpu.VMEM((count, own, D), jnp.bfloat16),
            pltpu.VMEM((halves, here, 128), jnp.float32),
            pltpu.VMEM((halves, here, D), jnp.float32),
            pltpu.SemaphoreType.DMA((count,)),
            pltpu.SemaphoreType.DMA((count,)),
            pltpu.SemaphoreType.DMA((count,)),
            pltpu.SemaphoreType.DMA((count,)),
            pltpu.SemaphoreType.DMA,
            pltpu.SemaphoreType.DMA,
            pltpu.SemaphoreType.DMA,
            pltpu.SemaphoreType.DMA,
        ],
        compiler_params=pltpu.CompilerParams(
            collective_id=1, has_side_effects=True, vmem_limit_bytes=big_vmem
        ),
        name="contrast",
    )(leading, queries, positives)
    return query_gradient, lead_back, loss


def total_kernel(bits, value_ref, out_ref, slots, send_sem, recv_sem):
    me = lax.axis_index("dp")
    half = lax.axis_index("tensor")

    def partner(stage):
        if stage == bits:
            return (me, 1 - half)
        gap = 1 << stage
        up = 1 - 2 * lax.rem(me // gap, 2)
        return (me + up * gap, half)

    barrier = pltpu.get_barrier_semaphore()
    for stage in range(bits + 1):
        pl.semaphore_signal(barrier, inc=1, device_id=partner(stage), device_id_type=MESH)
    pl.semaphore_wait(barrier, bits + 1)
    out_ref[...] = value_ref[...]
    slots[0] = value_ref[...]
    copies = []
    for stage in range(bits + 1):
        copy = pltpu.make_async_remote_copy(
            src_ref=slots.at[2 * stage],
            dst_ref=slots.at[2 * stage + 1],
            send_sem=send_sem.at[stage],
            recv_sem=recv_sem.at[stage],
            device_id=partner(stage),
            device_id_type=MESH,
        )
        copy.start()
        copies.append(copy)
        copy.wait_recv()
        summed = slots[2 * stage] + slots[2 * stage + 1]
        if stage < bits:
            slots[2 * stage + 2] = summed
        else:
            out_ref[...] = summed
    for copy in copies:
        copy.wait_send()


def all_total(value):
    bits = (lax.axis_size("dp") - 1).bit_length()
    whole = pl.BlockSpec(memory_space=pltpu.VMEM)
    return pl.pallas_call(
        functools.partial(total_kernel, bits),
        in_specs=[whole],
        out_specs=whole,
        out_shape=jax.ShapeDtypeStruct(value.shape, value.dtype),
        scratch_shapes=[
            pltpu.VMEM((2 * bits + 2,) + value.shape, value.dtype),
            pltpu.SemaphoreType.DMA((bits + 1,)),
            pltpu.SemaphoreType.DMA((bits + 1,)),
        ],
        compiler_params=pltpu.CompilerParams(collective_id=2, has_side_effects=True),
        name="all_total",
    )(value)


def tensor_swap(value):
    return lax.ppermute(value, "tensor", [(0, 1), (1, 0)])


def gathered(own):
    return lax.all_gather(own, ("tensor", "dp"), axis=0, tiled=True).reshape(
        lax.axis_size("tensor"), -1, own.shape[1]
    )


def scattered(whole):
    return lax.psum_scatter(
        whole.reshape(-1, whole.shape[2]), ("tensor", "dp"), scatter_dimension=0, tiled=True
    ).astype(jnp.float32)


def grid_place():
    me = lax.axis_index("dp")
    return lax.axis_index("tensor"), me // 4, lax.rem(me // 2, 2), lax.rem(me, 2)


def at_place(t, z, x, c):
    return (z * 4 + x * 2 + c, t)


def greet_neighbours(cube=False):
    t, z, x, c = grid_place()
    barrier = pltpu.get_barrier_semaphore()
    others = [at_place(t, lax.rem(z + gap, 4), x, c) for gap in range(1, 4)]
    others += [at_place(1 - t, z, x, c), at_place(t, z, 1 - x, c), at_place(t, z, x, 1 - c)]
    if cube:
        others += [at_place(1 - t, z, 1 - x, c), at_place(1 - t, z, x, 1 - c)]
        others += [at_place(t, z, 1 - x, 1 - c), at_place(1 - t, z, 1 - x, 1 - c)]
    for other in others:
        pl.semaphore_signal(barrier, inc=1, device_id=other, device_id_type=MESH)
    pl.semaphore_wait(barrier, len(others))


class Gather:
    count = 19

    def __init__(self, own, buffer, sends, lands, local, index):
        self.own, self.buffer, self.index = own, buffer, index
        self.sends, self.lands, self.local = sends, lands, local
        t, z, x, c = self.place = grid_place()
        even = c == 0
        self.mid = (jnp.where(even, t, 1 - t), jnp.where(even, 1 - x, x))
        self.last = (jnp.where(even, 1 - t, t), jnp.where(even, x, 1 - x))
        self.both = (1 - t, 1 - x)

    def group(self, spot, c):
        return self.buffer.at[spot[0], :, spot[1], c]

    def slot(self, spot, gap):
        _, z, _, c = self.place
        return self.buffer.at[spot[0], lax.rem(z + 4 - gap, 4), spot[1], c]

    def copy(self, source, target, which, device):
        return pltpu.make_async_remote_copy(
            src_ref=source,
            dst_ref=target,
            send_sem=self.sends.at[self.index, which],
            recv_sem=self.lands.at[self.index, which],
            device_id=device,
            device_id_type=MESH,
        )

    def outgoing(self, which):
        t, z, x, c = self.place
        here = (t, x)
        middle = at_place(self.mid[0], z, self.mid[1], c)
        last = at_place(self.last[0], z, self.last[1], c)
        if which < 3:
            device = at_place(t, lax.rem(z + which + 1, 4), x, c)
            return self.copy(self.own, self.slot(here, 0), which, device)
        if which < 5:
            return self.copy(self.own, self.slot(here, 0), which, (middle, last)[which - 3])
        if which < 11:
            slot = self.slot(here, (which - 5) % 3 + 1)
            return self.copy(slot, slot, which, middle if which < 8 else last)
        if which < 15:
            slot = self.slot(self.mid, which - 11)
            return self.copy(slot, slot, which, last)
        group = self.group((here, self.mid, self.last, self.both)[which - 15], c)
        return self.copy(group, group, which, at_place(t, z, x, 1 - c))

    def arrived(self, which):
        t, z, x, c = self.place
        if which < 3:
            target = self.slot((t, x), which + 1)
        elif which < 5:
            target = self.slot((self.mid, self.last)[which - 3], 0)
        elif which < 11:
            target = self.slot(self.mid if which < 8 else self.last, (which - 5) % 3 + 1)
        elif which < 15:
            target = self.slot(self.both, which - 11)
        else:
            target = self.group(((t, x), self.last, self.mid, self.both)[which - 15], 1 - c)
        self.copy(target, target, which, at_place(t, z, x, 1 - c)).wait_recv()

    def keep(self):
        t, z, x, c = self.place
        return pltpu.make_async_copy(self.own, self.slot((t, x), 0), self.local.at[self.index])

    def start(self):
        self.keep().start()
        for which in (0, 2, 1, 3, 4):
            self.outgoing(which).start()

    def line_part(self, gap):
        self.arrived(gap)
        self.outgoing(5 + gap).start()
        self.outgoing(8 + gap).start()

    def line_kept(self):
        self.keep().wait()
        self.outgoing(15).start()

    def line_ready(self):
        for gap in (0, 2, 1):
            self.line_part(gap)
        self.line_kept()

    def middle_ready(self):
        self.arrived(3)
        self.outgoing(11).start()
        for gap in (0, 2, 1):
            self.arrived(5 + gap)
            self.outgoing(12 + gap).start()
        self.outgoing(16).start()

    def last_ready(self):
        for which in (4, 8, 10, 9):
            self.arrived(which)
        self.outgoing(17).start()

    def both_ready(self):
        for which in range(11, 15):
            self.arrived(which)
        self.outgoing(18).start()

    def finish(self):
        for which in range(15, 19):
            self.arrived(which)

    def drain(self):
        for which in range(self.count):
            self.outgoing(which).wait_send()


def forward_gather_kernel(
    piece, chunks, spans, mixing_ref, middle_ref, shrink_ref, offsets_ref, scales_ref, short_ref, long_ref,
    qkv_ref, ctx_ref, hb_ref, g_ref, slope_ref, n1_ref, r1_ref, out_ref, n2_ref, r2_ref, lead_ref,
    mixing_out, middle_out, shrink_out,
    w_ref, me_ref, st_ref, both_ref, flat_ref, up_ref, ctx_all, g_all, hidden_all,
    sends, lands, local, swap_send, swap_land, stores,
):
    step = pl.program_id(0)
    t, z, x, c = grid_place()
    mixing, middle, shrink = (
        Gather(own, full, sends, lands, local, index)
        for index, (own, full) in enumerate(
            ((mixing_ref, w_ref), (middle_ref, me_ref), (shrink_ref, st_ref))
        )
    )

    def swap(which):
        return pltpu.make_async_remote_copy(
            src_ref=both_ref.at[which],
            dst_ref=both_ref.at[which],
            send_sem=swap_send,
            recv_sem=swap_land,
            device_id=at_place(1 - t, z, x, c),
            device_id_type=MESH,
        )

    def store(index):
        target = (mixing_out, middle_out, shrink_out)[index]
        return pltpu.make_async_copy((w_ref, me_ref, st_ref)[index], target, stores.at[index])

    rows = long_ref.shape[0]
    width = w_ref.shape[5] // 3

    def tokens(first):
        return jnp.where(step == first, short_ref[...], long_ref[...])


    @pl.when(step == 0)
    def _():
        both_ref[t] = offsets_ref[...]
        greet_neighbours()
        mixing.start()
        swap(t).start()
        middle.start()
        shrink.start()
        mixing.line_ready()
        mixing.middle_ready()
        mixing.last_ready()
        middle.line_part(0)
        mixing.both_ready()
        mixing.finish()
        store(0).start()
        middle.line_part(2)
        middle.line_part(1)
        middle.line_kept()
        swap(1 - t).wait_recv()
        for half in range(2):
            flat_ref[half] = jnp.concatenate(
                [both_ref[half, index : index + 1, :] for index in range(both_ref.shape[1])], axis=1
            )
            wide = up_ref.shape[1] // 2
            up_ref[:, half * wide : (half + 1) * wide] = flat_ref[half][:, 2 * width :]

    @pl.when(step == 2)
    def _():
        middle.middle_ready()

    @pl.when(step == chunks - 1)
    def _():
        shrink.line_ready()
        middle.last_ready()

    @pl.when(step == chunks)
    def _():
        middle.both_ready()
        middle.finish()
        store(1).start()

    @pl.when(step == chunks + 1)
    def _():
        shrink.middle_ready()

    @pl.when(step == 2 * chunks - 2)
    def _():
        shrink.last_ready()

    @pl.when(step == 2 * chunks)
    def _():
        shrink.both_ready()
        shrink.finish()
        store(2).start()

    def here(first):
        return pl.ds(pl.multiple_of((step - first) * rows, rows), rows)

    @pl.when(step < chunks)
    def _():
        visible = visible_keys(spans, step, rows, piece, 1)
        for half in range(2):
            weight = w_ref[half].reshape(D, 3 * width)
            bias = flat_ref[half]
            bias = jnp.concatenate(
                [bias[:, :width], jnp.zeros((1, width), jnp.float32), bias[:, width : 2 * width]],
                axis=1,
            )
            attend_half(half, weight, bias, visible, tokens(0), qkv_ref, ctx_ref)
        ctx_all[here(0), :] = ctx_ref[...]

    @pl.when(jnp.logical_and(step >= chunks, step < 2 * chunks))
    def _():
        outs = (hb_ref, g_ref, slope_ref, n1_ref, r1_ref)
        place = here(chunks)
        hidden, activated = feed_up(ctx_all[place, :], tokens(chunks), me_ref, scales_ref, up_ref, outs)
        hidden_all[place, :] = hidden
        for half in range(2):
            wide = st_ref.shape[5]
            g_all[place, half * wide : (half + 1) * wide] = activated[half]

    @pl.when(step >= 2 * chunks)
    def _():
        place = here(2 * chunks)
        wide = st_ref.shape[5]
        activated = [g_all[place, half * wide : (half + 1) * wide] for half in range(2)]
        outs = (out_ref, n2_ref, r2_ref, lead_ref)
        feed_down(piece, hidden_all[place, :], activated, st_ref, scales_ref, outs)

    @pl.when(step == pl.num_programs(0) - 1)
    def _():
        swap(t).wait_send()
        for each in (mixing, middle, shrink):
            each.drain()
        for index in range(3):
            store(index).wait()


def forward_gather(piece, spans, short_rows, long_rows, owns, offsets, scales, chunk, chunks):
    rows = chunks * chunk
    halves = lax.axis_size("tensor")
    columns = halves * owns[0].shape[1]
    anywhere = pl.BlockSpec(memory_space=pl.ANY)
    bf16, f32 = jnp.bfloat16, jnp.float32

    def buffer(own):
        return (halves, 4, 2, 2) + own.shape

    def spec(width, first):
        return pl.BlockSpec((chunk, width), lambda i: (jnp.clip(i - first * chunks, 0, chunks - 1), 0))

    shapes = [(columns, bf16, 0), (D, bf16, 0)]
    shapes += [(D, bf16, 1), (FF, bf16, 1), (FF, bf16, 1), (D, f32, 1), (1, f32, 1)]
    shapes += [(D, bf16, 2), (D, f32, 2), (1, f32, 2)]
    outs = pl.pallas_call(
        functools.partial(forward_gather_kernel, piece, chunks),
        grid=(3 * chunks,),
        in_specs=[
            pl.BlockSpec(memory_space=pltpu.SMEM),
            *(full_spec(own.shape) for own in owns),
            full_spec((offsets.shape[0] // 128, 128)),
            full_spec(scales.shape),
            *half_specs(chunk, chunks, lambda i: jnp.minimum(i, 2 * chunks - 1) % chunks),
        ],
        out_specs=[spec(width, first) for width, _, first in shapes]
        + [pl.BlockSpec((1, 8, D), lambda i: (jnp.maximum(i - 2 * chunks, 0), 0, 0))]
        + [anywhere] * 3,
        out_shape=[jax.ShapeDtypeStruct((rows, width), dtype) for width, dtype, _ in shapes]
        + [jax.ShapeDtypeStruct((chunks, 8, D), f32)]
        + [jax.ShapeDtypeStruct(buffer(own), bf16) for own in owns],
        scratch_shapes=[pltpu.VMEM(buffer(own), bf16) for own in owns]
        + [
            pltpu.VMEM((halves, offsets.shape[0] // 128, 128), f32),
            pltpu.VMEM((halves, 1, offsets.shape[0]), f32),
            pltpu.VMEM((1, FF), f32),
            pltpu.VMEM((rows, D), bf16),
            pltpu.VMEM((rows, FF), bf16),
            pltpu.VMEM((rows, D), f32),
            pltpu.SemaphoreType.DMA((3, Gather.count)),
            pltpu.SemaphoreType.DMA((3, Gather.count)),
            pltpu.SemaphoreType.DMA((3,)),
            pltpu.SemaphoreType.DMA,
            pltpu.SemaphoreType.DMA,
            pltpu.SemaphoreType.DMA((3,)),
        ],
        compiler_params=pltpu.CompilerParams(
            collective_id=3, has_side_effects=True, vmem_limit_bytes=big_vmem
        ),
        name="forward_gather",
    )(spans, *owns, offsets.reshape(-1, 128), scales, short_rows, long_rows)
    fulls = [full.reshape(halves, -1, full.shape[-1]) for full in outs[-3:]]
    return outs[:2], outs[2:-3], fulls


class Scatter:
    def __init__(self, whole, acc, sib, one, two, line, out, sends, lands, local, index):
        self.whole, self.acc, self.sib, self.out, self.index = whole, acc, sib, out, index
        self.one, self.two, self.line = one, two, line
        self.sends, self.lands, self.local = sends, lands, local
        t, z, x, c = self.place = grid_place()
        even = c == 0
        self.first = (jnp.where(even, 1 - t, t), jnp.where(even, x, 1 - x))
        self.second = (jnp.where(even, t, 1 - t), jnp.where(even, 1 - x, x))
        self.order = (2, 1, 0, 3)
        self.spots = (self.first, (1 - t, 1 - x), self.second, (t, x))

    def copy(self, source, target, which, device):
        return pltpu.make_async_remote_copy(
            src_ref=source,
            dst_ref=target,
            send_sem=self.sends.at[self.index, which],
            recv_sem=self.lands.at[self.index, which],
            device_id=device,
            device_id_type=MESH,
        )

    def outgoing(self, which):
        t, z, x, c = self.place
        if which < 4:
            spot = self.spots[self.order[which]]
            return self.copy(
                self.whole.at[spot[0], :, spot[1], 1 - c],
                self.sib.at[spot[0], :, spot[1]],
                which,
                at_place(t, z, x, 1 - c),
            )
        if which < 6:
            spot = self.spots[which - 4]
            device = at_place(self.first[0], z, self.first[1], c)
            return self.copy(self.acc.at[spot[0], :, spot[1]], self.one.at[which - 4], which, device)
        if which == 6:
            spot = self.second
            device = at_place(spot[0], z, spot[1], c)
            return self.copy(self.acc.at[spot[0], :, spot[1]], self.two, which, device)
        there = lax.rem(z + which - 6, 4)
        return self.copy(
            self.acc.at[t, there, x], self.line.at[which - 7], which, at_place(t, there, x, c)
        )

    def arrived(self, which):
        t, z, x, c = self.place
        if which < 4:
            spot = self.spots[which]
            target = self.sib.at[spot[0], :, spot[1]]
        elif which < 6:
            target = self.one.at[which - 4]
        elif which == 6:
            target = self.two
        else:
            target = self.line.at[which - 7]
        self.copy(target, target, which, at_place(t, z, x, 1 - c)).wait_recv()

    def load(self, which):
        c = self.place[3]
        spot = self.spots[which]
        return pltpu.make_async_copy(
            self.whole.at[spot[0], :, spot[1], c],
            self.acc.at[spot[0], :, spot[1]],
            self.local.at[self.index, which],
        )

    def add(self, spot, read):
        @pl.loop(0, 4)
        def _(z):
            low = self.acc[spot[0], z, spot[1]].astype(jnp.float32)
            low = low + read(z).astype(jnp.float32)
            self.acc[spot[0], z, spot[1]] = low.astype(jnp.bfloat16)

    def start(self):
        for which in range(4):
            self.outgoing(which).start()
            self.load(which).start()

    def cores_ready(self):
        for which in range(4):
            spot = self.spots[which]
            self.arrived(which)
            self.load(which).wait()
            self.add(spot, lambda z: self.sib[spot[0], z, spot[1]])
            if which < 2:
                self.outgoing(4 + which).start()

    def first_ready(self):
        self.arrived(5)
        self.add(self.second, lambda z: self.one[1, z])
        self.outgoing(6).start()
        self.arrived(4)
        self.add(self.spots[3], lambda z: self.one[0, z])

    def second_ready(self):
        self.arrived(6)
        self.add(self.spots[3], lambda z: self.two[z])
        for which in range(7, 10):
            self.outgoing(which).start()

    def finish(self):
        t, z, x, c = self.place
        total = self.acc[t, z, x].astype(jnp.float32)
        for which in range(7, 10):
            self.arrived(which)
            total = total + self.line[which - 7].astype(jnp.float32)
        self.out[...] = total
        return jnp.sum(total * total, axis=0, keepdims=True)

    def drain(self):
        for which in range(10):
            self.outgoing(which).wait_send()


class LateScatter(Scatter):
    def __init__(self, *args):
        super().__init__(*args)
        _, _, x, _ = self.place
        self.order = (0, 1, 2, 3)
        self.spots = ((0, 1 - x), (1, 1 - x), (0, x), (1, x))

    def outgoing(self, which):
        t, z, x, c = self.place
        if which < 4:
            return super().outgoing(which)
        if which < 6:
            side = which - 4
            return self.copy(
                self.acc.at[side, :, 1 - x], self.one.at[side], which, at_place(t, z, 1 - x, c)
            )
        if which == 6:
            return self.copy(self.acc.at[1 - t, z, x], self.two, which, at_place(1 - t, z, x, c))
        there = lax.rem(z + which - 6, 4)
        return self.copy(
            self.acc.at[:, there, x], self.line.at[which - 7], which, at_place(t, there, x, c)
        )

    def first_ready(self):
        for side in range(2):
            self.arrived(4 + side)
            self.add((side, self.place[2]), lambda z: self.one[side, z])
        for which in range(7, 10):
            self.outgoing(which).start()

    def second_ready(self):
        t, z, x, _ = self.place
        for which in range(7, 10):
            self.arrived(which)

        def total(side):
            value = self.acc[side, z, x].astype(jnp.float32)
            for which in range(3):
                value = value + self.line[which, side].astype(jnp.float32)
            return value

        self.acc[1 - t, z, x] = total(1 - t).astype(jnp.bfloat16)
        self.outgoing(6).start()
        self.out[...] = total(t)

    def finish(self):
        self.arrived(6)
        total = self.out[...] + self.two[...].astype(jnp.float32)
        self.out[...] = total
        return jnp.sum(total * total, axis=0, keepdims=True)


class Total:
    def __init__(self, slots, line, sends, lands):
        self.slots, self.line, self.sends, self.lands = slots, line, sends, lands
        t, z, x, c = self.place = grid_place()
        self.partners = (at_place(t, z, x, 1 - c), at_place(t, z, 1 - x, c), at_place(1 - t, z, x, c))

    def pair(self, stage):
        return pltpu.make_async_remote_copy(
            src_ref=self.slots.at[2 * stage],
            dst_ref=self.slots.at[2 * stage + 1],
            send_sem=self.sends.at[stage],
            recv_sem=self.lands.at[stage],
            device_id=self.partners[stage],
            device_id_type=MESH,
        )

    def along(self, gap):
        t, z, x, c = self.place
        return pltpu.make_async_remote_copy(
            src_ref=self.line.at[z],
            dst_ref=self.line.at[z],
            send_sem=self.sends.at[2 + gap],
            recv_sem=self.lands.at[2 + gap],
            device_id=at_place(t, lax.rem(z + gap, 4), x, c),
            device_id_type=MESH,
        )

    def landed(self, gap):
        t, z, x, c = self.place
        spot = self.line.at[lax.rem(z + 4 - gap, 4)]
        pltpu.make_async_remote_copy(
            src_ref=spot,
            dst_ref=spot,
            send_sem=self.sends.at[2 + gap],
            recv_sem=self.lands.at[2 + gap],
            device_id=self.partners[0],
            device_id_type=MESH,
        ).wait_recv()

    def start(self, value):
        self.slots[0] = value
        self.pair(0).start()

    def advance(self, stage):
        self.pair(stage).wait_recv()
        summed = self.slots[2 * stage] + self.slots[2 * stage + 1]
        if stage < 2:
            self.slots[2 * stage + 2] = summed
            self.pair(stage + 1).start()
            return
        z = self.place[1]
        self.line[z] = summed
        for gap in range(1, 4):
            self.along(gap).start()

    def finish(self):
        for gap in range(1, 4):
            self.landed(gap)
        return (self.line[0] + self.line[1]) + (self.line[2] + self.line[3])

    def drain(self):
        for stage in range(3):
            self.pair(stage).wait_send()
        for gap in range(1, 4):
            self.along(gap).wait_send()


class Cube:
    def __init__(self, slots, line, sends, lands):
        self.slots, self.line, self.sends, self.lands = slots, line, sends, lands
        self.place = grid_place()

    def turned(self, flip):
        t, _, x, c = self.place
        return (1 - t if flip & 4 else t), (1 - x if flip & 2 else x), (1 - c if flip & 1 else c)

    def copy(self, slot, which, device):
        return pltpu.make_async_remote_copy(
            src_ref=slot,
            dst_ref=slot,
            send_sem=self.sends.at[which],
            recv_sem=self.lands.at[which],
            device_id=device,
            device_id_type=MESH,
        )

    def slot(self, flip):
        t, x, c = self.turned(flip)
        return self.slots.at[t * 4 + x * 2 + c]

    def push(self, flip):
        t, x, c = self.turned(flip)
        return self.copy(self.slot(0), flip - 1, at_place(t, self.place[1], x, c))

    def along(self, gap, back=False):
        t, z, x, c = self.place
        slot = self.line.at[lax.rem(z + 4 - gap, 4) if back else z]
        return self.copy(slot, 6 + gap, at_place(t, lax.rem(z + gap, 4), x, c))

    def total(self, value):
        t, z, x, c = self.place
        self.slots[t * 4 + x * 2 + c] = value
        for flip in range(1, 8):
            self.push(flip).start()
        for flip in range(1, 8):
            self.copy(self.slot(flip), flip - 1, self.place_of(flip)).wait_recv()
        self.line[z] = jnp.sum(self.slots[...], axis=0)
        for gap in range(1, 4):
            self.along(gap).start()
        for gap in range(1, 4):
            self.along(gap, True).wait_recv()
        return (self.line[0] + self.line[1]) + (self.line[2] + self.line[3])

    def place_of(self, flip):
        t, x, c = self.turned(flip)
        return at_place(t, self.place[1], x, c)

    def drain(self):
        for flip in range(1, 8):
            self.push(flip).wait_send()
        for gap in range(1, 4):
            self.along(gap).wait_send()


def scatter_buffers(whole, columns, late=False):
    halves = lax.axis_size("tensor")
    rows = whole.shape[1] // lax.axis_size("dp")
    two, line = ((), (3, halves)) if late else ((4,), (3,))
    shapes = ((halves, 4, 2), (halves, 4, 2), (2, 4), two, line)
    return [pltpu.VMEM(shape + (rows, columns), jnp.bfloat16) for shape in shapes]


def scatter_parts(pieces, buffers, sems, kind=Scatter):
    return [
        kind(
            whole.at[:, :, :, :, :, first : first + columns],
            *buffers[5 * index : 5 * index + 5],
            out.at[:, first : first + columns],
            *sems,
            index,
        )
        for index, (whole, out, first, columns) in enumerate(pieces)
    ]


def scatter_sems(count):
    return [
        pltpu.SemaphoreType.DMA((count, 10)),
        pltpu.SemaphoreType.DMA((count, 10)),
        pltpu.SemaphoreType.DMA((count, 4)),
    ]


def scatter_input(whole):
    return whole.reshape(lax.axis_size("tensor"), 4, 2, 2, -1, whole.shape[2])


def scatter_shape(whole):
    return jax.ShapeDtypeStruct((whole.shape[1] // lax.axis_size("dp"), whole.shape[2]), jnp.float32)


def push_partner(source, target, index, sends, lands):
    t, z, x, c = grid_place()
    return pltpu.make_async_remote_copy(
        src_ref=source.at[index],
        dst_ref=target.at[index],
        send_sem=sends.at[index],
        recv_sem=lands.at[index],
        device_id=at_place(1 - t, z, x, c),
        device_id_type=MESH,
    )


class Plan:
    def __init__(self, actions, times):
        self.at, self.rest = {}, []
        points = sorted(times.items(), key=lambda item: item[1])
        at = 0
        for due, action in sorted(actions, key=lambda item: item[0]):
            while at < len(points) and points[at][1] < due:
                at += 1
            if at < len(points):
                self.at.setdefault(points[at][0], []).append(action)
            else:
                self.rest.append(action)

    def run(self, point):
        for (step, where), actions in self.at.items():
            if where == point:

                @pl.when(pl.program_id(0) == step)
                def _():
                    for action in actions:
                        action()

    def finish(self):
        for action in self.rest:
            action()


def scatter_actions(parts, ready, link, ended=lambda part: part.finish):
    actions = []
    for index, part in enumerate(parts):
        due = ready + link * index
        actions += [
            (due, part.cores_ready),
            (due + link + 2, part.first_ready),
            (due + 2 * link + 4, part.second_ready),
            (due + 2 * link + 47, ended(part)),
        ]
    return actions


def feed_back_scatter_kernel(chunks, early, columns, whole_ref, tail_ref, *refs):
    ins, outs, (tail_out, out_ref) = refs[:9], refs[9:15], refs[15:17]
    scratch, rest = refs[17:20], refs[20:]
    count = whole_ref.shape[5] // columns
    buffers, sems, (sends, lands) = rest[: 5 * count], rest[5 * count : 5 * count + 3], rest[5 * count + 3 :]
    parts = scatter_parts(
        [(whole_ref, out_ref, index * columns, columns) for index in range(count)], buffers, sems, LateScatter
    )

    def begin():
        greet_neighbours()
        for part in parts:
            part.start()
        for index in range(early):
            push_partner(tail_ref.at[chunks - early :], tail_out, index, sends, lands).start()

    actions = [(0, begin)] + scatter_actions(parts, 8, 6.6)
    steps = chunks + D // ins[5].shape[1] + 2 * (ins[7].shape[2] // outs[5].shape[2])
    times = {(step, 0): 4 + 5.3 * step for step in range(chunks)}
    times |= {(step, 0): 30.5 + 1.7 * (step - chunks) for step in range(chunks, steps)}
    times |= {(step, 1 + half): 6 + 5.3 * step + 2 * half for step in range(chunks) for half in range(2)}
    times[(0, 0)] = 0
    plan = Plan(actions, times)
    feed_back_kernel(chunks, *ins, *outs, *scratch, plan.run)

    @pl.when(pl.program_id(0) == pl.num_programs(0) - 1)
    def _():
        plan.finish()
        for part in parts:
            part.drain()
        for index in range(early):
            push_partner(tail_ref.at[chunks - early :], tail_out, index, sends, lands).wait()


def attend_last_kernel(piece, chunks, columns, spans, one_ref, two_ref, *refs):
    ins, short_ref, long_ref, done_ref = refs[:4], *refs[4:7]
    first_ref, second_ref, upward_ref, loss_ref = refs[7:11]
    refs = refs[1:]
    dx_ref, low_out, one_out, two_out, last_out, total_ref, norm_ref = refs[10:17]
    dproj_ref, bias_ref, turned_ref, grad_ref, square_ref, low_ref, sends, lands = refs[17:25]
    rest = refs[25:]
    count = one_ref.shape[5] // columns + 1
    late = scatter_parts(
        [(one_ref, one_out, index * columns, columns) for index in range(count - 1)]
        + [(two_ref, two_out, 0, columns)],
        rest[: 5 * count],
        rest[5 * count : 5 * count + 3],
        LateScatter,
    )
    rest = rest[5 * count + 3 :]
    tail = grad_ref.shape[5] // columns
    last = scatter_parts(
        [(grad_ref, last_out, index * columns, columns) for index in range(tail)],
        rest[: 5 * tail],
        rest[5 * tail : 5 * tail + 3],
    )
    rest = rest[5 * tail + 3 :]
    vector, norm = Total(*rest[:4]), Cube(*rest[4:])
    step = pl.program_id(0)

    def begin():
        greet_neighbours(True)
        for part in late:
            part.start()
        square_ref[...] = jnp.zeros_like(square_ref)
        turned_ref[:, : short_ref.shape[0]] = short_ref[...].T
        turned_ref[:, short_ref.shape[0] :] = long_ref[...].T

    def ended(part):
        def action():
            square_ref[0:1, :] += part.finish()

        return action

    actions = [(0, begin)] + scatter_actions(late, 8, 6.6, ended)
    actions += scatter_actions(last, 46, 5, ended)
    actions += [(46.5, lambda: vector.advance(0)), (50, lambda: vector.advance(1)), (57, lambda: vector.advance(2))]
    times = {(step, point): 4 + 7.3 * step + 1.15 * point for step in range(chunks) for point in range(7)}
    times |= {(chunks + tile, 0): 41 + 2.0 * tile for tile in range(2 * tail)}
    times[(0, 0)] = 0
    plan = Plan(actions, times)
    plan.run(0)

    @pl.when(step < chunks)
    def _():
        rows = dx_ref.shape[0]
        here = dproj_ref.at[pl.ds(pl.multiple_of(step * rows, rows), rows), :]
        attend_back_kernel(piece, spans, *ins, here, dx_ref, bias_ref, low_ref, plan.run)

    for index in range(chunks):

        @pl.when(step == index)
        def _():
            if index == chunks - 1:
                base = bias_ref.shape[1] // 2
                wide = upward_ref.shape[1] // 2
                lines = [first_ref[0:2, :], second_ref[0:2, :], first_ref[2:3, :], second_ref[2:3, :]]
                for half in range(2):
                    at = half * base
                    pair = [bias_ref[0:1, at : at + columns]]
                    pair += [bias_ref[0:1, at + 2 * columns : at + 3 * columns]]
                    lines.append(jnp.concatenate(pair, axis=1))
                    lines += [
                        upward_ref[0:1, half * wide + first : half * wide + first + D]
                        for first in range(0, wide, D)
                    ]
                column = lax.broadcasted_iota(jnp.int32, (1, D), 1)
                lines.append(jnp.where(column == 1, loss_ref[0:1, 0:1], 0.0))
                lines.append(jnp.zeros((3, D), jnp.float32))
                pack = jnp.concatenate(lines, axis=0)
                vector.start(pack)
            push_partner(low_ref, low_out, index, sends, lands).start()

    @pl.when(step >= chunks)
    def _():
        tile = step - chunks
        half, piece_index = lax.rem(tile, 2), lax.div(tile, 2)
        start = pl.multiple_of((half * tail + piece_index) * columns, columns)
        grad = dot_nn(turned_ref[...], dproj_ref[:, pl.ds(start, columns)]).astype(jnp.bfloat16)
        start = pl.multiple_of(piece_index * columns, columns)
        grad_ref[half, :, :, :, :, pl.ds(start, columns)] = grad.reshape(
            grad_ref.shape[1:5] + (columns,)
        )

    for index, part in enumerate(last):

        @pl.when(step == chunks + 2 * index + 1)
        def _():
            part.start()

    @pl.when(step == pl.num_programs(0) - 1)
    def _():
        plan.finish()
        total_ref[...] = vector.finish()
        squares = jnp.sum(square_ref[...]) + jnp.sum(done_ref[...] * done_ref[...])
        norm_ref[...] = norm.total(jnp.full(norm_ref.shape, squares))
        for each in late + last + [vector, norm]:
            each.drain()
        for index in range(chunks):
            push_partner(low_ref, low_out, index, sends, lands).wait()


def adam(weight, moment, square, average, gradient, rate, scalars):
    factor, first_fix, second_fix = scalars
    clipped = gradient * factor
    first = first_decay * moment + (1.0 - first_decay) * clipped
    second = second_decay * square + (1.0 - second_decay) * clipped * clipped
    master = weight - rate * (
        first / first_fix / (jnp.sqrt(second / second_fix) + adam_eps) + decay_weight * weight
    )
    smooth = smooth_decay * average + (1.0 - smooth_decay) * master
    return master, first, second, smooth


def finish_kernel(chunk, chunks, rates, passages, halves, *refs):
    out_own, out_head, out_tail, dx_own, dx_other = refs[:5]
    large, grads = refs[5:21], refs[21:25]
    scales_refs, offsets_refs, total_ref, norm_ref, step_ref = refs[25:29], refs[29:33], *refs[33:36]
    short_out, long_out, short_dx, long_dx = refs[36:40]
    large_outs, scales_outs, offsets_outs, figures_ref = refs[40:56], refs[56:60], refs[60:64], refs[64]
    scratch = refs[65:]
    ins, outs = scratch[:16], scratch[16:32]
    rows_ref, own_ref, low_ref, wide_ref, in_sems, out_sems, block_sems, wide_sems, load_sems = scratch[32:]
    place = lax.axis_index("tensor")
    longs = chunks - 1

    def rows(first, count):
        return pl.ds(pl.multiple_of(first * chunk, chunk), count * chunk)

    ahead = out_head.shape[0] // chunk
    other = 1 - place
    brought = [
        pltpu.make_async_copy(source, target, load_sems.at[k])
        for k, (source, target) in enumerate(
            (
                (dx_other, low_ref),
                (out_own, rows_ref.at[rows(0, chunks)]),
                (out_head, rows_ref.at[rows(chunks, ahead)]),
                (out_tail, rows_ref.at[rows(chunks + ahead, chunks - ahead)]),
                (dx_own, own_ref),
            )
        )
    ]
    for load in brought:
        load.start()
    loads = [pltpu.make_async_copy(large[k], ins[k], in_sems.at[k]) for k in range(16)]
    for load in loads:
        load.start()
    blocks = [
        (rows_ref.at[rows(0, 1)], short_out.at[rows(place, 1)]),
        (rows_ref.at[rows(1, longs)], long_out.at[rows(place * longs, longs)]),
        (rows_ref.at[rows(chunks, 1)], short_out.at[rows(other, 1)]),
        (rows_ref.at[rows(chunks + 1, longs)], long_out.at[rows(other * longs, longs)]),
        (own_ref.at[rows(0, 1)], short_dx.at[rows(place, 1)]),
        (own_ref.at[rows(1, longs)], long_dx.at[rows(place * longs, longs)]),
    ]
    copies = [
        pltpu.make_async_copy(source, target, block_sems.at[k])
        for k, (source, target) in enumerate(blocks)
    ]
    brought[0].wait()
    for index in range(chunks):
        wide_ref[index] = low_ref[rows(index, 1), :].astype(jnp.float32)
        target = short_dx.at[rows(other, 1)]
        if index > 0:
            target = long_dx.at[rows(other * longs + index - 1, 1)]
        copy = pltpu.make_async_copy(wide_ref.at[index], target, wide_sems.at[index])
        copy.start()
        copies.append(copy)
    for load in brought[1:]:
        load.wait()
    for copy in copies[:6]:
        copy.start()

    sums = total_ref[...]
    row = lax.broadcasted_iota(jnp.int32, sums.shape, 0)
    column = lax.broadcasted_iota(jnp.int32, sums.shape, 1)

    def whole_sum(value):
        return jnp.sum(jnp.sum(value, axis=1, keepdims=True), axis=0, keepdims=True)

    squares = norm_ref[0:1, 0:1] + whole_sum(jnp.where(row < 12, sums * sums, 0.0))
    loss = whole_sum(jnp.where(jnp.logical_and(row == 12, column == 1), sums, 0.0))
    norm = jnp.sqrt(squares)
    factor = clip_limit / jnp.maximum(norm, clip_limit)
    steps = jnp.full((1, 1), step_ref[0], jnp.int32).astype(jnp.float32)
    first_fix = 1.0 - jnp.exp(steps * math.log(first_decay))
    second_fix = 1.0 - jnp.exp(steps * math.log(second_decay))
    scalars = (factor, first_fix, second_fix)
    figure = lax.broadcasted_iota(jnp.int32, figures_ref.shape, 0)
    figures_ref[...] = jnp.where(figure == 0, norm, loss / (halves * passages))
    for each in range(4):
        values = []
        for k in range(4 * each, 4 * each + 4):
            loads[k].wait()
            values.append(ins[k][...])
        gradient = grads[each][...]
        if values[0].ndim == 3:
            width = values[0].shape[2]
            gradient = jnp.stack([gradient[:, k * width : (k + 1) * width] for k in range(3)])
        fixed = [one.reshape((1,) * values[0].ndim) for one in scalars]
        new = adam(*values, gradient, rates[each], fixed)
        for part in range(4):
            k = 4 * each + part
            outs[k][...] = new[part]
            copy = pltpu.make_async_copy(outs[k], large_outs[k], out_sems.at[k])
            copy.start()
            copies.append(copy)
    new = adam(*(ref[...] for ref in scales_refs), sums[:6], rates[4], scalars)
    for ref, value in zip(scales_outs, new):
        ref[...] = value
    mine = jnp.where(place == 0, sums[6:9], sums[9:12])
    width = offsets_refs[0].shape[1]
    mine = jnp.concatenate(
        [mine[r : r + 1, c : c + width] for r in range(3) for c in range(0, D, width)], axis=0
    )
    new = adam(*(ref[...] for ref in offsets_refs), mine, rates[5], scalars)
    for ref, value in zip(offsets_outs, new):
        ref[...] = value
    for copy in copies:
        copy.wait()


def finish(chunk, halves_of_rows, large, grads, scales, offsets, total, norm, step_count, passages):
    chunks = halves_of_rows[0].shape[0] // chunk
    halves = lax.axis_size("tensor")
    anywhere = pl.BlockSpec(memory_space=pl.ANY)
    vmem = pl.BlockSpec(memory_space=pltpu.VMEM)
    smem = pl.BlockSpec(memory_space=pltpu.SMEM)
    f32, bf16 = jnp.float32, jnp.bfloat16
    rates = (1.0 / math.sqrt(D), 8.0 / math.sqrt(D), 1.0 / math.sqrt(D), 1.0 / math.sqrt(FF), 0.3, 0.3)
    offsets = [each.reshape(-1, 128) for each in offsets]
    shaped = [jax.ShapeDtypeStruct(each.shape, f32) for each in (*large, *scales, *offsets)]
    both = [
        jax.ShapeDtypeStruct((halves * count * chunk, D), dtype)
        for dtype in (bf16, f32)
        for count in (1, chunks - 1)
    ]
    outs = pl.pallas_call(
        functools.partial(finish_kernel, chunk, chunks, rates, passages, halves),
        in_specs=[anywhere] * 21 + [vmem] * 14 + [smem],
        out_specs=[anywhere] * 20 + [vmem] * 9,
        out_shape=both + shaped + [jax.ShapeDtypeStruct((8, 128), f32)],
        scratch_shapes=[pltpu.VMEM(each.shape, f32) for each in large] * 2
        + [
            pltpu.VMEM((halves * chunks * chunk, D), bf16),
            pltpu.VMEM((chunks * chunk, D), f32),
            pltpu.VMEM((chunks * chunk, D), bf16),
            pltpu.VMEM((chunks, chunk, D), f32),
            pltpu.SemaphoreType.DMA((16,)),
            pltpu.SemaphoreType.DMA((16,)),
            pltpu.SemaphoreType.DMA((6,)),
            pltpu.SemaphoreType.DMA((chunks,)),
            pltpu.SemaphoreType.DMA((5,)),
        ],
        compiler_params=pltpu.CompilerParams(vmem_limit_bytes=big_vmem),
        name="finish",
    )(*halves_of_rows, *large, *grads, *scales, *offsets, total, norm, step_count)
    return outs[:4], outs[4:20], outs[20:24], [each.reshape(-1) for each in outs[24:28]], outs[28]


def half_specs(chunk, chunks, at):
    def long_at(i):
        return (lax.axis_index("tensor") * (chunks - 1) + jnp.maximum(at(i) - 1, 0), 0)

    return [
        pl.BlockSpec((chunk, D), lambda i: (lax.axis_index("tensor"), 0)),
        pl.BlockSpec((chunk, D), long_at),
    ]


def row_spec(rows, columns):
    return pl.BlockSpec((rows, columns), lambda i: (i, 0))


def full_spec(shape):
    return pl.BlockSpec(shape, lambda i: (0,) * len(shape), pipeline_mode=pl.Buffered(1))


def shards(
    short_tokens,
    long_tokens,
    short_cotangent,
    long_cotangent,
    short_lengths,
    long_lengths,
    queries,
    positives,
    step_count,
    mixing_weight,
    mixing_moment,
    mixing_square,
    mixing_average,
    merging_weight,
    merging_moment,
    merging_square,
    merging_average,
    expand_weight,
    expand_moment,
    expand_square,
    expand_average,
    shrink_weight,
    shrink_moment,
    shrink_square,
    shrink_average,
    scales_weight,
    scales_moment,
    scales_square,
    scales_average,
    offsets_weight,
    offsets_moment,
    offsets_square,
    offsets_average,
):
    halves = lax.axis_size("tensor")
    place = lax.axis_index("tensor")
    short_span = short_tokens.shape[1]
    long_span = long_tokens.shape[1]
    shorts = short_tokens.shape[0] // halves
    longs = long_tokens.shape[0] // halves
    chunk = long_span
    piece = short_span
    assert shorts * short_span == chunk and shorts == longs
    chunks = longs + 1
    rows = chunks * chunk
    width = mixing_weight.shape[2]
    wide = expand_weight.shape[1]

    def own_half(short_all, long_all):
        return jnp.concatenate(
            [
                lax.dynamic_slice_in_dim(short_all, place * shorts, shorts).reshape(-1, D),
                lax.dynamic_slice_in_dim(long_all, place * longs, longs).reshape(-1, D),
            ],
            axis=0,
        )

    fast = lax.axis_size("dp") == 16 and halves == 2
    mixing_own = mixing_weight.astype(jnp.bfloat16).reshape(-1, 3 * width)
    middle_own = jnp.concatenate([merging_weight.T, expand_weight], axis=1).astype(jnp.bfloat16)
    shrink_own = shrink_weight.T.astype(jnp.bfloat16)
    short_limits = lax.dynamic_slice_in_dim(short_lengths, place * shorts, shorts)
    long_limits = lax.dynamic_slice_in_dim(long_lengths, place * longs, longs)
    spans = jnp.concatenate(
        [
            short_limits[None, :],
            long_limits[:, None] - piece * jnp.arange(chunk // piece, dtype=jnp.int32)[None, :],
        ],
        axis=0,
    )
    inputs = own_half(short_tokens, long_tokens)
    bf16, f32 = jnp.bfloat16, jnp.float32

    def shaped(columns, dtype):
        return jax.ShapeDtypeStruct((rows, columns), dtype)

    smem = pl.BlockSpec(memory_space=pltpu.SMEM)
    params = pltpu.CompilerParams(vmem_limit_bytes=big_vmem)
    mixing_columns = halves * 3 * width
    scores_flops = 2 * rows * chunk * PAIR * (halves * width // HEAD_DIM)
    if fast:
        (qkv, context), feed, (mixing_full, middle_full, shrink_full) = forward_gather(
            piece,
            spans,
            short_tokens.reshape(-1, D),
            long_tokens.reshape(-1, D),
            (mixing_own, middle_own, shrink_own),
            offsets_weight,
            scales_weight,
            chunk,
            chunks,
        )
    else:
        mixing_full, middle_full, shrink_full = (
            gathered(own) for own in (mixing_own, middle_own, shrink_own)
        )
        offsets_other = tensor_swap(offsets_weight)
        offsets_both = jnp.where(
            place == 0,
            jnp.stack([offsets_weight, offsets_other]),
            jnp.stack([offsets_other, offsets_weight]),
        )
        mixing_bias = jnp.concatenate(
            [
                offsets_both[:, :width],
                jnp.zeros((halves, width), jnp.float32),
                offsets_both[:, width : 2 * width],
            ],
            axis=1,
        ).reshape(1, -1)
        qkv, context = pl.pallas_call(
            functools.partial(attend_forward_kernel, piece),
            grid=(chunks,),
            in_specs=[
                smem,
                row_spec(chunk, D),
                full_spec(mixing_full.shape),
                full_spec(mixing_bias.shape),
            ],
            out_specs=[row_spec(chunk, mixing_columns), row_spec(chunk, D)],
            out_shape=[shaped(mixing_columns, bf16), shaped(D, bf16)],
            compiler_params=params,
            cost_estimate=pl.CostEstimate(
                flops=2 * rows * D * mixing_columns + 6 * scores_flops,
                bytes_accessed=16 * 1024 * 1024,
                transcendentals=rows * chunk * 12,
            ),
            name="attend_forward",
        )(spans, inputs, mixing_full, mixing_bias)
        upward_bias = offsets_both[:, 2 * width :].reshape(1, -1)
        feed_ins = [context, inputs, middle_full, shrink_full, scales_weight, upward_bias]
        feed_in_specs = [
            row_spec(chunk, D),
            row_spec(chunk, D),
            full_spec(middle_full.shape),
            full_spec(shrink_full.shape),
            full_spec(scales_weight.shape),
            full_spec(upward_bias.shape),
        ]
        feed_out_specs = [
            row_spec(chunk, D),
            row_spec(chunk, FF),
            row_spec(chunk, FF),
            row_spec(chunk, D),
            row_spec(chunk, 1),
            row_spec(chunk, D),
            row_spec(chunk, D),
            row_spec(chunk, 1),
            pl.BlockSpec((1, 8, D), lambda i: (i, 0, 0)),
        ]
        feed_outs = [
            shaped(D, bf16),
            shaped(FF, bf16),
            shaped(FF, bf16),
            shaped(D, f32),
            shaped(1, f32),
            shaped(D, bf16),
            shaped(D, f32),
            shaped(1, f32),
            jax.ShapeDtypeStruct((chunks, 8, D), f32),
        ]
        feed_cost = pl.CostEstimate(
            flops=2 * rows * D * (D + 2 * FF),
            bytes_accessed=48 * 1024 * 1024,
            transcendentals=2 * rows * FF,
        )
        feed = pl.pallas_call(
            functools.partial(feed_forward_kernel, piece),
            grid=(chunks,),
            in_specs=feed_in_specs,
            out_specs=feed_out_specs,
            out_shape=feed_outs,
            compiler_params=params,
            cost_estimate=feed_cost,
            name="feed_forward",
        )(*feed_ins)
    anywhere = pl.BlockSpec(memory_space=pl.ANY)
    (
        hidden_low,
        activated,
        slope,
        normed_first,
        rstd_first,
        output,
        normed_second,
        rstd_second,
        leading,
    ) = feed
    query_gradient, lead_rows, loss_rows = contrast(leading, queries, positives)
    ahead = 2
    if fast:
        output_head = lax.optimization_barrier((output[: ahead * chunk], lead_rows))[0]
        output_head = tensor_swap(output_head)
    tile = 512
    per = wide // tile

    def chunk_spec(columns):
        return pl.BlockSpec((chunk, columns), lambda i: (jnp.minimum(i, chunks - 1), 0))

    second_back, second_grad, shrink_grad = pl.pallas_call(
        functools.partial(out_back_kernel, piece, chunks),
        grid=(chunks + FF // tile,),
        in_specs=[
            *half_specs(chunk, chunks, lambda i: jnp.minimum(i, chunks - 1)),
            pl.BlockSpec((1, 8, D), lambda i: (jnp.minimum(i, chunks - 1), 0, 0)),
            chunk_spec(D),
            chunk_spec(1),
            full_spec(scales_weight.shape),
            pl.BlockSpec((rows, tile), lambda i: (0, jnp.maximum(i - chunks, 0))),
        ],
        out_specs=[
            chunk_spec(D),
            pl.BlockSpec((8, D), lambda i: (0, 0)),
            pl.BlockSpec(
                (1, D, tile),
                lambda i: (jnp.maximum(i - chunks, 0) // per, 0, jnp.maximum(i - chunks, 0) % per),
            ),
        ],
        out_shape=[
            shaped(D, f32),
            jax.ShapeDtypeStruct((8, D), f32),
            jax.ShapeDtypeStruct((halves, D, wide), bf16),
        ],
        scratch_shapes=[pltpu.VMEM((D, rows), bf16)],
        compiler_params=params,
        cost_estimate=pl.CostEstimate(
            flops=2 * rows * D * FF, bytes_accessed=32 * 1024 * 1024, transcendentals=0
        ),
        name="out_back",
    )(
        short_cotangent.reshape(-1, D),
        long_cotangent.reshape(-1, D),
        lead_rows, normed_second, rstd_second, scales_weight, activated)
    back_ins = [
        second_back,
        normed_first,
        rstd_first,
        slope,
        hidden_low,
        context,
        middle_full,
        shrink_full,
        scales_weight,
    ]
    merging_tiles = D // width
    back_steps = chunks + merging_tiles + FF // tile

    def merging_at(i):
        return jnp.clip(i - chunks, 0, merging_tiles - 1)

    def expand_at(i):
        return jnp.maximum(i - chunks - merging_tiles, 0)

    back_in_specs = [
        chunk_spec(D),
        chunk_spec(D),
        chunk_spec(1),
        chunk_spec(FF),
        chunk_spec(D),
        pl.BlockSpec((rows, width), lambda i: (0, merging_at(i))),
        full_spec(middle_full.shape),
        full_spec(shrink_full.shape),
        full_spec(scales_weight.shape),
    ]
    back_out_specs = [
        chunk_spec(D),
        chunk_spec(D),
        pl.BlockSpec((8, D), lambda i: (0, 0)),
        pl.BlockSpec((8, FF), lambda i: (0, 0)),
        pl.BlockSpec((1, D, width), lambda i: (merging_at(i), 0, 0)),
        pl.BlockSpec((1, D, tile), lambda i: (expand_at(i) // per, 0, expand_at(i) % per)),
    ]
    back_outs = [
        shaped(D, f32),
        shaped(D, bf16),
        jax.ShapeDtypeStruct((8, D), f32),
        jax.ShapeDtypeStruct((8, FF), f32),
        jax.ShapeDtypeStruct((halves, D, width), bf16),
        jax.ShapeDtypeStruct((halves, D, wide), bf16),
    ]
    back_scratch = [
        pltpu.VMEM((rows, FF), bf16),
        pltpu.VMEM((D, rows), bf16),
        pltpu.VMEM((D, rows), bf16),
    ]
    back_cost = pl.CostEstimate(
        flops=2 * rows * D * (2 * D + 3 * FF), bytes_accessed=48 * 1024 * 1024, transcendentals=0
    )
    if fast:
        shrink_grad, output_head = lax.optimization_barrier((shrink_grad, output_head))
        tail = output.reshape(chunks, chunk, D)
        *back, output_tail, shrink_sum = pl.pallas_call(
            functools.partial(feed_back_scatter_kernel, chunks, chunks - ahead, width),
            grid=(back_steps,),
            in_specs=[anywhere, full_spec(tail.shape)] + back_in_specs,
            out_specs=back_out_specs + [anywhere, full_spec(scatter_shape(shrink_grad).shape)],
            out_shape=back_outs
            + [jax.ShapeDtypeStruct((chunks - ahead, chunk, D), bf16), scatter_shape(shrink_grad)],
            scratch_shapes=back_scratch
            + scatter_buffers(shrink_grad, width, True) * (wide // width)
            + scatter_sems(wide // width)
            + [pltpu.SemaphoreType.DMA((chunks - ahead,))] * 2,
            compiler_params=pltpu.CompilerParams(
                collective_id=5, has_side_effects=True, vmem_limit_bytes=big_vmem
            ),
            cost_estimate=back_cost,
            name="feed_back_scatter",
        )(scatter_input(shrink_grad), tail, *back_ins)
    else:
        back = pl.pallas_call(
            functools.partial(feed_back_kernel, chunks),
            grid=(back_steps,),
            in_specs=back_in_specs,
            out_specs=back_out_specs,
            out_shape=back_outs,
            scratch_shapes=back_scratch,
            compiler_params=params,
            cost_estimate=back_cost,
            name="feed_back",
        )(*back_ins)
        shrink_sum = scattered(shrink_grad)
        output_head = tensor_swap(output[: ahead * chunk])
        output_tail = tensor_swap(output[ahead * chunk :])
    first_back, context_back, first_grad, upward_grad, merging_grad, expand_grad = back
    pair_ins = [qkv, context_back, first_back, mixing_full]
    pair_in_specs = [
        chunk_spec(mixing_columns),
        chunk_spec(D),
        chunk_spec(D),
        full_spec(mixing_full.shape),
    ]
    pair_cost = pl.CostEstimate(
        flops=2 * rows * D * mixing_columns + 15 * scores_flops,
        bytes_accessed=24 * 1024 * 1024,
        transcendentals=rows * chunk * 12,
    )
    lane = lax.broadcasted_iota(jnp.int32, (1, D), 1)
    losses = jnp.where(lane == 1, loss_rows[0, 0], 0.0)

    def stacked(bias_both, scalars):
        scalars = jnp.pad(scalars, ((0, 3), (0, 0)))
        offsets_grad = jnp.concatenate([bias_both, upward_grad[0].reshape(halves, wide)], axis=1)
        vectors = [first_grad[:2], second_grad[:2], first_grad[2:3], second_grad[2:3]]
        return jnp.concatenate(vectors + [offsets_grad.reshape(-1, D), scalars], axis=0)

    if fast:
        parts = (expand_grad, merging_grad)
        late_count, last_count = wide // width + 1, 3
        last_whole = jax.ShapeDtypeStruct((halves, D, 3 * width), bf16)
        vector = jax.ShapeDtypeStruct((16, D), f32)
        more = (shrink_sum, first_grad, second_grad, upward_grad, loss_rows)
        small = (8, 128)
        out_shape = [
            shaped(D, f32),
            jax.ShapeDtypeStruct((chunks, chunk, D), bf16),
            scatter_shape(expand_grad),
            scatter_shape(merging_grad),
            scatter_shape(last_whole),
            jax.ShapeDtypeStruct(vector.shape, f32),
            jax.ShapeDtypeStruct(small, f32),
        ]
        input_back, input_other, expand_sum, merging_sum, mixing_sum, summed, squares_all = (
            pl.pallas_call(
                functools.partial(attend_last_kernel, piece, chunks, width),
                grid=(chunks + 2 * last_count,),
                in_specs=[smem, anywhere, anywhere]
                + pair_in_specs
                + [
                    pl.BlockSpec((count * chunk, D), lambda i: (lax.axis_index("tensor"), 0), pipeline_mode=pl.Buffered(1))
                    for count in (1, chunks - 1)
                ]
                + [full_spec(each.shape) for each in more],
                out_specs=[chunk_spec(D), anywhere]
                + [full_spec(each.shape) for each in out_shape[2:]],
                out_shape=out_shape,
                scratch_shapes=[
                    pltpu.VMEM((rows, mixing_columns), bf16),
                    pltpu.VMEM((8, mixing_columns), f32),
                    pltpu.VMEM((D, rows), bf16),
                    pltpu.VMEM((halves, 4, 2, 2, D // 16, 3 * width), bf16),
                    pltpu.VMEM((8, width), f32),
                    pltpu.VMEM((chunks, chunk, D), bf16),
                    pltpu.SemaphoreType.DMA((chunks,)),
                    pltpu.SemaphoreType.DMA((chunks,)),
                ]
                + scatter_buffers(expand_grad, width, True) * late_count
                + scatter_sems(late_count)
                + scatter_buffers(last_whole, width) * last_count
                + scatter_sems(last_count)
                + [
                    pltpu.VMEM((6,) + vector.shape, f32),
                    pltpu.VMEM((4,) + vector.shape, f32),
                    pltpu.SemaphoreType.DMA((6,)),
                    pltpu.SemaphoreType.DMA((6,)),
                    pltpu.VMEM((8,) + small, f32),
                    pltpu.VMEM((4,) + small, f32),
                    pltpu.SemaphoreType.DMA((10,)),
                    pltpu.SemaphoreType.DMA((10,)),
                ],
                compiler_params=pltpu.CompilerParams(
                    collective_id=6, has_side_effects=True, vmem_limit_bytes=big_vmem
                ),
                cost_estimate=pair_cost,
                name="attend_last",
            )(
                spans,
                *(scatter_input(part) for part in parts),
                *pair_ins,
                short_tokens.reshape(-1, D),
                long_tokens.reshape(-1, D),
                *more,
            )
        )
    else:
        projected_back, input_back, bias_grad, input_low = pl.pallas_call(
            functools.partial(attend_back_kernel, piece),
            grid=(chunks,),
            in_specs=[smem] + pair_in_specs,
            out_specs=[
                row_spec(chunk, mixing_columns),
                row_spec(chunk, D),
                pl.BlockSpec((8, mixing_columns), lambda i: (0, 0)),
                pl.BlockSpec((1, chunk, D), lambda i: (i, 0, 0)),
            ],
            out_shape=[
                shaped(mixing_columns, bf16),
                shaped(D, f32),
                jax.ShapeDtypeStruct((8, mixing_columns), f32),
                jax.ShapeDtypeStruct((chunks, chunk, D), bf16),
            ],
            compiler_params=params,
            cost_estimate=pair_cost,
            name="attend_back",
        )(spans, *pair_ins)
        expand_sum, merging_sum = scattered(expand_grad), scattered(merging_grad)
        input_other = tensor_swap(input_low)
        mixing_sum = scattered(weight_grad(inputs, projected_back, halves, 384))
        sums = (shrink_sum, expand_sum, merging_sum, mixing_sum)
        squares_part = sum(jnp.sum(each * each) for each in sums)
        bias_both = bias_grad[0].reshape(halves, 3, width)
        bias_both = jnp.concatenate([bias_both[:, 0], bias_both[:, 2]], axis=1)
        summed = all_total(stacked(bias_both, jnp.where(lane == 0, squares_part, losses)))
        squares_all = jnp.full((8, 128), summed[12, 0])
    grads = (mixing_sum, merging_sum, expand_sum, shrink_sum)

    def turn(value):
        return value.transpose(1, 0, 2)

    large = (
        turn(mixing_weight),
        turn(mixing_moment),
        turn(mixing_square),
        turn(mixing_average),
        merging_weight.T,
        merging_moment.T,
        merging_square.T,
        merging_average.T,
        expand_weight,
        expand_moment,
        expand_square,
        expand_average,
        shrink_weight.T,
        shrink_moment.T,
        shrink_square.T,
        shrink_average.T,
    )
    both, large_new, scales_new, offsets_new, figures = finish(
        chunk,
        (output, output_head, output_tail.reshape(-1, D), input_back, input_other.reshape(rows, D)),
        large,
        grads,
        (scales_weight, scales_moment, scales_square, scales_average),
        (offsets_weight, offsets_moment, offsets_square, offsets_average),
        summed,
        squares_all,
        step_count,
        queries.shape[0] * lax.axis_size("dp"),
    )
    return (
        (
            both[0].reshape(short_tokens.shape),
            both[1].reshape(long_tokens.shape),
            both[2].reshape(short_tokens.shape),
            both[3].reshape(long_tokens.shape),
            query_gradient,
            figures[1, :1],
            figures[0, :1],
        )
        + tuple(turn(each) for each in large_new[:4])
        + tuple(each.T for each in large_new[4:8])
        + tuple(large_new[8:12])
        + tuple(each.T for each in large_new[12:])
        + tuple(scales_new)
        + tuple(offsets_new)
    )


def solution(mesh):
    placed = (
        P("dp", None, None),
        P("dp", None, None),
        P("dp", None, None),
        P("dp", None, None),
        P("dp"),
        P("dp"),
        P("dp", None),
        P("dp"),
        P(),
        P("dp", None, "tensor"),
        P("dp", None, "tensor"),
        P("dp", None, "tensor"),
        P("dp", None, "tensor"),
        P("tensor", "dp"),
        P("tensor", "dp"),
        P("tensor", "dp"),
        P("tensor", "dp"),
        P("dp", "tensor"),
        P("dp", "tensor"),
        P("dp", "tensor"),
        P("dp", "tensor"),
        P("tensor", "dp"),
        P("tensor", "dp"),
        P("tensor", "dp"),
        P("tensor", "dp"),
        P(),
        P(),
        P(),
        P(),
        P("tensor"),
        P("tensor"),
        P("tensor"),
        P("tensor"),
    )
    return jax.shard_map(
        shards,
        mesh=mesh,
        in_specs=placed,
        out_specs=(
            P("dp", None, None),
            P("dp", None, None),
            P("dp", None, None),
            P("dp", None, None),
            P("dp", None),
            P(),
            P(),
            P("dp", None, "tensor"),
            P("dp", None, "tensor"),
            P("dp", None, "tensor"),
            P("dp", None, "tensor"),
            P("tensor", "dp"),
            P("tensor", "dp"),
            P("tensor", "dp"),
            P("tensor", "dp"),
            P("dp", "tensor"),
            P("dp", "tensor"),
            P("dp", "tensor"),
            P("dp", "tensor"),
            P("tensor", "dp"),
            P("tensor", "dp"),
            P("tensor", "dp"),
            P("tensor", "dp"),
            P(),
            P(),
            P(),
            P(),
            P("tensor"),
            P("tensor"),
            P("tensor"),
            P("tensor"),
        ),
        check_vma=False,
    )
```
